32 devices in a mesh: groups: 2 (over y), sector: 4 (over z), env: 2 (over x), rep: 2 (over core).
Axes of the slice: x: 2, y: 2, z: 4, core: 2. Of those that a mesh axis runs over, the one named last changes fastest.
Arguments:
- vectors: bfloat16 [2, 192, 256, 256], P(None, ('groups', 'sector'), ('env', 'rep')), parts along dimension 1, may hold values from -6 to 6
- left_env: bfloat16 [2, 192, 256, 256], P('env', ('groups', 'sector'), 'rep'), parts along dimension 1, may hold values from -0.375 to 0.375
- right_env: bfloat16 [2, 192, 256, 256], P('env', ('groups', 'sector'), 'rep'), parts along dimension 1, may hold values from -0.375 to 0.375
- energy: float32 [192], P(('groups', 'sector')), parts along dimension 0, may hold values from 0.5 to 4
- partner: int32 [2, 192], P('env', 'groups'), parts along dimension 1, may hold values from 0 to 95, as said below
Outputs:
- image: float32 [2, 192, 256, 256], P(None, ('groups', 'sector'), ('env', 'rep')), parts along dimension 1
- expectation: float32 [4], P('groups'), parts along dimension 0
The draws below stay inside these ranges and needn't reach their ends.
There are 2 independent parts, one for each index of `groups`. The reference program is written for one: setup_inputs(seed, part) draws one part's arguments, and reference() takes and returns one part's arrays. A program takes and returns all parts, laid end to end along the dimension named above; each array names one. Nothing has to cross between parts.
Inputs may be any that keep to these rules, and one draw needn't show every extreme that they name: For each term, partner is a permutation of the sectors. Reading sectors in groups of 24 (one group an index of sector), the sectors at one position of every group take their partners from the group the same number of groups below (modulo the number of groups), at one common position; for one term no group takes partners for more than 6 of its sectors from one group, and some group takes exactly 6.
All inputs are finite; a program needn't handle non-finite values.
Results may differ from the reference program's by a relative error of at most 0.0035.
Values may be sent and summed in bfloat16 or wider, within the bound.
No kernel may reach another device: no remote copies, remote signals or barrier semaphores. Data moves between devices by JAX's collectives and lax.ppermute only.
A program may use at most 64 MiB of HBM per device.

```python
import math
import jax
import jax.numpy as jnp
from jax import lax

M = 256
SEC_DEV = 24
VECTORS = 2
SECTORS = 96
TERMS = 2


def shuffled(key, count):
    scores = jax.random.randint(key, (count,), 0, 1048576).astype(jnp.int32)
    distinct = scores * count + jnp.arange(count, dtype=jnp.int32)
    return jnp.argsort(distinct, stable=True).astype(jnp.int32)


def draw_partner(key, part):
    key = jax.random.fold_in(key, 7)
    groups_along = SECTORS // SEC_DEV
    rows = []
    for term in range(TERMS):
        term_key = jax.random.fold_in(key, 100 + term)
        key_offsets = jax.random.fold_in(term_key, 1)
        key_slots = jax.random.fold_in(term_key, 2)
        offsets = shuffled(key_offsets, groups_along)
        within = shuffled(key_slots, SEC_DEV)
        slot_ids = jnp.arange(SEC_DEV, dtype=jnp.int32)
        distance = offsets[slot_ids // 2 % groups_along]
        targets = jnp.arange(groups_along, dtype=jnp.int32)[:, None]
        anchor = (targets - distance[None, :]) % groups_along
        rows.append((anchor * SEC_DEV + within[None, :]).reshape(-1))
    return jnp.stack(rows, axis=0).astype(jnp.int32)


def block_levels(rng, shape, split, low, largest):
    def one(dim, blocks):
        steps = jax.random.uniform(jax.random.fold_in(jax.random.fold_in(rng, 6), dim), (blocks,), jnp.float32, low / len(split), largest / len(split))
        return jnp.repeat(jnp.exp(steps), shape[dim] // blocks).reshape((-1,) + (1,) * (len(shape) - dim - 1))

    factor_of = one(*split[0])
    for cut in split[1:]:
        factor_of = factor_of * one(*cut)
    return factor_of


def gaussian(stream_key, shape, spread, bound, pieces=(), kind=jnp.bfloat16):
    factor_of = block_levels(stream_key, shape, pieces, -0.22, 0.18) if pieces else 1.0
    result = jax.random.normal(stream_key, shape, jnp.float32) * spread * factor_of
    return jnp.minimum(jnp.maximum(result, -bound), bound).astype(kind)


def setup_inputs(seed: int = 0, part: int = 0) -> dict:
    arg_keys = jax.random.split(jax.random.key(seed), 6)
    own_keys = jax.random.split(jax.random.fold_in(arg_keys[5], part), 6)
    return {
        "vectors": gaussian(own_keys[0], (VECTORS, SECTORS, M, M), 1.0, 6.0, ((1, 4), (2, 4))),
        "left_env": gaussian(own_keys[1], (TERMS, SECTORS, M, M), M ** -0.5, 0.375, ((0, 2), (1, 4), (2, 2))),
        "right_env": gaussian(own_keys[2], (TERMS, SECTORS, M, M), M ** -0.5, 0.375, ((0, 2), (1, 4), (2, 2))),
        "energy": jnp.clip(jnp.exp(math.log(4.0) - 2.0794415 * jax.random.uniform(own_keys[3], (SECTORS,), jnp.float32) ** block_levels(own_keys[3], (SECTORS,), ((0, 4),), -0.2, 0.2)), 0.5, 4.0),
        "partner": draw_partner(jax.random.fold_in(jax.random.fold_in(arg_keys[5], part), 71), part),
    }


def reference(vectors, left_env, right_env, energy, partner):
    floats_in = vectors.astype(jnp.float32)

    def accumulate(running, inputs):
        left_block, right_block, sources = inputs
        products = jnp.einsum("vpac,pbc->vpab", floats_in, right_block.astype(jnp.float32))
        products = lax.optimization_barrier(products.astype(jnp.bfloat16)).astype(jnp.float32)
        chosen = jnp.take(products, sources.astype(jnp.int32), axis=1)
        contribution = jnp.einsum("qia,vqab->vqib", left_block.astype(jnp.float32), chosen)
        contribution = lax.optimization_barrier(contribution.astype(jnp.bfloat16)).astype(jnp.float32)
        return running + contribution, None

    start_sum = jnp.zeros(vectors.shape, jnp.float32)
    summed, unused = lax.scan(accumulate, start_sum, (left_env, right_env, partner))
    applied = summed + energy[None, :, None, None] * floats_in
    expectation = jnp.mean(floats_in * applied, axis=(1, 2, 3))
    return applied, expectation
```

```python
import functools

import jax
import jax.numpy as jnp
from jax import lax
from jax.experimental import pallas as pl
from jax.experimental.pallas import tpu as pltpu
from jax.sharding import PartitionSpec as P

HBM = pl.BlockSpec(memory_space=pl.ANY)
SMEM = pl.BlockSpec(memory_space=pltpu.SMEM)
VMEM = pl.BlockSpec(memory_space=pltpu.VMEM)


def aligned(index, size):
    return pl.multiple_of(index * size, size)


class Sizes:
    def __init__(self, vectors, left_env):
        self.env = lax.axis_size("env")
        self.rep = lax.axis_size("rep")
        self.sector = lax.axis_size("sector")
        self.batch, self.slots, self.own_rows, self.order = vectors.shape
        assert self.batch == self.rep
        self.half = left_env.shape[2]
        self.chip_rows = self.own_rows * self.rep
        self.capacity = 2 * ((self.slots + 2 * self.sector - 1) // (2 * self.sector))
        self.flat = self.sector * self.capacity
        self.source, self.target, self.valid = 0, self.flat, 2 * self.flat
        self.core, self.chip = 3 * self.flat, 3 * self.flat + 1


def plan_body(z, partner, ids, plan, count):
    def clear(i, carry):
        plan[i] = 0
        return carry

    lax.fori_loop(0, 3 * z.flat, clear, 0)
    for d in range(z.sector):
        count[d] = 0

    def place(j, carry):
        sector = partner[0, j]
        group = lax.div(sector, z.slots)
        slot = sector - group * z.slots
        distance = lax.rem(z.sector - group, z.sector)
        rank = count[distance]
        count[distance] = rank + 1
        index = distance * z.capacity + rank
        plan[z.source + index] = slot
        plan[z.target + index] = j
        plan[z.valid + index] = 1
        return carry

    lax.fori_loop(0, z.slots, place, 0)
    plan[z.core] = ids[0]
    plan[z.chip] = ids[1]


def make_plan(z, partner, ids):
    return pl.pallas_call(
        functools.partial(plan_body, z),
        out_shape=jax.ShapeDtypeStruct((3 * z.flat + 2,), jnp.int32),
        in_specs=[SMEM, SMEM],
        out_specs=SMEM,
        scratch_shapes=[pltpu.SMEM((z.sector,), jnp.int32)],
    )(partner, ids)


def products_body(z, first, count, pieces, *refs):
    per_piece = z.rep
    plan = refs[0]
    right = refs[1 : 1 + z.rep]
    rows = refs[1 + z.rep : 1 + z.rep + pieces * per_piece]
    outs = refs[1 + z.rep + pieces * per_piece : -3]
    vbuf, rbuf, sem = refs[-3:]
    core = plan[z.core]

    def copies(n):
        slot = plan[z.source + first + n]
        made = []
        for s in range(z.rep):
            who = lax.rem(core + z.rep - s, z.rep)
            made.append(
                pltpu.make_async_copy(
                    right[s].at[0, slot],
                    rbuf.at[n, pl.ds(aligned(who, z.half), z.half)],
                    sem.at[n, s],
                )
            )
            for piece in range(pieces):
                ref = rows[piece * per_piece + s]
                source = ref.at[core, slot] if s == 0 else ref.at[slot]
                start = pl.multiple_of(piece * z.chip_rows + who * z.own_rows, z.own_rows)
                made.append(
                    pltpu.make_async_copy(
                        source,
                        vbuf.at[n, pl.ds(start, z.own_rows)],
                        sem.at[n, z.rep + piece * per_piece + s],
                    )
                )
        return made

    def begin(n, carry):
        for copy in copies(n):
            copy.start()
        return carry

    lax.fori_loop(0, count, begin, 0)
    each = z.capacity
    for d, out in enumerate(outs):

        def work(i, carry):
            n = d * each + i
            for copy in copies(n):
                copy.wait()
            out[i] = lax.dot_general(
                vbuf[n], rbuf[n], (((1,), (1,)), ((), ())), preferred_element_type=jnp.float32
            ).astype(jnp.bfloat16)
            return carry

        lax.fori_loop(0, each, work, 0)


def products(z, plan, right, rows, distances, pieces):
    count = len(distances) * z.capacity
    height = pieces * z.chip_rows
    block = jax.ShapeDtypeStruct((z.capacity, height, z.order), jnp.bfloat16)
    return pl.pallas_call(
        functools.partial(products_body, z, distances[0] * z.capacity, count, pieces),
        out_shape=[block] * len(distances),
        in_specs=[SMEM] + [HBM] * (len(right) + len(rows)),
        out_specs=[VMEM] * len(distances),
        scratch_shapes=[
            pltpu.VMEM((count, height, z.order), jnp.bfloat16),
            pltpu.VMEM((count, z.order, z.order), jnp.bfloat16),
            pltpu.SemaphoreType.DMA((count, z.rep * (1 + pieces))),
        ],
        cost_estimate=pl.CostEstimate(
            flops=2 * count * height * z.order * z.order,
            bytes_accessed=2 * count * z.order * (z.order + 2 * height),
            transcendentals=0,
        ),
    )(plan, *right, *rows)


def terms_body(z, first, groups, *refs):
    count = groups * z.capacity
    refs = list(refs)
    plan = refs.pop(0)
    left = [refs.pop(0) for _ in range(z.rep)]
    near = [refs.pop(0) for _ in range(groups)]
    far = [refs.pop(0) for _ in range(groups)]
    vec = [[refs.pop(0) for _ in range(z.rep)] for _ in range(z.env)]
    outs = [[refs.pop(0) for _ in range(z.rep)] for _ in range(z.env)]
    dots = refs.pop(0)
    lbuf, pbuf, vbuf, tbuf, sem = refs
    core, chip = plan[z.core], plan[z.chip]

    def copies(d, i):
        n = d * z.capacity + i
        slot = plan[z.target + first + n]
        pairs = []
        for s in range(z.rep):
            who = lax.rem(core + z.rep - s, z.rep)
            pairs.append((left[s].at[0, slot], lbuf.at[n, pl.ds(aligned(who, z.half), z.half)]))
            for e in range(z.env):
                place = lax.rem(chip + z.env - e, z.env) * z.rep + who
                ref = vec[e][s]
                source = ref.at[core, slot] if s == 0 else ref.at[slot]
                pairs.append((source, vbuf.at[n, pl.ds(aligned(place, z.own_rows), z.own_rows)]))
        for e in range(z.env):
            place = lax.rem(chip + z.env - e, z.env)
            if e == 0:
                source = near[d].at[i]
            else:
                source = far[d].at[i, pl.ds((e - 1) * z.chip_rows, z.chip_rows)]
            pairs.append((source, pbuf.at[n, pl.ds(aligned(place, z.chip_rows), z.chip_rows)]))
        return [pltpu.make_async_copy(a, b, sem.at[n, k]) for k, (a, b) in enumerate(pairs)]

    for d in range(groups):

        def begin(i, carry):
            for copy in copies(d, i):
                copy.start()
            return carry

        lax.fori_loop(0, z.capacity, begin, 0)
    dots[...] = jnp.zeros_like(dots)
    for d in range(groups):

        def work(i, carry):
            n = d * z.capacity + i
            for copy in copies(d, i):
                copy.wait()
            term = jnp.dot(lbuf[n], pbuf[n], preferred_element_type=jnp.float32).astype(
                jnp.bfloat16
            )
            tbuf[...] = term
            for e in range(z.env):
                for s in range(z.rep):
                    place = lax.rem(chip + e, z.env) * z.rep + lax.rem(core + s, z.rep)
                    outs[e][s][n] = tbuf[pl.ds(aligned(place, z.own_rows), z.own_rows)]
            both = vbuf[n].astype(jnp.float32) * term.astype(jnp.float32)
            both = jnp.where(plan[z.valid + first + n] == 1, both, 0.0)
            folded = jnp.sum(both.reshape(z.order // 8, 8, z.order), axis=0)
            dots[...] += folded
            return carry

        lax.fori_loop(0, z.capacity, work, 0)


def terms(z, plan, left, near, far, vec, distances):
    groups = len(distances)
    count = groups * z.capacity
    flat = [ref for piece in vec for ref in piece]
    block = jax.ShapeDtypeStruct((count, z.own_rows, z.order), jnp.bfloat16)
    kinds = z.rep * (1 + z.env) + z.env
    whole = (count, z.order, z.order)
    made = pl.pallas_call(
        functools.partial(terms_body, z, distances[0] * z.capacity, groups),
        out_shape=[block] * (z.env * z.rep) + [jax.ShapeDtypeStruct((8, z.order), jnp.float32)],
        in_specs=[SMEM] + [HBM] * (len(left) + len(near) + len(far) + len(flat)),
        out_specs=[VMEM] * (z.env * z.rep + 1),
        scratch_shapes=[
            pltpu.VMEM(whole, jnp.bfloat16),
            pltpu.VMEM(whole, jnp.bfloat16),
            pltpu.VMEM(whole, jnp.bfloat16),
            pltpu.VMEM((z.order, z.order), jnp.bfloat16),
            pltpu.SemaphoreType.DMA((count, kinds)),
        ],
        cost_estimate=pl.CostEstimate(
            flops=2 * count * z.order**3,
            bytes_accessed=8 * count * z.order * z.order,
            transcendentals=0,
        ),
    )(plan, *left, *near, *far, *flat)
    blocks = [made[e * z.rep : (e + 1) * z.rep] for e in range(z.env)]
    return blocks, made[-1]


def image_body(z, sizes, *refs):
    refs = list(refs)
    plans = [refs.pop(0) for _ in range(z.env)]
    energy, vectors = refs.pop(0), refs.pop(0)
    parts = [[[refs.pop(0) for _ in sizes] for _ in range(z.rep)] for _ in range(z.env)]
    image = refs.pop(0)
    core = plans[0][z.core]

    def start(j, carry):
        for v in range(z.batch):
            image[v, j] = energy[j] * vectors[v, j].astype(jnp.float32)
        return carry

    lax.fori_loop(0, z.slots, start, 0)
    for e, plan in enumerate(plans):
        first = 0
        for g, count in enumerate(sizes):

            def add(n, carry):
                slot = plan[z.target + first + n]

                @pl.when(plan[z.valid + first + n] == 1)
                def _():
                    for s in range(z.rep):
                        v = lax.rem(core + z.rep - s, z.rep)
                        image[v, slot] += parts[e][s][g][n].astype(jnp.float32)

                return carry

            lax.fori_loop(0, count, add, 0)
            first += count


def make_image(z, plans, energy, vectors, parts):
    sizes = tuple(block.shape[0] for block in parts[0][0])
    flat = [ref for piece in parts for kind in piece for ref in kind]
    return pl.pallas_call(
        functools.partial(image_body, z, sizes),
        out_shape=jax.ShapeDtypeStruct(vectors.shape, jnp.float32),
        in_specs=[SMEM] * (z.env + 1) + [VMEM] * (len(flat) + 1),
        out_specs=VMEM,
    )(*plans, energy, vectors, *flat)


def shift(array, axis, size, step):
    return lax.ppermute(array, axis, [(i, (i + step) % size) for i in range(size)])


def shift_both(z, array, e, s):
    perm = []
    for x in range(z.env):
        for c in range(z.rep):
            perm.append((x * z.rep + c, (x + e) % z.env * z.rep + (c + s) % z.rep))
    return lax.ppermute(array, ("env", "rep"), perm)


def total_over(array, axis):
    size = lax.axis_size(axis)
    if size & (size - 1):
        return lax.psum(array, axis)
    step = 1
    while step < size:
        array = array + lax.ppermute(array, axis, [(i, i ^ step) for i in range(size)])
        step *= 2
    return array


def on_device(vectors, left_env, right_env, energy, partner):
    z = Sizes(vectors, left_env)
    core, chip = lax.axis_index("rep"), lax.axis_index("env")
    ids = jnp.stack([core, chip]).astype(jnp.int32)

    def rows_for(array, s):
        wanted = lax.rem(core + s, z.rep)
        own = lax.dynamic_index_in_dim(array, wanted, axis=0, keepdims=False)
        return shift(own, "rep", z.rep, s)

    others = [shift(vectors, "env", z.env, e) for e in range(1, z.env)]
    plan = make_plan(z, partner, ids)
    plans = [plan]
    for e in range(1, z.env):
        plans.append(make_plan(z, shift(partner, "env", z.env, e), ids))
    right = [right_env] + [shift(right_env, "rep", z.rep, s) for s in range(1, z.rep)]
    near_rows = [vectors] + [rows_for(vectors, s) for s in range(1, z.rep)]
    left = [left_env] + [shift(left_env, "rep", z.rep, s) for s in range(1, z.rep)]

    many = min(z.sector, 4)
    each = z.sector // many
    groups = [list(range(g * each, (g + 1) * each)) for g in range(many)]
    order = groups[1:] + groups[:1]

    def across(array, distance):
        return shift(array, "sector", z.sector, distance) if distance else array

    near = {}
    for distances in order:
        made = products(z, plan, right, near_rows, distances, 1)
        for distance, block in zip(distances, made):
            near[distance] = across(block, distance)
    vec = [near_rows]
    for other in others:
        vec.append([other] + [rows_for(other, s) for s in range(1, z.rep)])
    far_rows = [ref for piece in vec[1:] for ref in piece]
    far = {}
    for distances in order:
        made = products(z, plan, right, far_rows, distances, z.env - 1)
        for distance, block in zip(distances, made):
            far[distance] = across(block, distance)

    own_block = vectors.astype(jnp.float32)
    partial_sum = jnp.sum(energy[None, :, None, None] * own_block * own_block, axis=(1, 2, 3))
    parts = [[[] for _ in range(z.rep)] for _ in range(z.env)]
    dots = 0.0
    for distances in groups:
        blocks, folded = terms(
            z, plan, left, [near[d] for d in distances], [far[d] for d in distances], vec, distances
        )
        dots = dots + folded
        for e in range(z.env):
            for s in range(z.rep):
                block = blocks[e][s]
                parts[e][s].append(block if e + s == 0 else shift_both(z, block, e, s))
    image = make_image(z, plans, energy, vectors, parts)
    own_vector = (jnp.arange(z.batch) == core).astype(jnp.float32)
    partial_sum = partial_sum + own_vector * jnp.sum(dots)
    for axis in ("rep", "env", "sector"):
        partial_sum = total_over(partial_sum, axis)
    entries = z.slots * z.sector * z.order * z.order
    return (image, partial_sum / entries)


def solution(mesh):
    return jax.shard_map(
        on_device,
        mesh=mesh,
        in_specs=(
            P(None, ("groups", "sector"), ("env", "rep"), None),
            P("env", ("groups", "sector"), "rep", None),
            P("env", ("groups", "sector"), "rep", None),
            P(("groups", "sector")),
            P("env", "groups"),
        ),
        out_specs=(P(None, ("groups", "sector"), ("env", "rep"), None), P("groups")),
        check_vma=False,
    )
```

```python
import functools

import jax
import jax.numpy as jnp
from jax import lax
from jax.experimental import pallas as pl
from jax.experimental.pallas import tpu as pltpu
from jax.sharding import PartitionSpec as P

HBM = pl.BlockSpec(memory_space=pl.ANY)
SMEM = pl.BlockSpec(memory_space=pltpu.SMEM)
VMEM = pl.BlockSpec(memory_space=pltpu.VMEM)
LIMIT = 40 * 1024 * 1024
BRIEF = pl.CostEstimate(flops=0, bytes_accessed=0, transcendentals=0)


def aligned(index, size):
    return pl.multiple_of(index * size, size)


class Sizes:
    def __init__(self, vectors, left_env):
        self.env = lax.axis_size("env")
        self.rep = lax.axis_size("rep")
        self.sector = lax.axis_size("sector")
        self.batch, self.slots, self.own_rows, self.order = vectors.shape
        assert self.batch == self.rep
        self.half = left_env.shape[2]
        self.chip_rows = self.own_rows * self.rep
        self.capacity = 2 * ((self.slots + 2 * self.sector - 1) // (2 * self.sector))
        self.flat = self.sector * self.capacity
        self.source, self.target, self.valid = 0, self.flat, 2 * self.flat
        self.core, self.chip = 3 * self.flat, 3 * self.flat + 1


def plan_body(z, partner, ids, plan, count):
    def clear(i, carry):
        plan[i] = 0
        return carry

    lax.fori_loop(0, 3 * z.flat, clear, 0)
    for d in range(z.sector):
        count[d] = 0

    def place(j, carry):
        sector = partner[0, j]
        group = lax.div(sector, z.slots)
        slot = sector - group * z.slots
        distance = lax.rem(z.sector - group, z.sector)
        rank = count[distance]
        count[distance] = rank + 1
        index = distance * z.capacity + rank
        plan[z.source + index] = slot
        plan[z.target + index] = j
        plan[z.valid + index] = 1
        return carry

    lax.fori_loop(0, z.slots, place, 0)
    plan[z.core] = ids[0]
    plan[z.chip] = ids[1]


def make_plan(z, partner, ids):
    return pl.pallas_call(
        functools.partial(plan_body, z),
        out_shape=jax.ShapeDtypeStruct((3 * z.flat + 2,), jnp.int32),
        in_specs=[SMEM, SMEM],
        out_specs=SMEM,
        scratch_shapes=[pltpu.SMEM((z.sector,), jnp.int32)],
        cost_estimate=BRIEF,
    )(partner, ids)


def pick(z, core, place, candidates):
    chosen = candidates[0]
    for s in range(1, z.rep):
        chosen = jnp.where(lax.rem(core + z.rep - s, z.rep) == place, candidates[s], chosen)
    return chosen


def products_body(z, first, pieces, blocks, *refs):
    refs = list(refs)
    plan = refs.pop(0)
    right = [refs.pop(0) for _ in range(z.rep)]
    rows = [[refs.pop(0) for _ in range(z.rep)] for _ in range(pieces)]
    outs = refs[-blocks:]
    core = plan[z.core]
    for d, out in enumerate(outs):
        for i in range(out.shape[0]):
            slot = plan[z.source + first + d * z.capacity + i]
            halves = [ref[0, slot] for ref in right]
            parts = [[ref[core, slot] for ref in piece] for piece in rows]
            block = jnp.concatenate([pick(z, core, k, halves) for k in range(z.rep)], axis=0)
            lines = jnp.concatenate(
                [pick(z, core, k, part) for part in parts for k in range(z.rep)], axis=0
            )
            out[i] = lax.dot_general(
                lines, block, (((1,), (1,)), ((), ())), preferred_element_type=jnp.float32
            ).astype(jnp.bfloat16)


def products(z, plan, right, rows, first, sizes, after=()):
    pieces = len(rows)
    flat = [ref for piece in rows for ref in piece]
    height = pieces * z.chip_rows
    count = sum(sizes)
    return pl.pallas_call(
        functools.partial(products_body, z, first, pieces, len(sizes)),
        out_shape=[
            jax.ShapeDtypeStruct((size, height, z.order), jnp.bfloat16) for size in sizes
        ],
        in_specs=[SMEM] + [VMEM] * (len(right) + len(flat)) + [HBM] * len(after),
        out_specs=[VMEM] * len(sizes),
        compiler_params=pltpu.CompilerParams(vmem_limit_bytes=LIMIT),
        cost_estimate=BRIEF,
    )(plan, *right, *flat, *after)


def terms_body(z, first, groups, *refs):
    refs = list(refs)
    plan = refs.pop(0)
    left = [refs.pop(0) for _ in range(z.rep)]
    near = [refs.pop(0) for _ in range(groups)]
    far = [refs.pop(0) for _ in range(groups)]
    vec = [[refs.pop(0) for _ in range(z.rep)] for _ in range(z.env)]
    pbuf, tbuf = refs[-2:]
    dots = refs[-3]
    outs = refs[-3 - z.env * z.rep : -3]
    core, chip = plan[z.core], plan[z.chip]
    total = jnp.zeros(dots.shape, jnp.float32)
    n = 0
    for d in range(groups):
        for i in range(near[d].shape[0]):
            flat = first + d * z.capacity + i
            slot = plan[z.target + flat]
            for e in range(z.env):
                place = lax.rem(chip + z.env - e, z.env)
                if e == 0:
                    lines = near[d][i]
                else:
                    lines = far[d][i, (e - 1) * z.chip_rows : e * z.chip_rows]
                pbuf[n, pl.ds(aligned(place, z.chip_rows), z.chip_rows)] = lines
            halves = [ref[0, slot] for ref in left]
            block = jnp.concatenate([pick(z, core, k, halves) for k in range(z.rep)], axis=0)
            tbuf[n] = jnp.dot(block, pbuf[n], preferred_element_type=jnp.float32).astype(
                jnp.bfloat16
            )
            folded = jnp.zeros(dots.shape, jnp.float32)
            for e in range(z.env):
                for s in range(z.rep):
                    place = lax.rem(chip + e, z.env) * z.rep + lax.rem(core + s, z.rep)
                    term = tbuf[n, pl.ds(aligned(place, z.own_rows), z.own_rows)]
                    outs[e * z.rep + s][n] = term
                    lines = vec[(z.env - e) % z.env][(z.rep - s) % z.rep][core, slot]
                    both = lines.astype(jnp.float32) * term.astype(jnp.float32)
                    folded += jnp.sum(both.reshape(-1, *dots.shape), axis=0)
            total += jnp.where(plan[z.valid + flat] == 1, folded, 0.0)
            n += 1
    dots[...] = total


def terms(z, plan, left, near, far, vec, first, after=()):
    groups = len(near)
    count = sum(block.shape[0] for block in near)
    flat = [ref for piece in vec for ref in piece]
    block = jax.ShapeDtypeStruct((count, z.own_rows, z.order), jnp.bfloat16)
    whole = (count, z.order, z.order)
    made = pl.pallas_call(
        functools.partial(terms_body, z, first, groups),
        out_shape=[block] * (z.env * z.rep) + [jax.ShapeDtypeStruct((8, z.order), jnp.float32)],
        in_specs=[SMEM]
        + [VMEM] * (len(left) + len(near) + len(far) + len(flat))
        + [HBM] * len(after),
        out_specs=[VMEM] * (z.env * z.rep + 1),
        scratch_shapes=[pltpu.VMEM(whole, jnp.bfloat16), pltpu.VMEM(whole, jnp.bfloat16)],
        compiler_params=pltpu.CompilerParams(vmem_limit_bytes=LIMIT),
        cost_estimate=BRIEF,
    )(plan, *left, *near, *far, *flat, *after)
    blocks = [made[e * z.rep : (e + 1) * z.rep] for e in range(z.env)]
    return blocks, made[-1]


def image_body(z, sizes, *refs):
    refs = list(refs)
    plans = [refs.pop(0) for _ in range(z.env)]
    energy, vectors = refs.pop(0), refs.pop(0)
    parts = [[[refs.pop(0) for _ in sizes] for _ in range(z.rep)] for _ in range(z.env)]
    image = refs.pop(0)
    core = plans[0][z.core]

    def start(j, carry):
        for v in range(z.batch):
            image[v, j] = energy[j] * vectors[v, j].astype(jnp.float32)
        return carry

    lax.fori_loop(0, z.slots, start, 0)
    for e, plan in enumerate(plans):
        first = 0
        for g, count in enumerate(sizes):

            def add(n, carry):
                slot = plan[z.target + first + n]

                @pl.when(plan[z.valid + first + n] == 1)
                def _():
                    for s in range(z.rep):
                        v = lax.rem(core + z.rep - s, z.rep)
                        image[v, slot] += parts[e][s][g][n].astype(jnp.float32)

                return carry

            lax.fori_loop(0, count, add, 0)
            first += count


def make_image(z, plans, energy, vectors, parts):
    sizes = tuple(block.shape[0] for block in parts[0][0])
    flat = [ref for piece in parts for kind in piece for ref in kind]
    return pl.pallas_call(
        functools.partial(image_body, z, sizes),
        out_shape=jax.ShapeDtypeStruct(vectors.shape, jnp.float32),
        in_specs=[SMEM] * (z.env + 1) + [VMEM] * (len(flat) + 1),
        out_specs=VMEM,
        compiler_params=pltpu.CompilerParams(vmem_limit_bytes=LIMIT),
        cost_estimate=BRIEF,
    )(*plans, energy, vectors, *flat)


def shift(array, axis, size, step):
    return lax.ppermute(array, axis, [(i, (i + step) % size) for i in range(size)])


def shift_both(z, array, e, s):
    perm = []
    for x in range(z.env):
        for c in range(z.rep):
            perm.append((x * z.rep + c, (x + e) % z.env * z.rep + (c + s) % z.rep))
    return lax.ppermute(array, ("env", "rep"), perm)


def total_over(array, axis):
    size = lax.axis_size(axis)
    if size & (size - 1):
        return lax.psum(array, axis)
    step = 1
    while step < size:
        array = array + lax.ppermute(array, axis, [(i, i ^ step) for i in range(size)])
        step *= 2
    return array


def on_device(vectors, left_env, right_env, energy, partner):
    z = Sizes(vectors, left_env)
    core, chip = lax.axis_index("rep"), lax.axis_index("env")
    ids = jnp.stack([core, chip]).astype(jnp.int32)

    def around(array):
        return [array] + [shift(array, "rep", z.rep, s) for s in range(1, z.rep)]

    def across(array, distance):
        return shift(array, "sector", z.sector, distance) if distance else array

    others = [shift(vectors, "env", z.env, e) for e in range(1, z.env)]
    right = around(right_env)
    near_rows = around(vectors)
    plan = make_plan(z, partner, ids)
    plans = [plan]
    for e in range(1, z.env):
        plans.append(make_plan(z, shift(partner, "env", z.env, e), ids))

    many = min(z.sector, 4)
    each = z.sector // many
    sizes = [z.capacity] * each

    near, made_near, chain = {}, [], ()
    for g in [*range(1, many), 0]:
        made = products(z, plan, right, [near_rows], g * each * z.capacity, sizes, chain)
        chain = made[:1]
        made_near += made[:1]
        near[g] = [across(block, g * each + d) for d, block in enumerate(made)]
    left_env, *made_near = lax.optimization_barrier((left_env, *made_near))
    left = around(left_env)

    others, chain = lax.optimization_barrier((others, chain))
    vec = [near_rows] + [around(other) for other in others]
    far, parts, dots = {}, [[[None] * many for _ in range(z.rep)] for _ in range(z.env)], 0.0

    def send_products(g, after):
        made = products(z, plan, right, vec[1:], g * each * z.capacity, sizes, after)
        far[g] = [across(block, g * each + d) for d, block in enumerate(made)]
        return made[:1]

    def send_terms(g, after):
        blocks, folded = terms(z, plan, left, near[g], far[g], vec, g * each * z.capacity, after)
        for e in range(z.env):
            for s in range(z.rep):
                block = blocks[e][s]
                parts[e][s][g] = block if e + s == 0 else shift_both(z, block, e, s)
        return folded

    ways = [*range(1, many, 2), *range(2, many, 2)]
    chain = send_products(ways[0], chain)
    chain = send_products(0, chain)
    folded = send_terms(0, chain)
    dots += folded
    chain = (folded,)
    for i, g in enumerate(ways[1:]):
        held = near[ways[i]] if i == 0 else far[ways[i - 1]]
        chain = send_products(g, (*chain, held[-1]))
    for g in ways:
        folded = send_terms(g, chain)
        dots += folded
        chain = (folded,)
    image = make_image(z, plans, energy, vectors, parts)
    own_block = vectors.astype(jnp.float32)
    partial_sum = jnp.sum(energy[None, :, None, None] * own_block * own_block, axis=(1, 2, 3))
    own_vector = (jnp.arange(z.batch) == core).astype(jnp.float32)
    partial_sum = partial_sum + own_vector * jnp.sum(dots)
    for axis in ("rep", "env", "sector"):
        partial_sum = total_over(partial_sum, axis)
    entries = z.slots * z.sector * z.order * z.order
    return (image, partial_sum / entries)


def solution(mesh):
    return jax.shard_map(
        on_device,
        mesh=mesh,
        in_specs=(
            P(None, ("groups", "sector"), ("env", "rep"), None),
            P("env", ("groups", "sector"), "rep", None),
            P("env", ("groups", "sector"), "rep", None),
            P(("groups", "sector")),
            P("env", "groups"),
        ),
        out_specs=(P(None, ("groups", "sector"), ("env", "rep"), None), P("groups")),
        check_vma=False,
    )
```

```python
import functools

import jax
import jax.numpy as jnp
from jax import lax
from jax.experimental import pallas as pl
from jax.experimental.pallas import tpu as pltpu
from jax.sharding import PartitionSpec as P

ANY = pl.BlockSpec(memory_space=pl.ANY)
HBM = pl.BlockSpec(memory_space=pltpu.HBM)
SMEM = pl.BlockSpec(memory_space=pltpu.SMEM)
VMEM = pl.BlockSpec(memory_space=pltpu.VMEM)
LIMIT = 40 * 1024 * 1024
BRIEF = pl.CostEstimate(flops=0, bytes_accessed=0, transcendentals=0)


def aligned(index, size):
    return pl.multiple_of(index * size, size)


class Sizes:
    def __init__(self, vectors, left_env):
        self.env = lax.axis_size("env")
        self.rep = lax.axis_size("rep")
        self.sector = lax.axis_size("sector")
        self.batch, self.slots, self.own_rows, self.order = vectors.shape
        assert self.batch == self.rep and self.sector % 4 == 0
        self.half = left_env.shape[2]
        self.chip_rows = self.own_rows * self.rep
        self.capacity = 2 * ((self.slots + 2 * self.sector - 1) // (2 * self.sector))
        self.flat = self.sector * self.capacity
        self.full = self.flat == self.slots
        self.source, self.target, self.valid = 0, self.flat, 2 * self.flat
        self.core, self.chip = 3 * self.flat, 3 * self.flat + 1

    def when_valid(self, plan, flat, action):
        if self.full:
            action()
        else:
            pl.when(plan[self.valid + flat] == 1)(action)


def write_plan(z, partner, plan, count):
    if not z.full:

        def clear(i, carry):
            plan[i] = 0
            return carry

        lax.fori_loop(0, 3 * z.flat, clear, 0)
    for d in range(z.sector):
        count[d] = 0
    for j in range(z.slots):
        sector = partner[0, j]
        group = lax.div(sector, z.slots)
        slot = sector - group * z.slots
        distance = lax.rem(z.sector - group, z.sector)
        rank = count[distance]
        count[distance] = rank + 1
        index = distance * z.capacity + rank
        plan[z.source + index] = slot
        plan[z.target + index] = j
        plan[z.valid + index] = 1
    plan[z.core] = lax.axis_index("rep")
    plan[z.chip] = lax.axis_index("env")


def load_body(z, partner, vectors, right, plan, *refs):
    rows, block, count, sem = refs[: z.rep], refs[z.rep], refs[-2], refs[-1]
    core = lax.axis_index("rep")
    copies = [pltpu.make_async_copy(right, block, sem.at[z.rep])]
    for s, ref in enumerate(rows):
        copies.append(
            pltpu.make_async_copy(vectors.at[lax.rem(core + s, z.rep)], ref, sem.at[s])
        )
    for copy in copies:
        copy.start()
    write_plan(z, partner, plan, count)
    for copy in copies:
        copy.wait()


def load(z, partner, vectors, right_env):
    row = jax.ShapeDtypeStruct(vectors.shape[1:], jnp.bfloat16)
    plan, *made = pl.pallas_call(
        functools.partial(load_body, z),
        out_shape=[jax.ShapeDtypeStruct((3 * z.flat + 2,), jnp.int32)]
        + [row] * z.rep
        + [jax.ShapeDtypeStruct(right_env.shape, jnp.bfloat16)],
        in_specs=[SMEM, HBM, HBM],
        out_specs=[SMEM] + [VMEM] * (z.rep + 1),
        scratch_shapes=[pltpu.SMEM((z.sector,), jnp.int32), pltpu.SemaphoreType.DMA((z.rep + 1,))],
        compiler_params=pltpu.CompilerParams(vmem_limit_bytes=LIMIT),
        cost_estimate=BRIEF,
    )(
        partner,
        pltpu.with_memory_space_constraint(vectors, pltpu.HBM),
        pltpu.with_memory_space_constraint(right_env, pltpu.HBM),
    )
    return plan, made[: z.rep], made[z.rep]


def plan_only(z, partner):
    return pl.pallas_call(
        functools.partial(write_plan, z),
        out_shape=jax.ShapeDtypeStruct((3 * z.flat + 2,), jnp.int32),
        in_specs=[SMEM],
        out_specs=SMEM,
        scratch_shapes=[pltpu.SMEM((z.sector,), jnp.int32)],
        cost_estimate=BRIEF,
    )(partner)


def gate(arrays, after):
    def body(*refs):
        pass

    return pl.pallas_call(
        body,
        out_shape=[jax.ShapeDtypeStruct(a.shape, a.dtype) for a in arrays],
        in_specs=[ANY] * (len(arrays) + len(after)),
        out_specs=[ANY] * len(arrays),
        input_output_aliases={i: i for i in range(len(arrays))},
        cost_estimate=BRIEF,
    )(*arrays, *after)


def pick(z, core, place, candidates):
    chosen = candidates[0]
    for s in range(1, z.rep):
        chosen = jnp.where(lax.rem(core + z.rep - s, z.rep) == place, candidates[s], chosen)
    return chosen


def products_body(z, pieces, spans, copied, *refs):
    refs = list(refs)
    if copied:
        sem = refs.pop()
        copy = pltpu.make_async_copy(refs[1 + z.rep * (1 + pieces)], refs.pop(), sem)
        copy.start()
    plan = refs.pop(0)
    right = [refs.pop(0) for _ in range(z.rep)]
    rows = [[refs.pop(0) for _ in range(z.rep)] for _ in range(pieces)]
    outs = refs[-len(spans) :]
    core = plan[z.core]
    for (first, count), out in zip(spans, outs):
        for i in range(count):
            slot = plan[z.source + first + i]
            halves = [ref[0, slot] for ref in right]
            parts = [[ref[slot] for ref in piece] for piece in rows]
            block = jnp.concatenate([pick(z, core, k, halves) for k in range(z.rep)], axis=0)
            lines = jnp.concatenate(
                [pick(z, core, k, part) for part in parts for k in range(z.rep)], axis=0
            )
            out[i] = lax.dot_general(
                lines, block, (((1,), (1,)), ((), ())), preferred_element_type=jnp.float32
            ).astype(jnp.bfloat16)
    if copied:
        copy.wait()


def products(z, plan, right, rows, spans, after=(), copied=None):
    pieces = len(rows)
    flat = [ref for piece in rows for ref in piece]
    height = pieces * z.chip_rows
    shapes = [(count, height, z.order) for _, count in spans]
    scratch = []
    if copied is not None:
        shapes.append(copied.shape)
        scratch = [pltpu.SemaphoreType.DMA]
        after = (pltpu.with_memory_space_constraint(copied, pltpu.HBM), *after)
    return pl.pallas_call(
        functools.partial(products_body, z, pieces, spans, copied is not None),
        out_shape=[jax.ShapeDtypeStruct(shape, jnp.bfloat16) for shape in shapes],
        in_specs=[SMEM]
        + [VMEM] * (len(right) + len(flat))
        + [HBM if copied is not None and i == 0 else ANY for i in range(len(after))],
        out_specs=[VMEM] * len(shapes),
        scratch_shapes=scratch,
        compiler_params=pltpu.CompilerParams(vmem_limit_bytes=LIMIT),
        cost_estimate=BRIEF,
    )(plan, *right, *flat, *after)


def terms_body(z, spans, *refs):
    refs = list(refs)
    plan = refs.pop(0)
    left = [refs.pop(0) for _ in range(z.rep)]
    near = [refs.pop(0) for _ in spans]
    far = [refs.pop(0) for _ in spans]
    vec = [[refs.pop(0) for _ in range(z.rep)] for _ in range(z.env)]
    pbuf, tbuf = refs[-2:]
    dots = refs[-3]
    outs = refs[-3 - z.env * z.rep : -3]
    core, chip = plan[z.core], plan[z.chip]
    total = jnp.zeros(dots.shape, jnp.float32)
    n = 0
    for d, (first, count, skip) in enumerate(spans):
        for i in range(count):
            slot = plan[z.target + first + i]
            for e in range(z.env):
                place = lax.rem(chip + z.env - e, z.env)
                if e == 0:
                    lines = near[d][skip + i]
                else:
                    lines = far[d][i, (e - 1) * z.chip_rows : e * z.chip_rows]
                pbuf[n, pl.ds(aligned(place, z.chip_rows), z.chip_rows)] = lines
            halves = [ref[0, slot] for ref in left]
            block = jnp.concatenate([pick(z, core, k, halves) for k in range(z.rep)], axis=0)
            tbuf[n] = jnp.dot(block, pbuf[n], preferred_element_type=jnp.float32).astype(
                jnp.bfloat16
            )
            folded = jnp.zeros(dots.shape, jnp.float32)
            for e in range(z.env):
                for s in range(z.rep):
                    place = lax.rem(chip + e, z.env) * z.rep + lax.rem(core + s, z.rep)
                    term = tbuf[n, pl.ds(aligned(place, z.own_rows), z.own_rows)]
                    outs[e * z.rep + s][n] = term
                    lines = vec[(z.env - e) % z.env][(z.rep - s) % z.rep][slot]
                    both = lines.astype(jnp.float32) * term.astype(jnp.float32)
                    folded += jnp.sum(both.reshape(-1, *dots.shape), axis=0)
            if not z.full:
                folded = jnp.where(plan[z.valid + first + i] == 1, folded, 0.0)
            total += folded
            n += 1
    dots[...] = total


def terms(z, plan, left, near, far, vec, spans, after=()):
    count = sum(span[1] for span in spans)
    flat = [ref for piece in vec for ref in piece]
    shapes = [(count, z.own_rows, z.order)] * (z.env * z.rep)
    whole = (count, z.order, z.order)
    *made, dots = pl.pallas_call(
        functools.partial(terms_body, z, spans),
        out_shape=[jax.ShapeDtypeStruct(shape, jnp.bfloat16) for shape in shapes]
        + [jax.ShapeDtypeStruct((8, z.order), jnp.float32)],
        in_specs=[SMEM]
        + [VMEM] * (len(left) + len(near) + len(far) + len(flat))
        + [ANY] * len(after),
        out_specs=[VMEM] * (len(shapes) + 1),
        scratch_shapes=[pltpu.VMEM(whole, jnp.bfloat16), pltpu.VMEM(whole, jnp.bfloat16)],
        compiler_params=pltpu.CompilerParams(vmem_limit_bytes=LIMIT),
        cost_estimate=BRIEF,
    )(plan, *left, *near, *far, *flat, *after)
    return made, dots


def add_terms(z, plans, image, parts, spans):
    core = plans[0][z.core]
    n = 0
    for first, count, _ in spans:
        for i in range(count):
            for e, plan in enumerate(plans):

                def add():
                    slot = plan[z.target + first + i]
                    for s in range(z.rep):
                        v = lax.rem(core + z.rep - s, z.rep)
                        image[v, slot] += parts[e][s][n].astype(jnp.float32)

                z.when_valid(plan, first + i, add)
            n += 1


def gather_body(z, chunks, *refs):
    refs = list(refs)
    plans = [refs.pop(0) for _ in range(z.env)]
    energy, vectors, image = refs.pop(0), refs.pop(0), refs[-1]

    def start(j, carry):
        for v in range(z.batch):
            image[v, j] = energy[j] * vectors[v, j].astype(jnp.float32)
        return carry

    lax.fori_loop(0, z.slots, start, 0, unroll=2)
    for spans in chunks:
        parts = [[refs.pop(0) for _ in range(z.rep)] for _ in range(z.env)]
        add_terms(z, plans, image, parts, spans)


def gather_terms(z, plans, energy, vectors, parts, chunks, after=()):
    flat = [ref for chunk in parts for piece in chunk for ref in piece]
    return pl.pallas_call(
        functools.partial(gather_body, z, chunks),
        out_shape=jax.ShapeDtypeStruct(vectors.shape, jnp.float32),
        in_specs=[SMEM] * (z.env + 1) + [VMEM] * (1 + len(flat)) + [ANY] * len(after),
        out_specs=VMEM,
        compiler_params=pltpu.CompilerParams(vmem_limit_bytes=LIMIT),
        cost_estimate=BRIEF,
    )(*plans, energy, vectors, *flat, *after)


def image_body(z, spans, *refs):
    refs = list(refs)
    plans = [refs.pop(0) for _ in range(z.env)]
    so_far = refs.pop(0)
    image = refs.pop()
    parts = [[refs.pop(0) for _ in range(z.rep)] for _ in range(z.env)]

    def start(j, carry):
        for v in range(z.batch):
            image[v, j] = so_far[v, j]
        return carry

    lax.fori_loop(0, z.slots, start, 0, unroll=2)
    add_terms(z, plans, image, parts, spans)


def make_image(z, plans, so_far, parts, spans):
    flat = [ref for piece in parts for ref in piece]
    return pl.pallas_call(
        functools.partial(image_body, z, spans),
        out_shape=jax.ShapeDtypeStruct(so_far.shape, jnp.float32),
        in_specs=[SMEM] * z.env + [VMEM] * (1 + len(flat)),
        out_specs=VMEM,
        compiler_params=pltpu.CompilerParams(vmem_limit_bytes=LIMIT),
        cost_estimate=BRIEF,
    )(*plans, so_far, *flat)


def shift(array, axis, size, step):
    return lax.ppermute(array, axis, [(i, (i + step) % size) for i in range(size)])


def shift_both(z, array, e, s):
    perm = []
    for x in range(z.env):
        for c in range(z.rep):
            perm.append((x * z.rep + c, (x + e) % z.env * z.rep + (c + s) % z.rep))
    return lax.ppermute(array, ("env", "rep"), perm)


def total_over(array, axis):
    size = lax.axis_size(axis)
    if size & (size - 1):
        return lax.psum(array, axis)
    step = 1
    while step < size:
        array = array + lax.ppermute(array, axis, [(i, i ^ step) for i in range(size)])
        step *= 2
    return array


def on_device(vectors, left_env, right_env, energy, partner):
    z = Sizes(vectors, left_env)
    each = z.sector // 4
    span = z.capacity

    def spans_of(g, low=0, count=span):
        return [((g * each + d) * span + low, count, low) for d in range(each)]

    def plain(spans):
        return tuple(piece[:2] for piece in spans)

    def around(array):
        return [array] + [shift(array, "rep", z.rep, s) for s in range(1, z.rep)]

    def across(arrays, g):
        steps = [g * each + d for d in range(each)]
        return [shift(a, "sector", z.sector, k) if k else a for a, k in zip(arrays, steps)]

    right_others = around(right_env)[1:]
    plan, own, right_own = load(z, partner, vectors, right_env)
    right = [right_own] + right_others
    near_rows = [own[0]] + [shift(own[s], "rep", z.rep, s) for s in range(1, z.rep)]
    vec = [near_rows]
    for e in range(1, z.env):
        vec.append([shift_both(z, own[s], e, s) for s in range(z.rep)])
    plans = [plan]
    for e in range(1, z.env):
        plans.append(plan_only(z, shift(partner, "env", z.env, e)))

    near = {}
    *made, left_own = products(z, plan, right, [near_rows], plain(spans_of(1)), (), left_env)
    near[1] = across(made, 1)
    left = around(left_own)
    made = products(z, plan, right, [near_rows], plain(spans_of(3)), made[:1])
    near[3] = across(made, 3)
    made = products(z, plan, right, [near_rows], plain(spans_of(2)), (made[0], *left[1:]))
    near[2] = across(made, 2)
    chain = (made[0], *plans[1:])

    chunks = {g: spans_of(g) for g in range(4)}
    far, parts = {}, {}

    def far_products(g, spans, after):
        return products(z, plan, right, vec[1:], plain(spans), after)

    def send_terms(g, after):
        made, folded = terms(z, plan, left, near[g], far[g], vec, chunks[g], after)
        parts[g] = [
            [
                shift_both(z, made[e * z.rep + s], e, s) if e + s else made[0]
                for s in range(z.rep)
            ]
            for e in range(z.env)
        ]
        return folded

    def arrived(g):
        return [part for piece in parts[g] for part in piece][1:]

    made = far_products(1, chunks[1], chain)
    sent = [array for g in (1, 3, 2) for array in near[g]]
    far[1] = across(gate(made, sent), 1)
    near[0] = products(z, plan, right, [near_rows], plain(chunks[0]), made[:1])
    far[0] = far_products(0, chunks[0], near[0][:1])
    dot0 = send_terms(0, ())
    made = far_products(3, chunks[3], (dot0,))
    far[3] = across(made, 3)
    made = far_products(2, chunks[2], (made[0], far[1][0]))
    far[2] = across(made, 2)
    dot1 = send_terms(1, made[:1])
    dot3 = send_terms(3, (dot1, *arrived(0)))
    dot2 = send_terms(2, (dot3, *arrived(1), *arrived(3)))
    early = (0, 1, 3)
    so_far = gather_terms(
        z,
        plans,
        energy,
        vectors,
        [parts[g] for g in early],
        [chunks[g] for g in early],
        (dot2,),
    )
    image = make_image(z, plans, so_far, parts[2], chunks[2])

    own_block = vectors.astype(jnp.float32)
    partial_sum = jnp.sum(energy[None, :, None, None] * own_block * own_block, axis=(1, 2, 3))
    own_vector = (jnp.arange(z.batch) == lax.axis_index("rep")).astype(jnp.float32)
    partial_sum = partial_sum + own_vector * jnp.sum(dot0 + dot1 + dot2 + dot3)
    for axis in ("sector", "env", "rep"):
        partial_sum = total_over(partial_sum, axis)
    entries = z.slots * z.sector * z.order * z.order
    return (image, partial_sum / entries)


def solution(mesh):
    return jax.shard_map(
        on_device,
        mesh=mesh,
        in_specs=(
            P(None, ("groups", "sector"), ("env", "rep"), None),
            P("env", ("groups", "sector"), "rep", None),
            P("env", ("groups", "sector"), "rep", None),
            P(("groups", "sector")),
            P("env", "groups"),
        ),
        out_specs=(P(None, ("groups", "sector"), ("env", "rep"), None), P("groups")),
        check_vma=False,
    )
```

```python
import functools

import jax
import jax.numpy as jnp
from jax import lax
from jax.experimental import pallas as pl
from jax.experimental.pallas import tpu as pltpu
from jax.sharding import PartitionSpec as P

ANY = pl.BlockSpec(memory_space=pl.ANY)
HBM = pl.BlockSpec(memory_space=pltpu.HBM)
SMEM = pl.BlockSpec(memory_space=pltpu.SMEM)
VMEM = pl.BlockSpec(memory_space=pltpu.VMEM)
LIMIT = 12 * 1024 * 1024
TAIL = 16
BRIEF = pl.CostEstimate(flops=0, bytes_accessed=0, transcendentals=0)


def aligned(index, size):
    return pl.multiple_of(index * size, size)


class Sizes:
    def __init__(self, vectors, left_env):
        self.env = lax.axis_size("env")
        self.rep = lax.axis_size("rep")
        self.sector = lax.axis_size("sector")
        self.batch, self.slots, self.own_rows, self.order = vectors.shape
        assert self.batch == self.rep and self.sector % 4 == 0
        self.half = left_env.shape[2]
        self.chip_rows = self.own_rows * self.rep
        self.capacity = 2 * ((self.slots + 2 * self.sector - 1) // (2 * self.sector))
        self.flat = self.sector * self.capacity
        self.full = self.flat == self.slots
        self.source, self.target, self.valid = 0, self.flat, 2 * self.flat
        self.core, self.chip = 3 * self.flat, 3 * self.flat + 1

    def when_valid(self, plan, flat, action):
        if self.full:
            action()
        else:
            pl.when(plan[self.valid + flat] == 1)(action)


def write_plan(z, partner, plan, count):
    if not z.full:

        def clear(i, carry):
            plan[i] = 0
            return carry

        lax.fori_loop(0, 3 * z.flat, clear, 0)
    for d in range(z.sector):
        count[d] = 0
    for j in range(z.slots):
        sector = partner[0, j]
        group = lax.div(sector, z.slots)
        slot = sector - group * z.slots
        distance = lax.rem(z.sector - group, z.sector)
        rank = count[distance]
        count[distance] = rank + 1
        index = distance * z.capacity + rank
        plan[z.source + index] = slot
        plan[z.target + index] = j
        plan[z.valid + index] = 1
    plan[z.core] = lax.axis_index("rep")
    plan[z.chip] = lax.axis_index("env")


def split_copy(source, target, slots, sem):
    step = slots // 4 if slots % 4 == 0 else slots
    copies = []
    for i in range(slots // step):
        part = pl.ds(i * step, step)
        copies.append(pltpu.make_async_copy(source.at[part], target.at[part], sem.at[i]))
    return copies


def load_body(z, partner, vectors, right, plan, *refs):
    rows, block, count, sem = refs[: z.rep], refs[z.rep], refs[-2], refs[-1]
    core = lax.axis_index("rep")
    copies = []
    for s, ref in enumerate(rows):
        mine = vectors.at[lax.rem(core + s, z.rep)]
        copies += split_copy(mine, ref, z.slots, sem.at[s])
    copies += split_copy(right.at[0], block.at[0], z.slots, sem.at[z.rep])
    for copy in copies:
        copy.start()
    write_plan(z, partner, plan, count)
    for copy in copies:
        copy.wait()


def load(z, partner, vectors, right_env):
    row = jax.ShapeDtypeStruct(vectors.shape[1:], jnp.bfloat16)
    plan, *made = pl.pallas_call(
        functools.partial(load_body, z),
        out_shape=[jax.ShapeDtypeStruct((3 * z.flat + 2,), jnp.int32)]
        + [row] * z.rep
        + [jax.ShapeDtypeStruct(right_env.shape, jnp.bfloat16)],
        in_specs=[SMEM, HBM, HBM],
        out_specs=[SMEM] + [VMEM] * (z.rep + 1),
        scratch_shapes=[
            pltpu.SMEM((z.sector,), jnp.int32),
            pltpu.SemaphoreType.DMA((z.rep + 1, 4)),
        ],
        compiler_params=pltpu.CompilerParams(vmem_limit_bytes=LIMIT),
        cost_estimate=BRIEF,
    )(
        partner,
        pltpu.with_memory_space_constraint(vectors, pltpu.HBM),
        pltpu.with_memory_space_constraint(right_env, pltpu.HBM),
    )
    return plan, made[: z.rep], made[z.rep]


def plan_only(z, partner):
    return pl.pallas_call(
        functools.partial(write_plan, z),
        out_shape=jax.ShapeDtypeStruct((3 * z.flat + 2,), jnp.int32),
        in_specs=[SMEM],
        out_specs=SMEM,
        scratch_shapes=[pltpu.SMEM((z.sector,), jnp.int32)],
        cost_estimate=BRIEF,
    )(partner)


def gate(arrays, after):
    def body(*refs):
        pass

    return pl.pallas_call(
        body,
        out_shape=[jax.ShapeDtypeStruct(a.shape, a.dtype) for a in arrays],
        in_specs=[ANY] * (len(arrays) + len(after)),
        out_specs=[ANY] * len(arrays),
        input_output_aliases={i: i for i in range(len(arrays))},
        cost_estimate=BRIEF,
    )(*arrays, *after)


def pick(z, core, place, candidates):
    chosen = candidates[0]
    for s in range(1, z.rep):
        chosen = jnp.where(lax.rem(core + z.rep - s, z.rep) == place, candidates[s], chosen)
    return chosen


def line(ref, core, slot):
    return ref[core, slot] if len(ref.shape) == 4 else ref[slot]


def products_body(z, pieces, spans, *refs):
    refs = list(refs)
    plan = refs.pop(0)
    right = [refs.pop(0) for _ in range(z.rep)]
    rows = [[refs.pop(0) for _ in range(z.rep)] for _ in range(pieces)]
    outs = refs[-len(spans) :]
    core = plan[z.core]
    for (first, count), out in zip(spans, outs):
        for i in range(count):
            slot = plan[z.source + first + i]
            halves = [ref[0, slot] for ref in right]
            parts = [[line(ref, core, slot) for ref in piece] for piece in rows]
            block = jnp.concatenate([pick(z, core, k, halves) for k in range(z.rep)], axis=0)
            lines = jnp.concatenate(
                [pick(z, core, k, part) for part in parts for k in range(z.rep)], axis=0
            )
            out[i] = lax.dot_general(
                lines, block, (((1,), (1,)), ((), ())), preferred_element_type=jnp.float32
            ).astype(jnp.bfloat16)


def products(z, plan, right, rows, spans, after=()):
    pieces = len(rows)
    flat = [ref for piece in rows for ref in piece]
    height = pieces * z.chip_rows
    return pl.pallas_call(
        functools.partial(products_body, z, pieces, spans),
        out_shape=[
            jax.ShapeDtypeStruct((count, height, z.order), jnp.bfloat16) for _, count in spans
        ],
        in_specs=[SMEM] + [VMEM] * (len(right) + len(flat)) + [ANY] * len(after),
        out_specs=[VMEM] * len(spans),
        compiler_params=pltpu.CompilerParams(vmem_limit_bytes=LIMIT),
        cost_estimate=BRIEF,
    )(plan, *right, *flat, *after)


def terms_body(z, spans, chained, last, *refs):
    refs = list(refs)
    plan = refs.pop(0)
    left = [refs.pop(0) for _ in range(z.rep)]
    near = [refs.pop(0) for _ in spans]
    far = [refs.pop(0) for _ in spans]
    vec = [[refs.pop(0) for _ in range(z.rep)] for _ in range(z.env)]
    so_far = refs.pop(0) if chained else None
    own_sums = refs.pop(0) if last else None
    pbuf, tbuf = refs[-2:]
    dots = refs[-3]
    outs = refs[-3 - z.env * z.rep : -3]
    core, chip = plan[z.core], plan[z.chip]
    total = so_far[...] if chained else jnp.zeros((8, z.order), jnp.float32)
    n = 0
    for d, (first, count, skip) in enumerate(spans):
        for i in range(count):
            slot = plan[z.target + first + i]
            for e in range(z.env):
                place = lax.rem(chip + z.env - e, z.env)
                if e == 0:
                    lines = near[d][skip + i]
                else:
                    lines = far[d][i, (e - 1) * z.chip_rows : e * z.chip_rows]
                pbuf[n, pl.ds(aligned(place, z.chip_rows), z.chip_rows)] = lines
            halves = [ref[0, slot] for ref in left]
            block = jnp.concatenate([pick(z, core, k, halves) for k in range(z.rep)], axis=0)
            tbuf[n] = jnp.dot(block, pbuf[n], preferred_element_type=jnp.float32).astype(
                jnp.bfloat16
            )
            folded = jnp.zeros(total.shape, jnp.float32)
            for e in range(z.env):
                for s in range(z.rep):
                    place = lax.rem(chip + e, z.env) * z.rep + lax.rem(core + s, z.rep)
                    term = tbuf[n, pl.ds(aligned(place, z.own_rows), z.own_rows)]
                    if last and e + s:
                        outs[e * z.rep + s][n * z.own_rows : (n + 1) * z.own_rows] = term
                    else:
                        outs[e * z.rep + s][n] = term
                    lines = line(vec[(z.env - e) % z.env][(z.rep - s) % z.rep], core, slot)
                    both = lines.astype(jnp.float32) * term.astype(jnp.float32)
                    folded += jnp.sum(both.reshape(-1, *total.shape), axis=0)
            if not z.full:
                folded = jnp.where(plan[z.valid + first + i] == 1, folded, 0.0)
            total += folded
            n += 1
    if not last:
        dots[...] = total
        return
    row = lax.broadcasted_iota(jnp.int32, dots.shape, 0)
    column = lax.broadcasted_iota(jnp.int32, dots.shape, 1)
    value = jnp.where(column == core, jnp.sum(total), 0.0)
    for v in range(z.batch):
        value += jnp.where(column == v, own_sums[v], 0.0)
    split = jnp.zeros(dots.shape, jnp.float32)
    for k in range(3):
        piece = value.astype(jnp.bfloat16).astype(jnp.float32)
        split = jnp.where(row == k, piece, split)
        value = value - piece
    split = split.astype(jnp.bfloat16)
    dots[...] = split
    for out in outs[1:]:
        out[n * z.own_rows :] = split


def terms(z, plan, left, near, far, vec, spans, so_far=None, own_sums=None, after=()):
    count = sum(span[1] for span in spans)
    flat = [ref for piece in vec for ref in piece]
    shapes = [(count, z.own_rows, z.order)] * (z.env * z.rep)
    whole = (count, z.order, z.order)
    last = own_sums is not None
    sums = jax.ShapeDtypeStruct((8, z.order), jnp.float32)
    if last:
        shapes[1:] = [(count * z.own_rows + TAIL, z.order)] * (z.env * z.rep - 1)
        sums = jax.ShapeDtypeStruct((TAIL, z.order), jnp.bfloat16)
    extra = [] if so_far is None else [so_far]
    specs = [VMEM] * len(extra)
    if last:
        extra.append(own_sums)
        specs.append(SMEM)
    *made, dots = pl.pallas_call(
        functools.partial(terms_body, z, spans, so_far is not None, last),
        out_shape=[jax.ShapeDtypeStruct(shape, jnp.bfloat16) for shape in shapes] + [sums],
        in_specs=[SMEM]
        + [VMEM] * (len(left) + len(near) + len(far) + len(flat))
        + specs
        + [ANY] * len(after),
        out_specs=[VMEM] * (len(shapes) + 1),
        scratch_shapes=[pltpu.VMEM(whole, jnp.bfloat16), pltpu.VMEM(whole, jnp.bfloat16)],
        compiler_params=pltpu.CompilerParams(vmem_limit_bytes=LIMIT),
        cost_estimate=BRIEF,
    )(plan, *left, *near, *far, *flat, *extra, *after)
    return made, dots


def add_terms(z, plans, image, parts, spans):
    core = plans[0][z.core]
    n = 0
    for first, count, _ in spans:
        for i in range(count):
            for e, plan in enumerate(plans):

                def add():
                    slot = plan[z.target + first + i]
                    for s in range(z.rep):
                        v = lax.rem(core + z.rep - s, z.rep)
                        ref = parts[e][s]
                        if len(ref.shape) == 3:
                            term = ref[n]
                        else:
                            term = ref[n * z.own_rows : (n + 1) * z.own_rows]
                        image[v, slot] += term.astype(jnp.float32)

                z.when_valid(plan, first + i, add)
            n += 1


def gather_body(z, chunks, *refs):
    refs = list(refs)
    plans = [refs.pop(0) for _ in range(z.env)]
    energy, vectors, image = refs.pop(0), refs.pop(0), refs[-1]

    def start(j, carry):
        for v in range(z.batch):
            image[v, j] = energy[j] * vectors[v, j].astype(jnp.float32)
        return carry

    lax.fori_loop(0, z.slots, start, 0, unroll=2)
    for spans in chunks:
        parts = [[refs.pop(0) for _ in range(z.rep)] for _ in range(z.env)]
        add_terms(z, plans, image, parts, spans)


def gather_terms(z, plans, energy, vectors, parts, chunks, after=()):
    flat = [ref for chunk in parts for piece in chunk for ref in piece]
    return pl.pallas_call(
        functools.partial(gather_body, z, chunks),
        out_shape=jax.ShapeDtypeStruct(vectors.shape, jnp.float32),
        in_specs=[SMEM] * (z.env + 1) + [VMEM] * (1 + len(flat)) + [ANY] * len(after),
        out_specs=VMEM,
        compiler_params=pltpu.CompilerParams(vmem_limit_bytes=LIMIT),
        cost_estimate=BRIEF,
    )(*plans, energy, vectors, *flat, *after)


def image_body(z, spans, *refs):
    refs = list(refs)
    plans = [refs.pop(0) for _ in range(z.env)]
    so_far = refs.pop(0)
    token, image = refs.pop(), refs.pop()
    token[...] = jnp.zeros_like(token)
    parts = [[refs.pop(0) for _ in range(z.rep)] for _ in range(z.env)]

    def start(j, carry):
        for v in range(z.batch):
            image[v, j] = so_far[v, j]
        return carry

    lax.fori_loop(0, z.slots, start, 0, unroll=2)
    add_terms(z, plans, image, parts, spans)


def make_image(z, plans, so_far, parts, spans):
    flat = [ref for piece in parts for ref in piece]
    return pl.pallas_call(
        functools.partial(image_body, z, spans),
        out_shape=[
            jax.ShapeDtypeStruct(so_far.shape, jnp.float32),
            jax.ShapeDtypeStruct((8, 128), jnp.float32),
        ],
        in_specs=[SMEM] * z.env + [VMEM] * (1 + len(flat)),
        out_specs=[VMEM, VMEM],
        compiler_params=pltpu.CompilerParams(vmem_limit_bytes=LIMIT),
        cost_estimate=BRIEF,
    )(*plans, so_far, *flat)


def in_order(parts, places, count):
    total = 0.0
    for place in range(count):
        for part, at in zip(parts, places):
            total = total + jnp.where(at == place, part, 0.0)
    return total


def chips_body(z, count, plan, own, *refs):
    arrived, out = refs[:count], refs[-1]
    core, chip = plan[z.core], plan[z.chip]
    parts, places = [], []
    for e in range(z.env):
        for s in range(z.rep):
            ref = arrived[e * z.rep + s - 1] if e + s else own
            tail = ref[ref.shape[0] - TAIL :].astype(jnp.float32)
            parts.append(tail[0:1] + tail[1:2] + tail[2:3])
            at = lax.rem(chip + z.env - e, z.env) * z.rep + lax.rem(core + z.rep - s, z.rep)
            places.append(at)
    total = in_order(parts, places, z.env * z.rep)
    out[...] = jnp.broadcast_to(total, out.shape)


def chip_sums(z, plan, own, arrived, after):
    return pl.pallas_call(
        functools.partial(chips_body, z, len(arrived)),
        out_shape=jax.ShapeDtypeStruct((8, z.order), jnp.float32),
        in_specs=[SMEM] + [VMEM] * (1 + len(arrived)) + [ANY] * len(after),
        out_specs=VMEM,
        cost_estimate=BRIEF,
    )(plan, own, *arrived, *after)


def mean_body(z, count, scale, *refs):
    out = refs[-1]
    me = lax.axis_index("sector")
    parts = [ref[0:1] for ref in refs[:count]]
    total = parts[0]
    if count > 1:
        places = [lax.rem(me + z.sector - step, z.sector) for step in range(count)]
        total = in_order(parts, places, count)
    out[...] = total * scale


def mean_over_sectors(z, array, entries, after):
    held = [array]
    if z.sector <= 4:
        held += [shift(array, "sector", z.sector, step) for step in range(1, z.sector)]
    else:
        held = [total_over(array, "sector")]
    made = pl.pallas_call(
        functools.partial(mean_body, z, len(held), 1.0 / entries),
        out_shape=jax.ShapeDtypeStruct((1, z.order), jnp.float32),
        in_specs=[VMEM] * len(held) + [ANY] * len(after),
        out_specs=VMEM,
        cost_estimate=BRIEF,
    )(*held, *after)
    return made[0, : z.batch]


def shift(array, axis, size, step):
    return lax.ppermute(array, axis, [(i, (i + step) % size) for i in range(size)])


def shift_both(z, array, e, s):
    perm = []
    for x in range(z.env):
        for c in range(z.rep):
            perm.append((x * z.rep + c, (x + e) % z.env * z.rep + (c + s) % z.rep))
    return lax.ppermute(array, ("env", "rep"), perm)


def total_over(array, axis):
    size = lax.axis_size(axis)
    if size & (size - 1):
        return lax.psum(array, axis)
    step = 1
    while step < size:
        array = array + lax.ppermute(array, axis, [(i, i ^ step) for i in range(size)])
        step *= 2
    return array


def on_device(vectors, left_env, right_env, energy, partner):
    z = Sizes(vectors, left_env)
    each = z.sector // 4
    span = z.capacity

    def spans_of(g):
        return [((g * each + d) * span, span, 0) for d in range(each)]

    chunks = {g: spans_of(g) for g in range(4)}

    def around(array):
        return [array] + [shift(array, "rep", z.rep, s) for s in range(1, z.rep)]

    def across(arrays, g):
        steps = [g * each + d for d in range(each)]
        return [shift(a, "sector", z.sector, k) if k else a for a, k in zip(arrays, steps)]

    partners = [shift(partner, "env", z.env, e) for e in range(1, z.env)]
    vector_others = around(vectors)[1:]
    right_others = around(right_env)[1:]
    left = around(left_env)
    plan, own, right_own = load(z, partner, vectors, right_env)
    own = gate(own, partners)
    right = [right_own] + right_others
    near_rows = [own[0]] + vector_others
    vec = [near_rows]
    for e in range(1, z.env):
        vec.append([shift_both(z, own[s], e, s) for s in range(z.rep)])
    plans = [plan] + [plan_only(z, other) for other in partners]

    def near_products(g, after):
        return products(z, plan, right, [near_rows], [c[:2] for c in chunks[g]], after)

    def far_products(g, after):
        return products(z, plan, right, vec[1:], [c[:2] for c in chunks[g]], after)

    near, far, parts = {}, {}, {}
    spans = [piece[:2] for g in (1, 3) for piece in chunks[g]]
    made = products(z, plan, right, [near_rows], spans)
    near[1], near[3] = across(made[:each], 1), across(made[each:], 3)
    made = near_products(2, (made[0], *left[1:]))
    near[2] = across(made, 2)
    sent = [array for g in (1, 3, 2) for array in near[g]]

    def send_terms(g, so_far, own_sums, after):
        made, folded = terms(
            z, plan, left, near[g], far[g], vec, chunks[g], so_far, own_sums, after
        )
        parts[g] = [
            [
                shift_both(z, made[e * z.rep + s], e, s) if e + s else made[0]
                for s in range(z.rep)
            ]
            for e in range(z.env)
        ]
        return folded

    def arrived(g):
        return [part for piece in parts[g] for part in piece][1:]

    far1 = far_products(1, (made[0], *plans[1:]))
    far3 = far_products(3, far1[:1])
    far2 = far_products(2, far3[:1])
    near[0] = near_products(0, far2[:1])
    far[0] = far_products(0, near[0][:1])
    dots = send_terms(0, None, None, ())
    made = gate([*far1, *far3], [dots, *sent])
    far[1] = across(made[:each], 1)
    far[3] = across(made[each:], 3)
    made = gate(far2, far[1])
    far[2] = across(made, 2)
    dots = send_terms(1, dots, None, (*made, *arrived(0)))
    dots = send_terms(3, dots, None, arrived(1))
    own_block = vectors.astype(jnp.float32)
    own_sums = jnp.sum(energy[None, :, None, None] * own_block * own_block, axis=(1, 2, 3))
    dots = send_terms(2, dots, own_sums, arrived(3))
    early = (0, 1, 3)
    so_far = gather_terms(
        z,
        plans,
        energy,
        vectors,
        [parts[g] for g in early],
        [chunks[g] for g in early],
        (dots,),
    )
    sums = chip_sums(z, plan, dots, arrived(2), (so_far,))
    image, token = make_image(z, plans, so_far, parts[2], chunks[2])
    entries = z.slots * z.sector * z.order * z.order
    return (image, mean_over_sectors(z, sums, entries, (token,)))


def solution(mesh):
    return jax.shard_map(
        on_device,
        mesh=mesh,
        in_specs=(
            P(None, ("groups", "sector"), ("env", "rep"), None),
            P("env", ("groups", "sector"), "rep", None),
            P("env", ("groups", "sector"), "rep", None),
            P(("groups", "sector")),
            P("env", "groups"),
        ),
        out_specs=(P(None, ("groups", "sector"), ("env", "rep"), None), P("groups")),
        check_vma=False,
    )
```

```python
import functools

import jax
import jax.numpy as jnp
from jax import lax
from jax.experimental import pallas as pl
from jax.experimental.pallas import tpu as pltpu
from jax.sharding import PartitionSpec as P

ANY = pl.BlockSpec(memory_space=pl.ANY)
HBM = pl.BlockSpec(memory_space=pltpu.HBM)
SMEM = pl.BlockSpec(memory_space=pltpu.SMEM)
VMEM = pl.BlockSpec(memory_space=pltpu.VMEM)
LIMIT = 12 * 1024 * 1024
SMALL = 2 * 1024 * 1024
TAIL = 16
BRIEF = pl.CostEstimate(flops=0, bytes_accessed=0, transcendentals=0)


def aligned(index, size):
    return pl.multiple_of(index * size, size)


class Sizes:
    def __init__(self, vectors, left_env):
        self.env = lax.axis_size("env")
        self.rep = lax.axis_size("rep")
        self.sector = lax.axis_size("sector")
        self.batch, self.slots, self.own_rows, self.order = vectors.shape
        assert self.batch == self.rep and self.sector % 4 == 0
        self.half = left_env.shape[2]
        self.chip_rows = self.own_rows * self.rep
        self.capacity = 2 * ((self.slots + 2 * self.sector - 1) // (2 * self.sector))
        self.flat = self.sector * self.capacity
        self.full = self.flat == self.slots
        self.source, self.target, self.valid = 0, self.flat, 2 * self.flat
        self.core, self.chip = 3 * self.flat, 3 * self.flat + 1

    def when_valid(self, plan, flat, action):
        if self.full:
            action()
        else:
            pl.when(plan[self.valid + flat] == 1)(action)


def write_plan(z, partner, plan, count):
    if not z.full:

        def clear(i, carry):
            plan[i] = 0
            return carry

        lax.fori_loop(0, 3 * z.flat, clear, 0)
    for d in range(z.sector):
        count[d] = 0
    for j in range(z.slots):
        sector = partner[0, j]
        group = lax.div(sector, z.slots)
        slot = sector - group * z.slots
        distance = lax.rem(z.sector - group, z.sector)
        rank = count[distance]
        count[distance] = rank + 1
        index = distance * z.capacity + rank
        plan[z.source + index] = slot
        plan[z.target + index] = j
        plan[z.valid + index] = 1
    plan[z.core] = lax.axis_index("rep")
    plan[z.chip] = lax.axis_index("env")


def split_copy(source, target, slots, sem):
    step = slots // 4 if slots % 4 == 0 else slots
    copies = []
    for i in range(slots // step):
        part = pl.ds(i * step, step)
        copies.append(pltpu.make_async_copy(source.at[part], target.at[part], sem.at[i]))
    return copies


def load_body(z, partner, vectors, right, plan, *refs):
    rows, block, count, sem = refs[: z.rep], refs[z.rep], refs[-2], refs[-1]
    core = lax.axis_index("rep")
    copies = []
    for s, ref in enumerate(rows):
        mine = vectors.at[lax.rem(core + s, z.rep)]
        copies += split_copy(mine, ref, z.slots, sem.at[s])
    copies += split_copy(right.at[0], block.at[0], z.slots, sem.at[z.rep])
    for copy in copies:
        copy.start()
    write_plan(z, partner, plan, count)
    for copy in copies:
        copy.wait()


def load(z, partner, vectors, right_env):
    row = jax.ShapeDtypeStruct(vectors.shape[1:], jnp.bfloat16)
    plan, *made = pl.pallas_call(
        functools.partial(load_body, z),
        out_shape=[jax.ShapeDtypeStruct((3 * z.flat + 2,), jnp.int32)]
        + [row] * z.rep
        + [jax.ShapeDtypeStruct(right_env.shape, jnp.bfloat16)],
        in_specs=[SMEM, HBM, HBM],
        out_specs=[SMEM] + [VMEM] * (z.rep + 1),
        scratch_shapes=[
            pltpu.SMEM((z.sector,), jnp.int32),
            pltpu.SemaphoreType.DMA((z.rep + 1, 4)),
        ],
        compiler_params=pltpu.CompilerParams(vmem_limit_bytes=LIMIT),
        cost_estimate=BRIEF,
    )(
        partner,
        pltpu.with_memory_space_constraint(vectors, pltpu.HBM),
        pltpu.with_memory_space_constraint(right_env, pltpu.HBM),
    )
    return plan, made[: z.rep], made[z.rep]


def plan_only(z, partner):
    return pl.pallas_call(
        functools.partial(write_plan, z),
        out_shape=jax.ShapeDtypeStruct((3 * z.flat + 2,), jnp.int32),
        in_specs=[SMEM],
        out_specs=SMEM,
        scratch_shapes=[pltpu.SMEM((z.sector,), jnp.int32)],
        compiler_params=pltpu.CompilerParams(vmem_limit_bytes=SMALL),
        cost_estimate=BRIEF,
    )(partner)


def gate(arrays, after):
    def body(*refs):
        pass

    return pl.pallas_call(
        body,
        out_shape=[jax.ShapeDtypeStruct(a.shape, a.dtype) for a in arrays],
        in_specs=[ANY] * (len(arrays) + len(after)),
        out_specs=[ANY] * len(arrays),
        input_output_aliases={i: i for i in range(len(arrays))},
        compiler_params=pltpu.CompilerParams(vmem_limit_bytes=SMALL),
        cost_estimate=BRIEF,
    )(*arrays, *after)


def pick(z, core, place, candidates):
    chosen = candidates[0]
    for s in range(1, z.rep):
        chosen = jnp.where(lax.rem(core + z.rep - s, z.rep) == place, candidates[s], chosen)
    return chosen


def line(ref, core, slot):
    return ref[core, slot] if len(ref.shape) == 4 else ref[slot]


def products_body(z, pieces, spans, *refs):
    refs = list(refs)
    plan = refs.pop(0)
    right = [refs.pop(0) for _ in range(z.rep)]
    rows = [[refs.pop(0) for _ in range(z.rep)] for _ in range(pieces)]
    outs = refs[-len(spans) :]
    core = plan[z.core]
    for (first, count), out in zip(spans, outs):
        for i in range(count):
            slot = plan[z.source + first + i]
            halves = [ref[0, slot] for ref in right]
            parts = [[line(ref, core, slot) for ref in piece] for piece in rows]
            block = jnp.concatenate([pick(z, core, k, halves) for k in range(z.rep)], axis=0)
            lines = jnp.concatenate(
                [pick(z, core, k, part) for part in parts for k in range(z.rep)], axis=0
            )
            out[i] = lax.dot_general(
                lines, block, (((1,), (1,)), ((), ())), preferred_element_type=jnp.float32
            ).astype(jnp.bfloat16)


def products(z, plan, right, rows, spans, after=()):
    pieces = len(rows)
    flat = [ref for piece in rows for ref in piece]
    height = pieces * z.chip_rows
    return pl.pallas_call(
        functools.partial(products_body, z, pieces, spans),
        out_shape=[
            jax.ShapeDtypeStruct((count, height, z.order), jnp.bfloat16) for _, count in spans
        ],
        in_specs=[SMEM] + [VMEM] * (len(right) + len(flat)) + [ANY] * len(after),
        out_specs=[VMEM] * len(spans),
        compiler_params=pltpu.CompilerParams(vmem_limit_bytes=LIMIT),
        cost_estimate=BRIEF,
    )(plan, *right, *flat, *after)


def terms_body(z, spans, chained, last, *refs):
    refs = list(refs)
    plan = refs.pop(0)
    left = [refs.pop(0) for _ in range(z.rep)]
    near = [refs.pop(0) for _ in spans]
    far = [refs.pop(0) for _ in spans]
    vec = [[refs.pop(0) for _ in range(z.rep)] for _ in range(z.env)]
    so_far = refs.pop(0) if chained else None
    own_sums = refs.pop(0) if last else None
    pbuf, tbuf = refs[-2:]
    dots = refs[-3]
    outs = refs[-3 - z.env * z.rep : -3]
    core, chip = plan[z.core], plan[z.chip]
    total = so_far[...] if chained else jnp.zeros((8, z.order), jnp.float32)
    n = 0
    for d, (first, count, skip) in enumerate(spans):
        for i in range(count):
            slot = plan[z.target + first + i]
            for e in range(z.env):
                place = lax.rem(chip + z.env - e, z.env)
                if e == 0:
                    lines = near[d][skip + i]
                else:
                    lines = far[d][i, (e - 1) * z.chip_rows : e * z.chip_rows]
                pbuf[n, pl.ds(aligned(place, z.chip_rows), z.chip_rows)] = lines
            halves = [ref[0, slot] for ref in left]
            block = jnp.concatenate([pick(z, core, k, halves) for k in range(z.rep)], axis=0)
            tbuf[n] = jnp.dot(block, pbuf[n], preferred_element_type=jnp.float32).astype(
                jnp.bfloat16
            )
            folded = jnp.zeros(total.shape, jnp.float32)
            for e in range(z.env):
                for s in range(z.rep):
                    place = lax.rem(chip + e, z.env) * z.rep + lax.rem(core + s, z.rep)
                    term = tbuf[n, pl.ds(aligned(place, z.own_rows), z.own_rows)]
                    if last and e + s:
                        outs[e * z.rep + s][n * z.own_rows : (n + 1) * z.own_rows] = term
                    else:
                        outs[e * z.rep + s][n] = term
                    lines = line(vec[(z.env - e) % z.env][(z.rep - s) % z.rep], core, slot)
                    both = lines.astype(jnp.float32) * term.astype(jnp.float32)
                    folded += jnp.sum(both.reshape(-1, *total.shape), axis=0)
            if not z.full:
                folded = jnp.where(plan[z.valid + first + i] == 1, folded, 0.0)
            total += folded
            n += 1
    if not last:
        dots[...] = total
        return
    row = lax.broadcasted_iota(jnp.int32, dots.shape, 0)
    column = lax.broadcasted_iota(jnp.int32, dots.shape, 1)
    value = jnp.where(column == core, jnp.sum(total), 0.0)
    for v in range(z.batch):
        value += jnp.where(column == v, own_sums[v], 0.0)
    split = jnp.zeros(dots.shape, jnp.float32)
    for k in range(3):
        piece = value.astype(jnp.bfloat16).astype(jnp.float32)
        split = jnp.where(row == k, piece, split)
        value = value - piece
    split = split.astype(jnp.bfloat16)
    dots[...] = split
    for out in outs[1:]:
        out[n * z.own_rows :] = split


def terms(z, plan, left, near, far, vec, spans, so_far=None, own_sums=None, after=()):
    count = sum(span[1] for span in spans)
    flat = [ref for piece in vec for ref in piece]
    shapes = [(count, z.own_rows, z.order)] * (z.env * z.rep)
    whole = (count, z.order, z.order)
    last = own_sums is not None
    sums = jax.ShapeDtypeStruct((8, z.order), jnp.float32)
    if last:
        shapes[1:] = [(count * z.own_rows + TAIL, z.order)] * (z.env * z.rep - 1)
        sums = jax.ShapeDtypeStruct((TAIL, z.order), jnp.bfloat16)
    extra = [] if so_far is None else [so_far]
    specs = [VMEM] * len(extra)
    if last:
        extra.append(own_sums)
        specs.append(SMEM)
    *made, dots = pl.pallas_call(
        functools.partial(terms_body, z, spans, so_far is not None, last),
        out_shape=[jax.ShapeDtypeStruct(shape, jnp.bfloat16) for shape in shapes] + [sums],
        in_specs=[SMEM]
        + [VMEM] * (len(left) + len(near) + len(far) + len(flat))
        + specs
        + [ANY] * len(after),
        out_specs=[VMEM] * (len(shapes) + 1),
        scratch_shapes=[pltpu.VMEM(whole, jnp.bfloat16), pltpu.VMEM(whole, jnp.bfloat16)],
        compiler_params=pltpu.CompilerParams(vmem_limit_bytes=LIMIT),
        cost_estimate=BRIEF,
    )(plan, *left, *near, *far, *flat, *extra, *after)
    return made, dots


def add_terms(z, plans, image, parts, spans):
    core = plans[0][z.core]
    n = 0
    for first, count, _ in spans:
        for i in range(count):
            for e, plan in enumerate(plans):

                def add():
                    slot = plan[z.target + first + i]
                    for s in range(z.rep):
                        v = lax.rem(core + z.rep - s, z.rep)
                        ref = parts[e][s]
                        if len(ref.shape) == 3:
                            term = ref[n]
                        else:
                            term = ref[n * z.own_rows : (n + 1) * z.own_rows]
                        image[v, slot] += term.astype(jnp.float32)

                z.when_valid(plan, first + i, add)
            n += 1


def gather_body(z, chunks, *refs):
    refs = list(refs)
    plans = [refs.pop(0) for _ in range(z.env)]
    energy, vectors, image = refs.pop(0), refs.pop(0), refs[-1]

    def start(j, carry):
        for v in range(z.batch):
            image[v, j] = energy[j] * vectors[v, j].astype(jnp.float32)
        return carry

    lax.fori_loop(0, z.slots, start, 0, unroll=2)
    for spans in chunks:
        parts = [[refs.pop(0) for _ in range(z.rep)] for _ in range(z.env)]
        add_terms(z, plans, image, parts, spans)


def gather_terms(z, plans, energy, vectors, parts, chunks, after=()):
    flat = [ref for chunk in parts for piece in chunk for ref in piece]
    return pl.pallas_call(
        functools.partial(gather_body, z, chunks),
        out_shape=jax.ShapeDtypeStruct(vectors.shape, jnp.float32),
        in_specs=[SMEM] * (z.env + 1) + [VMEM] * (1 + len(flat)) + [ANY] * len(after),
        out_specs=VMEM,
        compiler_params=pltpu.CompilerParams(vmem_limit_bytes=LIMIT),
        cost_estimate=BRIEF,
    )(*plans, energy, vectors, *flat, *after)


def image_body(z, spans, *refs):
    refs = list(refs)
    plans = [refs.pop(0) for _ in range(z.env)]
    so_far = refs.pop(0)
    token, image = refs.pop(), refs.pop()
    token[...] = jnp.zeros_like(token)
    parts = [[refs.pop(0) for _ in range(z.rep)] for _ in range(z.env)]

    def start(j, carry):
        for v in range(z.batch):
            image[v, j] = so_far[v, j]
        return carry

    lax.fori_loop(0, z.slots, start, 0, unroll=2)
    add_terms(z, plans, image, parts, spans)


def make_image(z, plans, so_far, parts, spans):
    flat = [ref for piece in parts for ref in piece]
    return pl.pallas_call(
        functools.partial(image_body, z, spans),
        out_shape=[
            jax.ShapeDtypeStruct(so_far.shape, jnp.float32),
            jax.ShapeDtypeStruct((8, 128), jnp.float32),
        ],
        in_specs=[SMEM] * z.env + [VMEM] * (1 + len(flat)),
        out_specs=[VMEM, VMEM],
        compiler_params=pltpu.CompilerParams(vmem_limit_bytes=LIMIT),
        cost_estimate=BRIEF,
    )(*plans, so_far, *flat)


def in_order(parts, places, count):
    total = 0.0
    for place in range(count):
        for part, at in zip(parts, places):
            total = total + jnp.where(at == place, part, 0.0)
    return total


def chips_body(z, count, plan, own, *refs):
    arrived, out = refs[:count], refs[-1]
    core, chip = plan[z.core], plan[z.chip]
    parts, places = [], []
    for e in range(z.env):
        for s in range(z.rep):
            ref = arrived[e * z.rep + s - 1] if e + s else own
            tail = ref[ref.shape[0] - TAIL :].astype(jnp.float32)
            parts.append(tail[0:1] + tail[1:2] + tail[2:3])
            at = lax.rem(chip + z.env - e, z.env) * z.rep + lax.rem(core + z.rep - s, z.rep)
            places.append(at)
    total = in_order(parts, places, z.env * z.rep)
    out[...] = jnp.broadcast_to(total, out.shape)


def chip_sums(z, plan, own, arrived, after):
    return pl.pallas_call(
        functools.partial(chips_body, z, len(arrived)),
        out_shape=jax.ShapeDtypeStruct((8, z.order), jnp.float32),
        in_specs=[SMEM] + [VMEM] * (1 + len(arrived)) + [ANY] * len(after),
        out_specs=VMEM,
        compiler_params=pltpu.CompilerParams(vmem_limit_bytes=SMALL),
        cost_estimate=BRIEF,
    )(plan, own, *arrived, *after)


def mean_body(z, count, scale, *refs):
    out = refs[-1]
    me = lax.axis_index("sector")
    parts = [ref[0:1] for ref in refs[:count]]
    total = parts[0]
    if count > 1:
        places = [lax.rem(me + z.sector - step, z.sector) for step in range(count)]
        total = in_order(parts, places, count)
    out[...] = total * scale


def mean_over_sectors(z, array, entries, after):
    held = [array]
    if z.sector <= 4:
        held += [shift(array, "sector", z.sector, step) for step in range(1, z.sector)]
    else:
        held = [total_over(array, "sector")]
    made = pl.pallas_call(
        functools.partial(mean_body, z, len(held), 1.0 / entries),
        out_shape=jax.ShapeDtypeStruct((1, z.order), jnp.float32),
        in_specs=[VMEM] * len(held) + [ANY] * len(after),
        out_specs=VMEM,
        compiler_params=pltpu.CompilerParams(vmem_limit_bytes=SMALL),
        cost_estimate=BRIEF,
    )(*held, *after)
    return made[0, : z.batch]


def shift(array, axis, size, step):
    return lax.ppermute(array, axis, [(i, (i + step) % size) for i in range(size)])


def shift_both(z, array, e, s):
    perm = []
    for x in range(z.env):
        for c in range(z.rep):
            perm.append((x * z.rep + c, (x + e) % z.env * z.rep + (c + s) % z.rep))
    return lax.ppermute(array, ("env", "rep"), perm)


def total_over(array, axis):
    size = lax.axis_size(axis)
    if size & (size - 1):
        return lax.psum(array, axis)
    step = 1
    while step < size:
        array = array + lax.ppermute(array, axis, [(i, i ^ step) for i in range(size)])
        step *= 2
    return array


def on_device(vectors, left_env, right_env, energy, partner):
    z = Sizes(vectors, left_env)
    each = z.sector // 4
    span = z.capacity

    def spans_of(g):
        return [((g * each + d) * span, span, 0) for d in range(each)]

    chunks = {g: spans_of(g) for g in range(4)}

    def around(array):
        return [array] + [shift(array, "rep", z.rep, s) for s in range(1, z.rep)]

    def across(arrays, g):
        steps = [g * each + d for d in range(each)]
        return [shift(a, "sector", z.sector, k) if k else a for a, k in zip(arrays, steps)]

    partners = [shift(partner, "env", z.env, e) for e in range(1, z.env)]
    vector_others = around(vectors)[1:]
    right_others = around(right_env)[1:]
    left = around(left_env)
    plan, own, right_own = load(z, partner, vectors, right_env)
    own = gate(own, partners)
    right = [right_own] + right_others
    near_rows = [own[0]] + vector_others
    vec = [near_rows]
    for e in range(1, z.env):
        vec.append([shift_both(z, own[s], e, s) for s in range(z.rep)])
    plans = [plan] + [plan_only(z, other) for other in partners]

    def near_products(g, after):
        return products(z, plan, right, [near_rows], [c[:2] for c in chunks[g]], after)

    def far_products(g, after):
        return products(z, plan, right, vec[1:], [c[:2] for c in chunks[g]], after)

    near, far, parts = {}, {}, {}
    spans = [piece[:2] for g in (1, 3) for piece in chunks[g]]
    made = products(z, plan, right, [near_rows], spans)
    near[1], near[3] = across(made[:each], 1), across(made[each:], 3)
    made = near_products(2, (made[0], *left[1:]))
    near[2] = across(made, 2)
    sent = [array for g in (1, 3, 2) for array in near[g]]

    def send_terms(g, so_far, own_sums, after):
        made, folded = terms(
            z, plan, left, near[g], far[g], vec, chunks[g], so_far, own_sums, after
        )
        parts[g] = [
            [
                shift_both(z, made[e * z.rep + s], e, s) if e + s else made[0]
                for s in range(z.rep)
            ]
            for e in range(z.env)
        ]
        return folded

    def arrived(g):
        return [part for piece in parts[g] for part in piece][1:]

    far1 = far_products(1, (made[0], *plans[1:]))
    far3 = far_products(3, far1[:1])
    far2 = far_products(2, far3[:1])
    near[0] = near_products(0, far2[:1])
    far[0] = far_products(0, near[0][:1])
    dots = send_terms(0, None, None, ())
    made = gate([*far1, *far3], [dots, *sent])
    far[1] = across(made[:each], 1)
    far[3] = across(made[each:], 3)
    made = gate(far2, far[1])
    far[2] = across(made, 2)
    dots = send_terms(1, dots, None, (*made, *arrived(0)))
    dots = send_terms(3, dots, None, arrived(1))
    own_block = vectors.astype(jnp.float32)
    own_sums = jnp.sum(energy[None, :, None, None] * own_block * own_block, axis=(1, 2, 3))
    dots = send_terms(2, dots, own_sums, arrived(3))
    early = (0, 1, 3)
    so_far = gather_terms(
        z,
        plans,
        energy,
        vectors,
        [parts[g] for g in early],
        [chunks[g] for g in early],
        (dots,),
    )
    sums = chip_sums(z, plan, dots, arrived(2), (so_far,))
    image, token = make_image(z, plans, so_far, parts[2], chunks[2])
    entries = z.slots * z.sector * z.order * z.order
    return (image, mean_over_sectors(z, sums, entries, (token,)))


def solution(mesh):
    return jax.shard_map(
        on_device,
        mesh=mesh,
        in_specs=(
            P(None, ("groups", "sector"), ("env", "rep"), None),
            P("env", ("groups", "sector"), "rep", None),
            P("env", ("groups", "sector"), "rep", None),
            P(("groups", "sector")),
            P("env", "groups"),
        ),
        out_specs=(P(None, ("groups", "sector"), ("env", "rep"), None), P("groups")),
        check_vma=False,
    )
```

```python
import functools

import jax
import jax.numpy as jnp
from jax import lax
from jax.experimental import pallas as pl
from jax.experimental.pallas import tpu as pltpu
from jax.sharding import PartitionSpec as P

ANY = pl.BlockSpec(memory_space=pl.ANY)
HBM = pl.BlockSpec(memory_space=pltpu.HBM)
SMEM = pl.BlockSpec(memory_space=pltpu.SMEM)
VMEM = pl.BlockSpec(memory_space=pltpu.VMEM)
LIMIT = 12 * 1024 * 1024
SMALL = 2 * 1024 * 1024
TAIL = 16
BRIEF = pl.CostEstimate(flops=0, bytes_accessed=0, transcendentals=0)


def aligned(index, size):
    return pl.multiple_of(index * size, size)


class Sizes:
    def __init__(self, vectors, left_env):
        self.env = lax.axis_size("env")
        self.rep = lax.axis_size("rep")
        self.sector = lax.axis_size("sector")
        self.batch, self.slots, self.own_rows, self.order = vectors.shape
        assert self.batch == self.rep and self.sector % 4 == 0
        self.half = left_env.shape[2]
        self.chip_rows = self.own_rows * self.rep
        self.capacity = 2 * ((self.slots + 2 * self.sector - 1) // (2 * self.sector))
        self.flat = self.sector * self.capacity
        self.full = self.flat == self.slots
        self.source, self.target, self.valid = 0, self.flat, 2 * self.flat
        self.core, self.chip = 3 * self.flat, 3 * self.flat + 1

    def when_valid(self, plan, flat, action):
        if self.full:
            action()
        else:
            pl.when(plan[self.valid + flat] == 1)(action)


def write_plan(z, partner, plan, count):
    if not z.full:

        def clear(i, carry):
            plan[i] = 0
            return carry

        lax.fori_loop(0, 3 * z.flat, clear, 0)
    for d in range(z.sector):
        count[d] = 0
    factor = -(-(1 << 16) // z.slots)
    assert all(i * factor >> 16 == i // z.slots for i in range(z.sector * z.slots))
    for j in range(z.slots):
        sector = partner[0, j]
        group = (sector * factor) >> 16
        slot = sector - group * z.slots
        distance = jnp.where(group == 0, 0, z.sector - group)
        rank = count[distance]
        count[distance] = rank + 1
        index = distance * z.capacity + rank
        plan[z.source + index] = slot
        plan[z.target + index] = j
        plan[z.valid + index] = 1
    plan[z.core] = lax.axis_index("rep")
    plan[z.chip] = lax.axis_index("env")


def split_copy(source, target, slots, sem):
    step = slots // 4 if slots % 4 == 0 else slots
    copies = []
    for i in range(slots // step):
        part = pl.ds(i * step, step)
        copies.append(pltpu.make_async_copy(source.at[part], target.at[part], sem.at[i]))
    return copies


def load_body(z, partner, vectors, right, plan, *refs):
    rows, block, count, sem = refs[: z.rep], refs[z.rep], refs[-2], refs[-1]
    core = lax.axis_index("rep")
    copies = []
    for s, ref in enumerate(rows):
        mine = vectors.at[lax.rem(core + s, z.rep)]
        copies += split_copy(mine, ref, z.slots, sem.at[s])
    copies += split_copy(right.at[0], block.at[0], z.slots, sem.at[z.rep])
    for copy in copies:
        copy.start()
    write_plan(z, partner, plan, count)
    for copy in copies:
        copy.wait()


def load(z, partner, vectors, right_env):
    row = jax.ShapeDtypeStruct(vectors.shape[1:], jnp.bfloat16)
    plan, *made = pl.pallas_call(
        functools.partial(load_body, z),
        out_shape=[jax.ShapeDtypeStruct((3 * z.flat + 2,), jnp.int32)]
        + [row] * z.rep
        + [jax.ShapeDtypeStruct(right_env.shape, jnp.bfloat16)],
        in_specs=[SMEM, HBM, HBM],
        out_specs=[SMEM] + [VMEM] * (z.rep + 1),
        scratch_shapes=[
            pltpu.SMEM((z.sector,), jnp.int32),
            pltpu.SemaphoreType.DMA((z.rep + 1, 4)),
        ],
        compiler_params=pltpu.CompilerParams(vmem_limit_bytes=LIMIT),
        cost_estimate=BRIEF,
    )(
        partner,
        pltpu.with_memory_space_constraint(vectors, pltpu.HBM),
        pltpu.with_memory_space_constraint(right_env, pltpu.HBM),
    )
    return plan, made[: z.rep], made[z.rep]


def plan_only(z, partner):
    return pl.pallas_call(
        functools.partial(write_plan, z),
        out_shape=jax.ShapeDtypeStruct((3 * z.flat + 2,), jnp.int32),
        in_specs=[SMEM],
        out_specs=SMEM,
        scratch_shapes=[pltpu.SMEM((z.sector,), jnp.int32)],
        compiler_params=pltpu.CompilerParams(vmem_limit_bytes=SMALL),
        cost_estimate=BRIEF,
    )(partner)


def gate(arrays, after):
    def body(*refs):
        pass

    return pl.pallas_call(
        body,
        out_shape=[jax.ShapeDtypeStruct(a.shape, a.dtype) for a in arrays],
        in_specs=[ANY] * (len(arrays) + len(after)),
        out_specs=[ANY] * len(arrays),
        input_output_aliases={i: i for i in range(len(arrays))},
        compiler_params=pltpu.CompilerParams(vmem_limit_bytes=SMALL),
        cost_estimate=BRIEF,
    )(*arrays, *after)


def pick(z, core, place, candidates):
    chosen = candidates[0]
    for s in range(1, z.rep):
        chosen = jnp.where(lax.rem(core + z.rep - s, z.rep) == place, candidates[s], chosen)
    return chosen


def line(ref, core, slot):
    return ref[core, slot] if len(ref.shape) == 4 else ref[slot]


def products_body(z, pieces, spans, *refs):
    refs = list(refs)
    plan = refs.pop(0)
    right = [refs.pop(0) for _ in range(z.rep)]
    rows = [[refs.pop(0) for _ in range(z.rep)] for _ in range(pieces)]
    outs = refs[-len(spans) :]
    core = plan[z.core]
    for (first, count), out in zip(spans, outs):
        for i in range(count):
            slot = plan[z.source + first + i]
            halves = [ref[0, slot] for ref in right]
            parts = [[line(ref, core, slot) for ref in piece] for piece in rows]
            block = jnp.concatenate([pick(z, core, k, halves) for k in range(z.rep)], axis=0)
            lines = jnp.concatenate(
                [pick(z, core, k, part) for part in parts for k in range(z.rep)], axis=0
            )
            out[i] = lax.dot_general(
                lines, block, (((1,), (1,)), ((), ())), preferred_element_type=jnp.float32
            ).astype(jnp.bfloat16)


def products(z, plan, right, rows, spans, after=()):
    pieces = len(rows)
    flat = [ref for piece in rows for ref in piece]
    height = pieces * z.chip_rows
    return pl.pallas_call(
        functools.partial(products_body, z, pieces, spans),
        out_shape=[
            jax.ShapeDtypeStruct((count, height, z.order), jnp.bfloat16) for _, count in spans
        ],
        in_specs=[SMEM] + [VMEM] * (len(right) + len(flat)) + [ANY] * len(after),
        out_specs=[VMEM] * len(spans),
        compiler_params=pltpu.CompilerParams(vmem_limit_bytes=LIMIT),
        cost_estimate=BRIEF,
    )(plan, *right, *flat, *after)


def terms_body(z, spans, chained, last, *refs):
    refs = list(refs)
    plan = refs.pop(0)
    left = [refs.pop(0) for _ in range(z.rep)]
    near = [refs.pop(0) for _ in spans]
    far = [refs.pop(0) for _ in spans]
    vec = [[refs.pop(0) for _ in range(z.rep)] for _ in range(z.env)]
    so_far = refs.pop(0) if chained else None
    own_sums = refs.pop(0) if last else None
    pbuf, tbuf = refs[-2:]
    dots = refs[-3]
    outs = refs[-3 - z.env * z.rep : -3]
    core, chip = plan[z.core], plan[z.chip]
    total = so_far[...] if chained else jnp.zeros((8, z.order), jnp.float32)
    n = 0
    for d, (first, count, skip) in enumerate(spans):
        for i in range(count):
            slot = plan[z.target + first + i]
            for e in range(z.env):
                place = lax.rem(chip + z.env - e, z.env)
                if e == 0:
                    lines = near[d][skip + i]
                else:
                    lines = far[d][i, (e - 1) * z.chip_rows : e * z.chip_rows]
                pbuf[n, pl.ds(aligned(place, z.chip_rows), z.chip_rows)] = lines
            halves = [ref[0, slot] for ref in left]
            block = jnp.concatenate([pick(z, core, k, halves) for k in range(z.rep)], axis=0)
            tbuf[n] = jnp.dot(block, pbuf[n], preferred_element_type=jnp.float32).astype(
                jnp.bfloat16
            )
            folded = jnp.zeros(total.shape, jnp.float32)
            for e in range(z.env):
                for s in range(z.rep):
                    place = lax.rem(chip + e, z.env) * z.rep + lax.rem(core + s, z.rep)
                    term = tbuf[n, pl.ds(aligned(place, z.own_rows), z.own_rows)]
                    if last and e + s:
                        outs[e * z.rep + s][n * z.own_rows : (n + 1) * z.own_rows] = term
                    else:
                        outs[e * z.rep + s][n] = term
                    lines = line(vec[(z.env - e) % z.env][(z.rep - s) % z.rep], core, slot)
                    both = lines.astype(jnp.float32) * term.astype(jnp.float32)
                    folded += jnp.sum(both.reshape(-1, *total.shape), axis=0)
            if not z.full:
                folded = jnp.where(plan[z.valid + first + i] == 1, folded, 0.0)
            total += folded
            n += 1
    if not last:
        dots[...] = total
        return
    row = lax.broadcasted_iota(jnp.int32, dots.shape, 0)
    column = lax.broadcasted_iota(jnp.int32, dots.shape, 1)
    value = jnp.where(column == core, jnp.sum(total), 0.0)
    for v in range(z.batch):
        value += jnp.where(column == v, own_sums[v], 0.0)
    split = jnp.zeros(dots.shape, jnp.float32)
    for k in range(3):
        piece = value.astype(jnp.bfloat16).astype(jnp.float32)
        split = jnp.where(row == k, piece, split)
        value = value - piece
    split = split.astype(jnp.bfloat16)
    dots[...] = split
    for out in outs[1:]:
        out[n * z.own_rows :] = split


def terms(z, plan, left, near, far, vec, spans, so_far=None, own_sums=None, after=()):
    count = sum(span[1] for span in spans)
    flat = [ref for piece in vec for ref in piece]
    shapes = [(count, z.own_rows, z.order)] * (z.env * z.rep)
    whole = (count, z.order, z.order)
    last = own_sums is not None
    sums = jax.ShapeDtypeStruct((8, z.order), jnp.float32)
    if last:
        shapes[1:] = [(count * z.own_rows + TAIL, z.order)] * (z.env * z.rep - 1)
        sums = jax.ShapeDtypeStruct((TAIL, z.order), jnp.bfloat16)
    extra = [] if so_far is None else [so_far]
    specs = [VMEM] * len(extra)
    if last:
        extra.append(own_sums)
        specs.append(SMEM)
    *made, dots = pl.pallas_call(
        functools.partial(terms_body, z, spans, so_far is not None, last),
        out_shape=[jax.ShapeDtypeStruct(shape, jnp.bfloat16) for shape in shapes] + [sums],
        in_specs=[SMEM]
        + [VMEM] * (len(left) + len(near) + len(far) + len(flat))
        + specs
        + [ANY] * len(after),
        out_specs=[VMEM] * (len(shapes) + 1),
        scratch_shapes=[pltpu.VMEM(whole, jnp.bfloat16), pltpu.VMEM(whole, jnp.bfloat16)],
        compiler_params=pltpu.CompilerParams(vmem_limit_bytes=LIMIT),
        cost_estimate=BRIEF,
    )(plan, *left, *near, *far, *flat, *extra, *after)
    return made, dots


def for_terms(z, plans, parts, spans, action):
    n = 0
    for first, count, _ in spans:
        for i in range(count):
            for e, plan in enumerate(plans):

                def act():
                    blocks = []
                    for ref in parts[e]:
                        if len(ref.shape) == 3:
                            blocks.append(lambda ref=ref: ref[n])
                        else:
                            rows = slice(n * z.own_rows, (n + 1) * z.own_rows)
                            blocks.append(lambda ref=ref: ref[rows])
                    action(plan[z.target + first + i], blocks)

                z.when_valid(plan, first + i, act)
            n += 1


def add_terms(z, plans, image, parts, spans):
    core = plans[0][z.core]

    def add(slot, blocks):
        for s, block in enumerate(blocks):
            v = lax.rem(core + z.rep - s, z.rep)
            image[v, slot] += block().astype(jnp.float32)

    for_terms(z, plans, parts, spans, add)


def gather_body(z, chunks, *refs):
    refs = list(refs)
    plans = [refs.pop(0) for _ in range(z.env)]
    energy, vectors = refs.pop(0), refs.pop(0)
    so_far, image, sem = refs[-3:]

    def start(j, carry):
        for v in range(z.batch):
            so_far[v, j] = energy[j] * vectors[v, j].astype(jnp.float32)
        return carry

    lax.fori_loop(0, z.slots, start, 0, unroll=2)
    for spans in chunks:
        parts = [[refs.pop(0) for _ in range(z.rep)] for _ in range(z.env)]
        add_terms(z, plans, so_far, parts, spans)
    copies = []
    for v in range(z.batch):
        copies += split_copy(so_far.at[v], image.at[v], z.slots, sem.at[v])
    for copy in copies:
        copy.start()
    for copy in copies:
        copy.wait()


def gather_terms(z, plans, energy, vectors, parts, chunks, after=()):
    flat = [ref for chunk in parts for piece in chunk for ref in piece]
    shape = jax.ShapeDtypeStruct(vectors.shape, jnp.float32)
    return pl.pallas_call(
        functools.partial(gather_body, z, chunks),
        out_shape=[shape, pltpu.HBM(vectors.shape, jnp.float32)],
        in_specs=[SMEM] * (z.env + 1) + [VMEM] * (1 + len(flat)) + [ANY] * len(after),
        out_specs=[VMEM, HBM],
        scratch_shapes=[pltpu.SemaphoreType.DMA((z.batch, 4))],
        compiler_params=pltpu.CompilerParams(vmem_limit_bytes=LIMIT),
        cost_estimate=BRIEF,
    )(*plans, energy, vectors, *flat, *after)


def image_body(z, spans, *refs):
    refs = list(refs)
    plans = [refs.pop(0) for _ in range(z.env)]
    so_far = refs.pop(0)
    parts = [[refs.pop(0) for _ in range(z.rep)] for _ in range(z.env)]
    image, token, sums, sem = refs[-4:]
    token[...] = jnp.zeros_like(token)

    def take(slot, blocks):
        for v in range(z.batch):
            sums[v, slot] = so_far[v, slot]

    for_terms(z, plans, parts, spans, take)
    add_terms(z, plans, sums, parts, spans)
    for wait in (False, True):
        used = []

        def put(slot, blocks):
            for v in range(z.batch):
                copy = pltpu.make_async_copy(
                    sums.at[v, slot], image.at[v, slot], sem.at[len(used), v]
                )
                if wait:
                    copy.wait()
                else:
                    copy.start()
            used.append(slot)

        for_terms(z, plans, parts, spans, put)


def make_image(z, plans, so_far, image, parts, spans):
    flat = [ref for piece in parts for ref in piece]
    count = z.env * sum(span[1] for span in spans)
    return pl.pallas_call(
        functools.partial(image_body, z, spans),
        out_shape=[
            pltpu.HBM(image.shape, jnp.float32),
            jax.ShapeDtypeStruct((8, 128), jnp.float32),
        ],
        in_specs=[SMEM] * z.env + [VMEM] * (1 + len(flat)) + [HBM],
        out_specs=[HBM, VMEM],
        input_output_aliases={z.env + 1 + len(flat): 0},
        scratch_shapes=[
            pltpu.VMEM(image.shape, jnp.float32),
            pltpu.SemaphoreType.DMA((count, z.batch)),
        ],
        compiler_params=pltpu.CompilerParams(vmem_limit_bytes=LIMIT),
        cost_estimate=BRIEF,
    )(*plans, so_far, *flat, image)


def in_order(parts, places, count):
    total = 0.0
    for place in range(count):
        for part, at in zip(parts, places):
            total = total + jnp.where(at == place, part, 0.0)
    return total


def chips_body(z, count, plan, own, *refs):
    arrived, out = refs[:count], refs[-1]
    core, chip = plan[z.core], plan[z.chip]
    parts, places = [], []
    for e in range(z.env):
        for s in range(z.rep):
            ref = arrived[e * z.rep + s - 1] if e + s else own
            tail = ref[ref.shape[0] - TAIL :].astype(jnp.float32)
            parts.append(tail[0:1] + tail[1:2] + tail[2:3])
            at = lax.rem(chip + z.env - e, z.env) * z.rep + lax.rem(core + z.rep - s, z.rep)
            places.append(at)
    total = in_order(parts, places, z.env * z.rep)
    out[...] = jnp.broadcast_to(total, out.shape)


def chip_sums(z, plan, own, arrived, after):
    return pl.pallas_call(
        functools.partial(chips_body, z, len(arrived)),
        out_shape=jax.ShapeDtypeStruct((8, z.order), jnp.float32),
        in_specs=[SMEM] + [VMEM] * (1 + len(arrived)) + [ANY] * len(after),
        out_specs=VMEM,
        compiler_params=pltpu.CompilerParams(vmem_limit_bytes=SMALL),
        cost_estimate=BRIEF,
    )(plan, own, *arrived, *after)


def mean_body(z, count, scale, *refs):
    out = refs[-1]
    me = lax.axis_index("sector")
    parts = [ref[0:1] for ref in refs[:count]]
    total = parts[0]
    if count > 1:
        places = [lax.rem(me + z.sector - step, z.sector) for step in range(count)]
        total = in_order(parts, places, count)
    out[...] = total[:, : out.shape[1]] * scale


def mean_over_sectors(z, array, entries, after):
    held = [array]
    if z.sector <= 4:
        held += [shift(array, "sector", z.sector, step) for step in range(1, z.sector)]
    else:
        held = [total_over(array, "sector")]
    made = pl.pallas_call(
        functools.partial(mean_body, z, len(held), 1.0 / entries),
        out_shape=jax.ShapeDtypeStruct((1, z.batch), jnp.float32),
        in_specs=[VMEM] * len(held) + [ANY] * len(after),
        out_specs=VMEM,
        compiler_params=pltpu.CompilerParams(vmem_limit_bytes=SMALL),
        cost_estimate=BRIEF,
    )(*held, *after)
    return made.reshape(z.batch)


def shift(array, axis, size, step):
    return lax.ppermute(array, axis, [(i, (i + step) % size) for i in range(size)])


def shift_both(z, array, e, s):
    perm = []
    for x in range(z.env):
        for c in range(z.rep):
            perm.append((x * z.rep + c, (x + e) % z.env * z.rep + (c + s) % z.rep))
    return lax.ppermute(array, ("env", "rep"), perm)


def total_over(array, axis):
    size = lax.axis_size(axis)
    if size & (size - 1):
        return lax.psum(array, axis)
    step = 1
    while step < size:
        array = array + lax.ppermute(array, axis, [(i, i ^ step) for i in range(size)])
        step *= 2
    return array


def on_device(vectors, left_env, right_env, energy, partner):
    z = Sizes(vectors, left_env)
    each = z.sector // 4
    span = z.capacity

    def spans_of(g, low=0, high=span):
        return [((g * each + d) * span + low, high - low, low) for d in range(each)]

    chunks = {g: spans_of(g) for g in range(4)}
    cut = 2 * span // 3
    chunks[2], chunks[4] = spans_of(2, 0, cut), spans_of(2, cut, span)

    def around(array):
        return [array] + [shift(array, "rep", z.rep, s) for s in range(1, z.rep)]

    def across(arrays, g):
        steps = [g * each + d for d in range(each)]
        return [shift(a, "sector", z.sector, k) if k else a for a, k in zip(arrays, steps)]

    partners = [shift(partner, "env", z.env, e) for e in range(1, z.env)]
    vector_others = around(vectors)[1:]
    right_others = around(right_env)[1:]
    left = around(left_env)
    plan, own, right_own = load(z, partner, vectors, right_env)
    own = gate(own, partners)
    right = [right_own] + right_others
    near_rows = [own[0]] + vector_others
    vec = [near_rows]
    for e in range(1, z.env):
        vec.append([shift_both(z, own[s], e, s) for s in range(z.rep)])
    plans = [plan] + [plan_only(z, other) for other in partners]

    def near_products(g, after):
        return products(z, plan, right, [near_rows], [c[:2] for c in spans_of(g)], after)

    def far_products(g, after):
        return products(z, plan, right, vec[1:], [c[:2] for c in chunks[g]], after)

    near, far, parts = {}, {}, {}
    spans = [piece[:2] for g in (1, 3) for piece in chunks[g]]
    made = products(z, plan, right, [near_rows], spans)
    near[1], near[3] = across(made[:each], 1), across(made[each:], 3)
    made = near_products(2, (made[0], *left[1:]))
    near[2] = across(made, 2)
    sent = [array for g in (1, 3, 2) for array in near[g]]

    def send_terms(g, so_far, own_sums, after):
        made, folded = terms(
            z, plan, left, near[2 if g == 4 else g], far[g], vec, chunks[g], so_far, own_sums, after
        )
        parts[g] = [
            [
                shift_both(z, made[e * z.rep + s], e, s) if e + s else made[0]
                for s in range(z.rep)
            ]
            for e in range(z.env)
        ]
        return folded

    def arrived(g):
        return [part for piece in parts[g] for part in piece][1:]

    far1 = far_products(1, (made[0], *plans[1:]))
    far3 = far_products(3, far1[:1])
    far2 = far_products(2, far3[:1])
    far4 = far_products(4, far2[:1])
    near[0] = near_products(0, far4[:1])
    far[0] = far_products(0, near[0][:1])
    dots = send_terms(0, None, None, ())
    far[1] = across(gate(far1, [dots, *sent]), 1)
    far3 = gate(far3, [*far[1], *arrived(0)])
    far[3] = across(far3, 3)
    dots = send_terms(1, dots, None, far3[:1])
    far2 = gate([*far2, *far4], far[3])
    far[2], far[4] = across(far2[:each], 2), across(far2[each:], 2)
    dots = send_terms(3, dots, None, (far2[0], *arrived(1)))
    own_block = vectors.astype(jnp.float32)
    own_sums = jnp.sum(energy[None, :, None, None] * own_block * own_block, axis=(1, 2, 3))
    dots = send_terms(2, dots, None, arrived(3))
    dots = send_terms(4, dots, own_sums, arrived(2))
    early = (0, 1, 3, 2)
    so_far, image = gather_terms(
        z,
        plans,
        energy,
        vectors,
        [parts[g] for g in early],
        [chunks[g] for g in early],
        (dots,),
    )
    sums = chip_sums(z, plan, dots, arrived(4), (so_far,))
    image, token = make_image(z, plans, so_far, image, parts[4], chunks[4])
    entries = z.slots * z.sector * z.order * z.order
    return (image, mean_over_sectors(z, sums, entries, (token,)))


def solution(mesh):
    return jax.shard_map(
        on_device,
        mesh=mesh,
        in_specs=(
            P(None, ("groups", "sector"), ("env", "rep"), None),
            P("env", ("groups", "sector"), "rep", None),
            P("env", ("groups", "sector"), "rep", None),
            P(("groups", "sector")),
            P("env", "groups"),
        ),
        out_specs=(P(None, ("groups", "sector"), ("env", "rep"), None), P("groups")),
        check_vma=False,
    )
```

```python
import functools

import jax
import jax.numpy as jnp
from jax import lax
from jax.experimental import pallas as pl
from jax.experimental.pallas import tpu as pltpu
from jax.sharding import PartitionSpec as P

ANY = pl.BlockSpec(memory_space=pl.ANY)
HBM = pl.BlockSpec(memory_space=pltpu.HBM)
SMEM = pl.BlockSpec(memory_space=pltpu.SMEM)
VMEM = pl.BlockSpec(memory_space=pltpu.VMEM)
LIMIT = 12 * 1024 * 1024
SMALL = 2 * 1024 * 1024
TAIL = 16
BRIEF = pl.CostEstimate(flops=0, bytes_accessed=0, transcendentals=0)


def aligned(index, size):
    return pl.multiple_of(index * size, size)


class Sizes:
    def __init__(self, vectors, left_env):
        self.env = lax.axis_size("env")
        self.rep = lax.axis_size("rep")
        self.sector = lax.axis_size("sector")
        self.batch, self.slots, self.own_rows, self.order = vectors.shape
        assert self.batch == self.rep and self.sector % 4 == 0
        self.half = left_env.shape[2]
        self.chip_rows = self.own_rows * self.rep
        self.capacity = 2 * ((self.slots + 2 * self.sector - 1) // (2 * self.sector))
        self.flat = self.sector * self.capacity
        self.full = self.flat == self.slots
        self.source, self.target, self.valid = 0, self.flat, 2 * self.flat
        self.core, self.chip = 3 * self.flat, 3 * self.flat + 1

    def when_valid(self, plan, flat, action):
        if self.full:
            action()
        else:
            pl.when(plan[self.valid + flat] == 1)(action)


def write_plan(z, partner, plan, count):
    if not z.full:

        def clear(i, carry):
            plan[i] = 0
            return carry

        lax.fori_loop(0, 3 * z.flat, clear, 0)
    for d in range(z.sector):
        count[d] = 0
    factor = -(-(1 << 16) // z.slots)
    assert all(i * factor >> 16 == i // z.slots for i in range(z.sector * z.slots))
    for j in range(z.slots):
        sector = partner[0, j]
        group = (sector * factor) >> 16
        slot = sector - group * z.slots
        distance = jnp.where(group == 0, 0, z.sector - group)
        rank = count[distance]
        count[distance] = rank + 1
        index = distance * z.capacity + rank
        plan[z.source + index] = slot
        plan[z.target + index] = j
        plan[z.valid + index] = 1
    plan[z.core] = lax.axis_index("rep")
    plan[z.chip] = lax.axis_index("env")


def split_copy(source, target, slots, sem):
    step = slots // 4 if slots % 4 == 0 else slots
    copies = []
    for i in range(slots // step):
        part = pl.ds(i * step, step)
        copies.append(pltpu.make_async_copy(source.at[part], target.at[part], sem.at[i]))
    return copies


def load_body(z, partner, vectors, right, plan, *refs):
    rows, block, count, sem = refs[: z.rep], refs[z.rep], refs[-2], refs[-1]
    core = lax.axis_index("rep")
    copies = []
    for s, ref in enumerate(rows):
        mine = vectors.at[lax.rem(core + s, z.rep)]
        copies += split_copy(mine, ref, z.slots, sem.at[s])
    copies += split_copy(right.at[0], block.at[0], z.slots, sem.at[z.rep])
    for copy in copies:
        copy.start()
    write_plan(z, partner, plan, count)
    for copy in copies:
        copy.wait()


def load(z, partner, vectors, right_env):
    row = jax.ShapeDtypeStruct(vectors.shape[1:], jnp.bfloat16)
    plan, *made = pl.pallas_call(
        functools.partial(load_body, z),
        out_shape=[jax.ShapeDtypeStruct((3 * z.flat + 2,), jnp.int32)]
        + [row] * z.rep
        + [jax.ShapeDtypeStruct(right_env.shape, jnp.bfloat16)],
        in_specs=[SMEM, HBM, HBM],
        out_specs=[SMEM] + [VMEM] * (z.rep + 1),
        scratch_shapes=[
            pltpu.SMEM((z.sector,), jnp.int32),
            pltpu.SemaphoreType.DMA((z.rep + 1, 4)),
        ],
        compiler_params=pltpu.CompilerParams(vmem_limit_bytes=LIMIT),
        cost_estimate=BRIEF,
    )(
        partner,
        pltpu.with_memory_space_constraint(vectors, pltpu.HBM),
        pltpu.with_memory_space_constraint(right_env, pltpu.HBM),
    )
    return plan, made[: z.rep], made[z.rep]


def plan_only(z, partner):
    return pl.pallas_call(
        functools.partial(write_plan, z),
        out_shape=jax.ShapeDtypeStruct((3 * z.flat + 2,), jnp.int32),
        in_specs=[SMEM],
        out_specs=SMEM,
        scratch_shapes=[pltpu.SMEM((z.sector,), jnp.int32)],
        compiler_params=pltpu.CompilerParams(vmem_limit_bytes=SMALL),
        cost_estimate=BRIEF,
    )(partner)


def gate(arrays, after):
    def body(*refs):
        pass

    return pl.pallas_call(
        body,
        out_shape=[jax.ShapeDtypeStruct(a.shape, a.dtype) for a in arrays],
        in_specs=[ANY] * (len(arrays) + len(after)),
        out_specs=[ANY] * len(arrays),
        input_output_aliases={i: i for i in range(len(arrays))},
        compiler_params=pltpu.CompilerParams(vmem_limit_bytes=SMALL),
        cost_estimate=BRIEF,
    )(*arrays, *after)


def pick(z, core, place, candidates):
    chosen = candidates[0]
    for s in range(1, z.rep):
        chosen = jnp.where(lax.rem(core + z.rep - s, z.rep) == place, candidates[s], chosen)
    return chosen


def line(ref, core, slot):
    return ref[core, slot] if len(ref.shape) == 4 else ref[slot]


def products_body(z, pieces, spans, *refs):
    refs = list(refs)
    plan = refs.pop(0)
    right = [refs.pop(0) for _ in range(z.rep)]
    rows = [[refs.pop(0) for _ in range(z.rep)] for _ in range(pieces)]
    outs = refs[-len(spans) :]
    core = plan[z.core]
    for (first, count), out in zip(spans, outs):
        for i in range(count):
            slot = plan[z.source + first + i]
            halves = [ref[0, slot] for ref in right]
            parts = [[line(ref, core, slot) for ref in piece] for piece in rows]
            block = jnp.concatenate([pick(z, core, k, halves) for k in range(z.rep)], axis=0)
            lines = jnp.concatenate(
                [pick(z, core, k, part) for part in parts for k in range(z.rep)], axis=0
            )
            out[i] = lax.dot_general(
                lines, block, (((1,), (1,)), ((), ())), preferred_element_type=jnp.float32
            ).astype(jnp.bfloat16)


def products(z, plan, right, rows, spans, after=()):
    pieces = len(rows)
    flat = [ref for piece in rows for ref in piece]
    height = pieces * z.chip_rows
    return pl.pallas_call(
        functools.partial(products_body, z, pieces, spans),
        out_shape=[
            jax.ShapeDtypeStruct((count, height, z.order), jnp.bfloat16) for _, count in spans
        ],
        in_specs=[SMEM] + [VMEM] * (len(right) + len(flat)) + [ANY] * len(after),
        out_specs=[VMEM] * len(spans),
        compiler_params=pltpu.CompilerParams(vmem_limit_bytes=LIMIT),
        cost_estimate=BRIEF,
    )(plan, *right, *flat, *after)


def terms_body(z, spans, chained, last, *refs):
    refs = list(refs)
    plan = refs.pop(0)
    left = [refs.pop(0) for _ in range(z.rep)]
    near = [refs.pop(0) for _ in spans]
    far = [refs.pop(0) for _ in spans]
    vec = [[refs.pop(0) for _ in range(z.rep)] for _ in range(z.env)]
    so_far = refs.pop(0) if chained else None
    own_sums = refs.pop(0) if last else None
    pbuf, tbuf = refs[-2:]
    dots = refs[-3]
    outs = refs[-3 - z.env * z.rep : -3]
    core, chip = plan[z.core], plan[z.chip]
    total = so_far[...] if chained else jnp.zeros((8, z.order), jnp.float32)
    n = 0
    for d, (first, count, skip) in enumerate(spans):
        for i in range(count):
            slot = plan[z.target + first + i]
            for e in range(z.env):
                place = lax.rem(chip + z.env - e, z.env)
                if e == 0:
                    lines = near[d][skip + i]
                else:
                    lines = far[d][i, (e - 1) * z.chip_rows : e * z.chip_rows]
                pbuf[n, pl.ds(aligned(place, z.chip_rows), z.chip_rows)] = lines
            halves = [ref[0, slot] for ref in left]
            block = jnp.concatenate([pick(z, core, k, halves) for k in range(z.rep)], axis=0)
            tbuf[n] = jnp.dot(block, pbuf[n], preferred_element_type=jnp.float32).astype(
                jnp.bfloat16
            )
            folded = jnp.zeros(total.shape, jnp.float32)
            for e in range(z.env):
                for s in range(z.rep):
                    place = lax.rem(chip + e, z.env) * z.rep + lax.rem(core + s, z.rep)
                    term = tbuf[n, pl.ds(aligned(place, z.own_rows), z.own_rows)]
                    if last and e + s:
                        outs[e * z.rep + s][n * z.own_rows : (n + 1) * z.own_rows] = term
                    else:
                        outs[e * z.rep + s][n] = term
                    lines = line(vec[(z.env - e) % z.env][(z.rep - s) % z.rep], core, slot)
                    both = lines.astype(jnp.float32) * term.astype(jnp.float32)
                    folded += jnp.sum(both.reshape(-1, *total.shape), axis=0)
            if not z.full:
                folded = jnp.where(plan[z.valid + first + i] == 1, folded, 0.0)
            total += folded
            n += 1
    if not last:
        dots[...] = total
        return
    row = lax.broadcasted_iota(jnp.int32, dots.shape, 0)
    column = lax.broadcasted_iota(jnp.int32, dots.shape, 1)
    value = jnp.where(column == core, jnp.sum(total), 0.0)
    for v in range(z.batch):
        value += jnp.where(column == v, own_sums[v], 0.0)
    split = jnp.zeros(dots.shape, jnp.float32)
    for k in range(3):
        piece = value.astype(jnp.bfloat16).astype(jnp.float32)
        split = jnp.where(row == k, piece, split)
        value = value - piece
    split = split.astype(jnp.bfloat16)
    dots[...] = split
    for out in outs[1:]:
        out[n * z.own_rows :] = split


def terms(z, plan, left, near, far, vec, spans, so_far=None, own_sums=None, after=()):
    count = sum(span[1] for span in spans)
    flat = [ref for piece in vec for ref in piece]
    shapes = [(count, z.own_rows, z.order)] * (z.env * z.rep)
    whole = (count, z.order, z.order)
    last = own_sums is not None
    sums = jax.ShapeDtypeStruct((8, z.order), jnp.float32)
    if last:
        shapes[1:] = [(count * z.own_rows + TAIL, z.order)] * (z.env * z.rep - 1)
        sums = jax.ShapeDtypeStruct((TAIL, z.order), jnp.bfloat16)
    extra = [] if so_far is None else [so_far]
    specs = [VMEM] * len(extra)
    if last:
        extra.append(own_sums)
        specs.append(SMEM)
    *made, dots = pl.pallas_call(
        functools.partial(terms_body, z, spans, so_far is not None, last),
        out_shape=[jax.ShapeDtypeStruct(shape, jnp.bfloat16) for shape in shapes] + [sums],
        in_specs=[SMEM]
        + [VMEM] * (len(left) + len(near) + len(far) + len(flat))
        + specs
        + [ANY] * len(after),
        out_specs=[VMEM] * (len(shapes) + 1),
        scratch_shapes=[pltpu.VMEM(whole, jnp.bfloat16), pltpu.VMEM(whole, jnp.bfloat16)],
        compiler_params=pltpu.CompilerParams(vmem_limit_bytes=LIMIT),
        cost_estimate=BRIEF,
    )(plan, *left, *near, *far, *flat, *extra, *after)
    return made, dots


def for_terms(z, plans, parts, spans, action):
    n = 0
    for first, count, _ in spans:
        for i in range(count):
            for e, plan in enumerate(plans):

                def act():
                    blocks = []
                    for ref in parts[e]:
                        if len(ref.shape) == 3:
                            blocks.append(lambda ref=ref: ref[n])
                        else:
                            rows = slice(n * z.own_rows, (n + 1) * z.own_rows)
                            blocks.append(lambda ref=ref: ref[rows])
                    action(plan[z.target + first + i], blocks)

                z.when_valid(plan, first + i, act)
            n += 1


def add_terms(z, plans, image, parts, spans):
    core = plans[0][z.core]

    def add(slot, blocks):
        for s, block in enumerate(blocks):
            v = lax.rem(core + z.rep - s, z.rep)
            image[v, slot] += block().astype(jnp.float32)

    for_terms(z, plans, parts, spans, add)


def gather_body(z, chunks, *refs):
    refs = list(refs)
    plans = [refs.pop(0) for _ in range(z.env)]
    energy, vectors = refs.pop(0), refs.pop(0)
    so_far, image, sem = refs[-3:]

    def start(j, carry):
        for v in range(z.batch):
            so_far[v, j] = energy[j] * vectors[v, j].astype(jnp.float32)
        return carry

    lax.fori_loop(0, z.slots, start, 0, unroll=2)
    for spans in chunks:
        parts = [[refs.pop(0) for _ in range(z.rep)] for _ in range(z.env)]
        add_terms(z, plans, so_far, parts, spans)
    copies = []
    for v in range(z.batch):
        copies += split_copy(so_far.at[v], image.at[v], z.slots, sem.at[v])
    for copy in copies:
        copy.start()
    for copy in copies:
        copy.wait()


def gather_terms(z, plans, energy, vectors, parts, chunks, after=()):
    flat = [ref for chunk in parts for piece in chunk for ref in piece]
    shape = jax.ShapeDtypeStruct(vectors.shape, jnp.float32)
    return pl.pallas_call(
        functools.partial(gather_body, z, chunks),
        out_shape=[shape, pltpu.HBM(vectors.shape, jnp.float32)],
        in_specs=[SMEM] * (z.env + 1) + [VMEM] * (1 + len(flat)) + [ANY] * len(after),
        out_specs=[VMEM, HBM],
        scratch_shapes=[pltpu.SemaphoreType.DMA((z.batch, 4))],
        compiler_params=pltpu.CompilerParams(vmem_limit_bytes=LIMIT),
        cost_estimate=BRIEF,
    )(*plans, energy, vectors, *flat, *after)


def image_body(z, spans, *refs):
    refs = list(refs)
    plans = [refs.pop(0) for _ in range(z.env)]
    so_far = refs.pop(0)
    parts = [[refs.pop(0) for _ in range(z.rep)] for _ in range(z.env)]
    image, token, sums, sem = refs[-4:]
    token[...] = jnp.zeros_like(token)

    def take(slot, blocks):
        for v in range(z.batch):
            sums[v, slot] = so_far[v, slot]

    for_terms(z, plans, parts, spans, take)
    add_terms(z, plans, sums, parts, spans)
    for wait in (False, True):
        used = []

        def put(slot, blocks):
            for v in range(z.batch):
                copy = pltpu.make_async_copy(
                    sums.at[v, slot], image.at[v, slot], sem.at[len(used), v]
                )
                if wait:
                    copy.wait()
                else:
                    copy.start()
            used.append(slot)

        for_terms(z, plans, parts, spans, put)


def make_image(z, plans, so_far, image, parts, spans):
    flat = [ref for piece in parts for ref in piece]
    count = z.env * sum(span[1] for span in spans)
    return pl.pallas_call(
        functools.partial(image_body, z, spans),
        out_shape=[
            pltpu.HBM(image.shape, jnp.float32),
            jax.ShapeDtypeStruct((8, 128), jnp.float32),
        ],
        in_specs=[SMEM] * z.env + [VMEM] * (1 + len(flat)) + [HBM],
        out_specs=[HBM, VMEM],
        input_output_aliases={z.env + 1 + len(flat): 0},
        scratch_shapes=[
            pltpu.VMEM(image.shape, jnp.float32),
            pltpu.SemaphoreType.DMA((count, z.batch)),
        ],
        compiler_params=pltpu.CompilerParams(vmem_limit_bytes=LIMIT),
        cost_estimate=BRIEF,
    )(*plans, so_far, *flat, image)


def in_order(parts, places, count):
    total = 0.0
    for place in range(count):
        for part, at in zip(parts, places):
            total = total + jnp.where(at == place, part, 0.0)
    return total


def chips_body(z, count, plan, own, *refs):
    arrived, out = refs[:count], refs[-1]
    core, chip = plan[z.core], plan[z.chip]
    parts, places = [], []
    for e in range(z.env):
        for s in range(z.rep):
            ref = arrived[e * z.rep + s - 1] if e + s else own
            tail = ref[ref.shape[0] - TAIL :].astype(jnp.float32)
            parts.append(tail[0:1] + tail[1:2] + tail[2:3])
            at = lax.rem(chip + z.env - e, z.env) * z.rep + lax.rem(core + z.rep - s, z.rep)
            places.append(at)
    total = in_order(parts, places, z.env * z.rep)
    out[...] = jnp.broadcast_to(total, out.shape)


def chip_sums(z, plan, own, arrived, after):
    return pl.pallas_call(
        functools.partial(chips_body, z, len(arrived)),
        out_shape=jax.ShapeDtypeStruct((8, z.order), jnp.float32),
        in_specs=[SMEM] + [VMEM] * (1 + len(arrived)) + [ANY] * len(after),
        out_specs=VMEM,
        compiler_params=pltpu.CompilerParams(vmem_limit_bytes=SMALL),
        cost_estimate=BRIEF,
    )(plan, own, *arrived, *after)


def mean_body(z, count, scale, *refs):
    out = refs[-1]
    me = lax.axis_index("sector")
    parts = [ref[0:1] for ref in refs[:count]]
    total = parts[0]
    if count > 1:
        places = [lax.rem(me + z.sector - step, z.sector) for step in range(count)]
        total = in_order(parts, places, count)
    out[...] = total[:, : out.shape[1]] * scale


def mean_over_sectors(z, array, entries, after):
    held = [array]
    if z.sector <= 4:
        held += [shift(array, "sector", z.sector, step) for step in range(1, z.sector)]
    else:
        held = [total_over(array, "sector")]
    made = pl.pallas_call(
        functools.partial(mean_body, z, len(held), 1.0 / entries),
        out_shape=jax.ShapeDtypeStruct((1, z.batch), jnp.float32),
        in_specs=[VMEM] * len(held) + [ANY] * len(after),
        out_specs=VMEM,
        compiler_params=pltpu.CompilerParams(vmem_limit_bytes=SMALL),
        cost_estimate=BRIEF,
    )(*held, *after)
    return made.reshape(z.batch)


def shift(array, axis, size, step):
    return lax.ppermute(array, axis, [(i, (i + step) % size) for i in range(size)])


def shift_both(z, array, e, s):
    perm = []
    for x in range(z.env):
        for c in range(z.rep):
            perm.append((x * z.rep + c, (x + e) % z.env * z.rep + (c + s) % z.rep))
    return lax.ppermute(array, ("env", "rep"), perm)


def total_over(array, axis):
    size = lax.axis_size(axis)
    if size & (size - 1):
        return lax.psum(array, axis)
    step = 1
    while step < size:
        array = array + lax.ppermute(array, axis, [(i, i ^ step) for i in range(size)])
        step *= 2
    return array


def on_device(vectors, left_env, right_env, energy, partner):
    z = Sizes(vectors, left_env)
    each = z.sector // 4
    span = z.capacity

    def spans_of(g, low=0, high=span):
        return [((g * each + d) * span + low, high - low, low) for d in range(each)]

    chunks = {g: spans_of(g) for g in range(4)}
    cut = 2 * span // 3
    chunks[2], chunks[4] = spans_of(2, 0, cut), spans_of(2, cut, span)

    def around(array):
        return [array] + [shift(array, "rep", z.rep, s) for s in range(1, z.rep)]

    def across(arrays, g):
        steps = [g * each + d for d in range(each)]
        return [shift(a, "sector", z.sector, k) if k else a for a, k in zip(arrays, steps)]

    partners = [shift(partner, "env", z.env, e) for e in range(1, z.env)]
    vector_others = around(vectors)[1:]
    right_others = around(right_env)[1:]
    left = around(left_env)
    plan, own, right_own = load(z, partner, vectors, right_env)
    own = gate(own, partners)
    right = [right_own] + right_others
    near_rows = [own[0]] + vector_others
    vec = [near_rows]
    for e in range(1, z.env):
        vec.append([shift_both(z, own[s], e, s) for s in range(z.rep)])
    plans = [plan] + [plan_only(z, other) for other in partners]

    def near_products(g, after):
        return products(z, plan, right, [near_rows], [c[:2] for c in spans_of(g)], after)

    def far_products(g, after):
        return products(z, plan, right, vec[1:], [c[:2] for c in chunks[g]], after)

    near, far, parts = {}, {}, {}
    spans = [piece[:2] for g in (1, 3) for piece in chunks[g]]
    made = products(z, plan, right, [near_rows], spans)
    near[1], near[3] = across(made[:each], 1), across(made[each:], 3)
    made = near_products(2, (made[0], *left[1:]))
    near[2] = across(made, 2)

    def send_terms(g, so_far, own_sums, after):
        made, folded = terms(
            z, plan, left, near[2 if g == 4 else g], far[g], vec, chunks[g], so_far, own_sums, after
        )
        parts[g] = [
            [
                shift_both(z, made[e * z.rep + s], e, s) if e + s else made[0]
                for s in range(z.rep)
            ]
            for e in range(z.env)
        ]
        return folded

    def arrived(g):
        return [part for piece in parts[g] for part in piece][1:]

    far1 = far_products(1, (made[0], *plans[1:]))
    far1 = gate(far1, [*near[1], *near[3]])
    far[1] = across(far1, 1)
    near[0] = near_products(0, far1[:1])
    far[0] = far_products(0, near[0][:1])
    dots = send_terms(0, None, None, ())
    far3 = far_products(3, (dots,))
    far2 = far_products(2, far3[:1])
    far4 = far_products(4, far2[:1])
    far3 = gate(far3, [far4[0], *near[2]])
    far[3] = across(far3, 3)
    far2 = gate([*far2, *far4], [far3[0], *far[1]])
    far[2], far[4] = across(far2[:each], 2), across(far2[each:], 2)
    dots = send_terms(1, dots, None, (far2[0], *arrived(0)))
    dots = send_terms(3, dots, None, arrived(1))
    own_block = vectors.astype(jnp.float32)
    own_sums = jnp.sum(energy[None, :, None, None] * own_block * own_block, axis=(1, 2, 3))
    dots = send_terms(2, dots, None, arrived(3))
    dots = send_terms(4, dots, own_sums, arrived(2))
    early = (0, 1, 3, 2)
    so_far, image = gather_terms(
        z,
        plans,
        energy,
        vectors,
        [parts[g] for g in early],
        [chunks[g] for g in early],
        (dots,),
    )
    sums = chip_sums(z, plan, dots, arrived(4), (so_far,))
    image, token = make_image(z, plans, so_far, image, parts[4], chunks[4])
    entries = z.slots * z.sector * z.order * z.order
    return (image, mean_over_sectors(z, sums, entries, (token,)))


def solution(mesh):
    return jax.shard_map(
        on_device,
        mesh=mesh,
        in_specs=(
            P(None, ("groups", "sector"), ("env", "rep"), None),
            P("env", ("groups", "sector"), "rep", None),
            P("env", ("groups", "sector"), "rep", None),
            P(("groups", "sector")),
            P("env", "groups"),
        ),
        out_specs=(P(None, ("groups", "sector"), ("env", "rep"), None), P("groups")),
        check_vma=False,
    )
```

```python
import functools

import jax
import jax.numpy as jnp
from jax import lax
from jax.experimental import pallas as pl
from jax.experimental.pallas import tpu as pltpu
from jax.sharding import PartitionSpec as P

ANY = pl.BlockSpec(memory_space=pl.ANY)
HBM = pl.BlockSpec(memory_space=pltpu.HBM)
SMEM = pl.BlockSpec(memory_space=pltpu.SMEM)
VMEM = pl.BlockSpec(memory_space=pltpu.VMEM)
LIMIT = 12 * 1024 * 1024
SMALL = 2 * 1024 * 1024
TAIL = 16
BRIEF = pl.CostEstimate(flops=0, bytes_accessed=0, transcendentals=0)


def aligned(index, size):
    return pl.multiple_of(index * size, size)


class Sizes:
    def __init__(self, vectors, left_env):
        self.env = lax.axis_size("env")
        self.rep = lax.axis_size("rep")
        self.sector = lax.axis_size("sector")
        self.batch, self.slots, self.own_rows, self.order = vectors.shape
        assert self.batch == self.rep and self.sector % 4 == 0
        self.half = left_env.shape[2]
        self.chip_rows = self.own_rows * self.rep
        self.capacity = 2 * ((self.slots + 2 * self.sector - 1) // (2 * self.sector))
        self.flat = self.sector * self.capacity
        self.full = self.flat == self.slots
        self.source, self.target, self.valid = 0, self.flat, 2 * self.flat
        self.core, self.chip = 3 * self.flat, 3 * self.flat + 1

    def when_valid(self, plan, flat, action):
        if self.full:
            action()
        else:
            pl.when(plan[self.valid + flat] == 1)(action)


def write_plan(z, partner, plan, count):
    if not z.full:

        def clear(i, carry):
            plan[i] = 0
            return carry

        lax.fori_loop(0, 3 * z.flat, clear, 0)
    for d in range(z.sector):
        count[d] = 0
    factor = -(-(1 << 16) // z.slots)
    assert all(i * factor >> 16 == i // z.slots for i in range(z.sector * z.slots))
    for j in range(z.slots):
        sector = partner[0, j]
        group = (sector * factor) >> 16
        slot = sector - group * z.slots
        distance = jnp.where(group == 0, 0, z.sector - group)
        rank = count[distance]
        count[distance] = rank + 1
        index = distance * z.capacity + rank
        plan[z.source + index] = slot
        plan[z.target + index] = j
        plan[z.valid + index] = 1
    plan[z.core] = lax.axis_index("rep")
    plan[z.chip] = lax.axis_index("env")


def split_copy(source, target, slots, sem):
    step = slots // 4 if slots % 4 == 0 else slots
    copies = []
    for i in range(slots // step):
        part = pl.ds(i * step, step)
        copies.append(pltpu.make_async_copy(source.at[part], target.at[part], sem.at[i]))
    return copies


def load_body(z, partner, vectors, right, plan, *refs):
    rows, block, count, sem = refs[: z.rep], refs[z.rep], refs[-2], refs[-1]
    core = lax.axis_index("rep")
    copies = []
    for s, ref in enumerate(rows):
        mine = vectors.at[lax.rem(core + s, z.rep)]
        copies += split_copy(mine, ref, z.slots, sem.at[s])
    copies += split_copy(right.at[0], block.at[0], z.slots, sem.at[z.rep])
    for copy in copies:
        copy.start()
    write_plan(z, partner, plan, count)
    for copy in copies:
        copy.wait()


def load(z, partner, vectors, right_env):
    row = jax.ShapeDtypeStruct(vectors.shape[1:], jnp.bfloat16)
    plan, *made = pl.pallas_call(
        functools.partial(load_body, z),
        out_shape=[jax.ShapeDtypeStruct((3 * z.flat + 2,), jnp.int32)]
        + [row] * z.rep
        + [jax.ShapeDtypeStruct(right_env.shape, jnp.bfloat16)],
        in_specs=[SMEM, HBM, HBM],
        out_specs=[SMEM] + [VMEM] * (z.rep + 1),
        scratch_shapes=[
            pltpu.SMEM((z.sector,), jnp.int32),
            pltpu.SemaphoreType.DMA((z.rep + 1, 4)),
        ],
        compiler_params=pltpu.CompilerParams(vmem_limit_bytes=LIMIT),
        cost_estimate=BRIEF,
    )(
        partner,
        pltpu.with_memory_space_constraint(vectors, pltpu.HBM),
        pltpu.with_memory_space_constraint(right_env, pltpu.HBM),
    )
    return plan, made[: z.rep], made[z.rep]


def plan_only(z, partner):
    return pl.pallas_call(
        functools.partial(write_plan, z),
        out_shape=jax.ShapeDtypeStruct((3 * z.flat + 2,), jnp.int32),
        in_specs=[SMEM],
        out_specs=SMEM,
        scratch_shapes=[pltpu.SMEM((z.sector,), jnp.int32)],
        compiler_params=pltpu.CompilerParams(vmem_limit_bytes=SMALL),
        cost_estimate=BRIEF,
    )(partner)


def gate(arrays, after):
    def body(*refs):
        pass

    return pl.pallas_call(
        body,
        out_shape=[jax.ShapeDtypeStruct(a.shape, a.dtype) for a in arrays],
        in_specs=[ANY] * (len(arrays) + len(after)),
        out_specs=[ANY] * len(arrays),
        input_output_aliases={i: i for i in range(len(arrays))},
        compiler_params=pltpu.CompilerParams(vmem_limit_bytes=SMALL),
        cost_estimate=BRIEF,
    )(*arrays, *after)


def pick(z, core, place, candidates):
    chosen = candidates[0]
    for s in range(1, z.rep):
        chosen = jnp.where(lax.rem(core + z.rep - s, z.rep) == place, candidates[s], chosen)
    return chosen


def line(ref, core, slot):
    return ref[core, slot] if len(ref.shape) == 4 else ref[slot]


def products_body(z, pieces, spans, *refs):
    refs = list(refs)
    plan = refs.pop(0)
    right = [refs.pop(0) for _ in range(z.rep)]
    rows = [[refs.pop(0) for _ in range(z.rep)] for _ in range(pieces)]
    outs = refs[-len(spans) :]
    core = plan[z.core]
    for (first, count), out in zip(spans, outs):
        for i in range(count):
            slot = plan[z.source + first + i]
            halves = [ref[0, slot] for ref in right]
            parts = [[line(ref, core, slot) for ref in piece] for piece in rows]
            block = jnp.concatenate([pick(z, core, k, halves) for k in range(z.rep)], axis=0)
            lines = jnp.concatenate(
                [pick(z, core, k, part) for part in parts for k in range(z.rep)], axis=0
            )
            out[i] = lax.dot_general(
                lines, block, (((1,), (1,)), ((), ())), preferred_element_type=jnp.float32
            ).astype(jnp.bfloat16)


def products(z, plan, right, rows, spans, after=()):
    pieces = len(rows)
    flat = [ref for piece in rows for ref in piece]
    height = pieces * z.chip_rows
    return pl.pallas_call(
        functools.partial(products_body, z, pieces, spans),
        out_shape=[
            jax.ShapeDtypeStruct((count, height, z.order), jnp.bfloat16) for _, count in spans
        ],
        in_specs=[SMEM] + [VMEM] * (len(right) + len(flat)) + [ANY] * len(after),
        out_specs=[VMEM] * len(spans),
        compiler_params=pltpu.CompilerParams(vmem_limit_bytes=LIMIT),
        cost_estimate=BRIEF,
    )(plan, *right, *flat, *after)


def terms_body(z, spans, chained, last, kept, *refs):
    refs = list(refs)
    plan = refs.pop(0)
    left = [refs.pop(0) for _ in range(z.rep)]
    near = [refs.pop(0) for _ in spans]
    far = [refs.pop(0) for _ in spans]
    vec = [[refs.pop(0) for _ in range(z.rep)] for _ in range(z.env)]
    so_far = refs.pop(0) if chained else None
    own_sums = refs.pop(0) if last else None
    kept = [[refs.pop(0) for _ in range(z.rep - 1)] for _ in range(kept)]
    pbuf, tbuf = refs[-2:]
    dots = refs[-3]
    outs = refs[-3 - z.env * z.rep : -3]
    core, chip = plan[z.core], plan[z.chip]
    total = so_far[...] if chained else jnp.zeros((8, z.order), jnp.float32)
    n = 0
    for d, (first, count, skip) in enumerate(spans):
        for i in range(count):
            slot = plan[z.target + first + i]
            for e in range(z.env):
                place = lax.rem(chip + z.env - e, z.env)
                if e == 0:
                    lines = near[d][skip + i]
                else:
                    lines = far[d][i, (e - 1) * z.chip_rows : e * z.chip_rows]
                pbuf[n, pl.ds(aligned(place, z.chip_rows), z.chip_rows)] = lines
            halves = [ref[0, slot] for ref in left]
            block = jnp.concatenate([pick(z, core, k, halves) for k in range(z.rep)], axis=0)
            tbuf[n] = jnp.dot(block, pbuf[n], preferred_element_type=jnp.float32).astype(
                jnp.bfloat16
            )
            folded = jnp.zeros(total.shape, jnp.float32)
            for e in range(z.env):
                for s in range(z.rep):
                    place = lax.rem(chip + e, z.env) * z.rep + lax.rem(core + s, z.rep)
                    term = tbuf[n, pl.ds(aligned(place, z.own_rows), z.own_rows)]
                    if last and e + s:
                        outs[e * z.rep + s][n * z.own_rows : (n + 1) * z.own_rows] = term
                    else:
                        outs[e * z.rep + s][n] = term
                    lines = line(vec[(z.env - e) % z.env][(z.rep - s) % z.rep], core, slot)
                    both = lines.astype(jnp.float32) * term.astype(jnp.float32)
                    folded += jnp.sum(both.reshape(-1, *total.shape), axis=0)
            if not z.full:
                folded = jnp.where(plan[z.valid + first + i] == 1, folded, 0.0)
            total += folded
            n += 1
    if not last:
        dots[...] = total
        return
    row = lax.broadcasted_iota(jnp.int32, dots.shape, 0)
    column = lax.broadcasted_iota(jnp.int32, dots.shape, 1)
    value = jnp.where(column == core, jnp.sum(total), 0.0)
    for v in range(z.batch):
        value += jnp.where(column == v, own_sums[v], 0.0)
    split = jnp.zeros(dots.shape, jnp.float32)
    for k in range(3):
        piece = value.astype(jnp.bfloat16).astype(jnp.float32)
        split = jnp.where(row == k, piece, split)
        value = value - piece
    split = split.astype(jnp.bfloat16)
    dots[...] = split
    at = n * z.own_rows
    for blocks in kept:
        for s, block in enumerate(blocks):
            for i in range(block.shape[0]):
                outs[1 + s][at + i * z.own_rows : at + (i + 1) * z.own_rows] = block[i]
        at += blocks[0].shape[0] * z.own_rows
    for out in outs[1:]:
        out[out.shape[0] - TAIL :] = split


def terms(z, plan, left, near, far, vec, spans, so_far=None, own_sums=None, kept=(), after=()):
    count = sum(span[1] for span in spans)
    flat = [ref for piece in vec for ref in piece]
    shapes = [(count, z.own_rows, z.order)] * (z.env * z.rep)
    whole = (count, z.order, z.order)
    last = own_sums is not None
    sums = jax.ShapeDtypeStruct((8, z.order), jnp.float32)
    if last:
        shapes[1:] = [(count * z.own_rows + TAIL, z.order)] * (z.env * z.rep - 1)
        more = sum(blocks[0].shape[0] for blocks in kept)
        shapes[1 : z.rep] = [((count + more) * z.own_rows + TAIL, z.order)] * (z.rep - 1)
        sums = jax.ShapeDtypeStruct((TAIL, z.order), jnp.bfloat16)
    extra = [] if so_far is None else [so_far]
    specs = [VMEM] * len(extra)
    if last:
        extra.append(own_sums)
        specs.append(SMEM)
    extra += [block for blocks in kept for block in blocks]
    specs += [VMEM] * (len(extra) - len(specs))
    *made, dots = pl.pallas_call(
        functools.partial(terms_body, z, spans, so_far is not None, last, len(kept)),
        out_shape=[jax.ShapeDtypeStruct(shape, jnp.bfloat16) for shape in shapes] + [sums],
        in_specs=[SMEM]
        + [VMEM] * (len(left) + len(near) + len(far) + len(flat))
        + specs
        + [ANY] * len(after),
        out_specs=[VMEM] * (len(shapes) + 1),
        scratch_shapes=[pltpu.VMEM(whole, jnp.bfloat16), pltpu.VMEM(whole, jnp.bfloat16)],
        compiler_params=pltpu.CompilerParams(vmem_limit_bytes=LIMIT),
        cost_estimate=BRIEF,
    )(plan, *left, *near, *far, *flat, *extra, *after)
    return made, dots


def for_terms(z, plans, parts, spans, action):
    n = 0
    for first, count, _ in spans:
        for i in range(count):
            for e, plan in enumerate(plans):

                def act():
                    blocks = []
                    for ref, skip in parts[e]:
                        if len(ref.shape) == 3:
                            blocks.append(lambda ref=ref: ref[n])
                        else:
                            rows = slice((skip + n) * z.own_rows, (skip + n + 1) * z.own_rows)
                            blocks.append(lambda ref=ref, rows=rows: ref[rows])
                    action(plan[z.target + first + i], blocks)

                z.when_valid(plan, first + i, act)
            n += 1


def add_terms(z, plans, image, parts, spans):
    core = plans[0][z.core]

    def add(slot, blocks):
        for s, block in enumerate(blocks):
            v = lax.rem(core + z.rep - s, z.rep)
            image[v, slot] += block().astype(jnp.float32)

    for_terms(z, plans, parts, spans, add)


def gather_body(z, chunks, skip, *refs):
    refs = list(refs)
    plans = [refs.pop(0) for _ in range(z.env)]
    energy, vectors = refs.pop(0), refs.pop(0)
    so_far, image, sem = refs[-3:]

    def start(j, carry):
        for v in range(z.batch):
            so_far[v, j] = energy[j] * vectors[v, j].astype(jnp.float32)
        return carry

    lax.fori_loop(0, z.slots, start, 0, unroll=2)
    joined = [refs.pop(0) for _ in range(z.rep - 1)]
    for spans in chunks:
        parts = [[(refs.pop(0), 0)] + [(ref, skip) for ref in joined]]
        for _ in range(1, z.env):
            parts.append([(refs.pop(0), 0) for _ in range(z.rep)])
        add_terms(z, plans, so_far, parts, spans)
        skip += sum(span[1] for span in spans)
    copies = []
    for v in range(z.batch):
        copies += split_copy(so_far.at[v], image.at[v], z.slots, sem.at[v])
    for copy in copies:
        copy.start()
    for copy in copies:
        copy.wait()


def gather_terms(z, plans, energy, vectors, joined, skip, parts, chunks, after=()):
    flat = [*joined]
    for chunk in parts:
        flat += [chunk[0][0]] + [ref for piece in chunk[1:] for ref in piece]
    shape = jax.ShapeDtypeStruct(vectors.shape, jnp.float32)
    return pl.pallas_call(
        functools.partial(gather_body, z, chunks, skip),
        out_shape=[shape, pltpu.HBM(vectors.shape, jnp.float32)],
        in_specs=[SMEM] * (z.env + 1) + [VMEM] * (1 + len(flat)) + [ANY] * len(after),
        out_specs=[VMEM, HBM],
        scratch_shapes=[pltpu.SemaphoreType.DMA((z.batch, 4))],
        compiler_params=pltpu.CompilerParams(vmem_limit_bytes=LIMIT),
        cost_estimate=BRIEF,
    )(*plans, energy, vectors, *flat, *after)


def image_body(z, spans, *refs):
    refs = list(refs)
    plans = [refs.pop(0) for _ in range(z.env)]
    so_far = refs.pop(0)
    parts = [[(refs.pop(0), 0) for _ in range(z.rep)] for _ in range(z.env)]
    image, token, sums, sem = refs[-4:]
    token[...] = jnp.zeros_like(token)

    def take(slot, blocks):
        for v in range(z.batch):
            sums[v, slot] = so_far[v, slot]

    for_terms(z, plans, parts, spans, take)
    add_terms(z, plans, sums, parts, spans)
    for wait in (False, True):
        used = []

        def put(slot, blocks):
            for v in range(z.batch):
                copy = pltpu.make_async_copy(
                    sums.at[v, slot], image.at[v, slot], sem.at[len(used), v]
                )
                if wait:
                    copy.wait()
                else:
                    copy.start()
            used.append(slot)

        for_terms(z, plans, parts, spans, put)


def make_image(z, plans, so_far, image, parts, spans):
    flat = [ref for piece in parts for ref in piece]
    count = z.env * sum(span[1] for span in spans)
    return pl.pallas_call(
        functools.partial(image_body, z, spans),
        out_shape=[
            pltpu.HBM(image.shape, jnp.float32),
            jax.ShapeDtypeStruct((8, 128), jnp.float32),
        ],
        in_specs=[SMEM] * z.env + [VMEM] * (1 + len(flat)) + [HBM],
        out_specs=[HBM, VMEM],
        input_output_aliases={z.env + 1 + len(flat): 0},
        scratch_shapes=[
            pltpu.VMEM(image.shape, jnp.float32),
            pltpu.SemaphoreType.DMA((count, z.batch)),
        ],
        compiler_params=pltpu.CompilerParams(vmem_limit_bytes=LIMIT),
        cost_estimate=BRIEF,
    )(*plans, so_far, *flat, image)


def in_order(parts, places, count):
    total = 0.0
    for place in range(count):
        for part, at in zip(parts, places):
            total = total + jnp.where(at == place, part, 0.0)
    return total


def chips_body(z, count, plan, own, *refs):
    arrived, out = refs[:count], refs[-1]
    core, chip = plan[z.core], plan[z.chip]
    parts, places = [], []
    for e in range(z.env):
        for s in range(z.rep):
            ref = arrived[e * z.rep + s - 1] if e + s else own
            tail = ref[ref.shape[0] - TAIL :].astype(jnp.float32)
            parts.append(tail[0:1] + tail[1:2] + tail[2:3])
            at = lax.rem(chip + z.env - e, z.env) * z.rep + lax.rem(core + z.rep - s, z.rep)
            places.append(at)
    total = in_order(parts, places, z.env * z.rep)
    out[...] = jnp.broadcast_to(total, out.shape)


def chip_sums(z, plan, own, arrived, after):
    return pl.pallas_call(
        functools.partial(chips_body, z, len(arrived)),
        out_shape=jax.ShapeDtypeStruct((8, z.order), jnp.float32),
        in_specs=[SMEM] + [VMEM] * (1 + len(arrived)) + [ANY] * len(after),
        out_specs=VMEM,
        compiler_params=pltpu.CompilerParams(vmem_limit_bytes=SMALL),
        cost_estimate=BRIEF,
    )(plan, own, *arrived, *after)


def mean_body(z, count, scale, *refs):
    out = refs[-1]
    me = lax.axis_index("sector")
    parts = [ref[0:1] for ref in refs[:count]]
    total = parts[0]
    if count > 1:
        places = [lax.rem(me + z.sector - step, z.sector) for step in range(count)]
        total = in_order(parts, places, count)
    out[...] = total[:, : out.shape[1]] * scale


def mean_over_sectors(z, array, entries, after):
    held = [array]
    if z.sector <= 4:
        held += [shift(array, "sector", z.sector, step) for step in range(1, z.sector)]
    else:
        held = [total_over(array, "sector")]
    made = pl.pallas_call(
        functools.partial(mean_body, z, len(held), 1.0 / entries),
        out_shape=jax.ShapeDtypeStruct((1, z.batch), jnp.float32),
        in_specs=[VMEM] * len(held) + [ANY] * len(after),
        out_specs=VMEM,
        compiler_params=pltpu.CompilerParams(vmem_limit_bytes=SMALL),
        cost_estimate=BRIEF,
    )(*held, *after)
    return made.reshape(z.batch)


def shift(array, axis, size, step):
    return lax.ppermute(array, axis, [(i, (i + step) % size) for i in range(size)])


def shift_both(z, array, e, s):
    perm = []
    for x in range(z.env):
        for c in range(z.rep):
            perm.append((x * z.rep + c, (x + e) % z.env * z.rep + (c + s) % z.rep))
    return lax.ppermute(array, ("env", "rep"), perm)


def total_over(array, axis):
    size = lax.axis_size(axis)
    if size & (size - 1):
        return lax.psum(array, axis)
    step = 1
    while step < size:
        array = array + lax.ppermute(array, axis, [(i, i ^ step) for i in range(size)])
        step *= 2
    return array


def on_device(vectors, left_env, right_env, energy, partner):
    z = Sizes(vectors, left_env)
    each = z.sector // 4
    span = z.capacity

    def spans_of(g, low=0, high=span):
        return [((g * each + d) * span + low, high - low, low) for d in range(each)]

    chunks = {g: spans_of(g) for g in range(4)}
    cut = 2 * span // 3
    chunks[2], chunks[4] = spans_of(2, 0, cut), spans_of(2, cut, span)

    def around(array):
        return [array] + [shift(array, "rep", z.rep, s) for s in range(1, z.rep)]

    def across(arrays, g):
        steps = [g * each + d for d in range(each)]
        return [shift(a, "sector", z.sector, k) if k else a for a, k in zip(arrays, steps)]

    partners = [shift(partner, "env", z.env, e) for e in range(1, z.env)]
    vector_others = around(vectors)[1:]
    right_others = around(right_env)[1:]
    left = around(left_env)
    plan, own, right_own = load(z, partner, vectors, right_env)
    own = gate(own, partners)
    right = [right_own] + right_others
    near_rows = [own[0]] + vector_others
    vec = [near_rows]
    for e in range(1, z.env):
        vec.append([shift_both(z, own[s], e, s) for s in range(z.rep)])
    plans = [plan] + [plan_only(z, other) for other in partners]

    def near_products(g, after):
        return products(z, plan, right, [near_rows], [c[:2] for c in spans_of(g)], after)

    def far_products(g, after):
        return products(z, plan, right, vec[1:], [c[:2] for c in chunks[g]], after)

    near, far, parts = {}, {}, {}
    spans = [piece[:2] for g in (1, 3) for piece in chunks[g]]
    made = products(z, plan, right, [near_rows], spans)
    near[1], near[3] = across(made[:each], 1), across(made[each:], 3)
    made = near_products(2, (made[0], *left[1:]))
    near[2] = across(made, 2)

    def send_terms(g, so_far, own_sums, kept, after):
        made, folded = terms(
            z, plan, left, near[2 if g == 4 else g], far[g], vec, chunks[g], so_far,
            own_sums, kept, after
        )
        first = made[: z.rep]
        if own_sums is not None:
            first[1:] = [shift(first[s], "rep", z.rep, s) for s in range(1, z.rep)]
        parts[g] = [first]
        for e in range(1, z.env):
            parts[g].append([shift_both(z, made[e * z.rep + s], e, s) for s in range(z.rep)])
        return folded

    def arrived(g):
        return [part for piece in parts[g][1:] for part in piece]

    near[0] = near_products(0, made[:1])
    far1 = far_products(1, (near[0][0], *plans[1:]))
    far1 = gate(far1, [*near[1], *near[3]])
    far[1] = across(far1, 1)
    far[0] = far_products(0, far1[:1])
    dots = send_terms(0, None, None, (), ())
    far3 = far_products(3, (dots,))
    far2 = far_products(2, far3[:1])
    far4 = far_products(4, far2[:1])
    far3 = gate(far3, [far4[0], *near[2]])
    far[3] = across(far3, 3)
    far2 = gate([*far2, *far4], [far3[0], *far[1]])
    far[2], far[4] = across(far2[:each], 2), across(far2[each:], 2)
    dots = send_terms(1, dots, None, (), (far2[0], *arrived(0)))
    dots = send_terms(3, dots, None, (), arrived(1))
    own_block = vectors.astype(jnp.float32)
    own_sums = jnp.sum(energy[None, :, None, None] * own_block * own_block, axis=(1, 2, 3))
    dots = send_terms(2, dots, None, (), arrived(3))
    early = (0, 1, 3, 2)
    kept = [parts[g][0][1:] for g in early]
    dots = send_terms(4, dots, own_sums, kept, arrived(2)[:1])
    so_far, image = gather_terms(
        z,
        plans,
        energy,
        vectors,
        parts[4][0][1:],
        sum(piece[1] for piece in chunks[4]),
        [parts[g] for g in early],
        [chunks[g] for g in early],
        (dots,),
    )
    sums = chip_sums(z, plan, dots, parts[4][0][1:] + arrived(4), (so_far,))
    image, token = make_image(z, plans, so_far, image, parts[4], chunks[4])
    entries = z.slots * z.sector * z.order * z.order
    return (image, mean_over_sectors(z, sums, entries, (token,)))


def solution(mesh):
    return jax.shard_map(
        on_device,
        mesh=mesh,
        in_specs=(
            P(None, ("groups", "sector"), ("env", "rep"), None),
            P("env", ("groups", "sector"), "rep", None),
            P("env", ("groups", "sector"), "rep", None),
            P(("groups", "sector")),
            P("env", "groups"),
        ),
        out_specs=(P(None, ("groups", "sector"), ("env", "rep"), None), P("groups")),
        check_vma=False,
    )
```

```python
import functools

import jax
import jax.numpy as jnp
from jax import lax
from jax.experimental import pallas as pl
from jax.experimental.pallas import tpu as pltpu
from jax.sharding import PartitionSpec as P

ANY = pl.BlockSpec(memory_space=pl.ANY)
HBM = pl.BlockSpec(memory_space=pltpu.HBM)
SMEM = pl.BlockSpec(memory_space=pltpu.SMEM)
VMEM = pl.BlockSpec(memory_space=pltpu.VMEM)
LIMIT = 12 * 1024 * 1024
SMALL = 2 * 1024 * 1024
TAIL = 16
BRIEF = pl.CostEstimate(flops=0, bytes_accessed=0, transcendentals=0)


def aligned(index, size):
    return pl.multiple_of(index * size, size)


class Sizes:
    def __init__(self, vectors, left_env):
        self.env = lax.axis_size("env")
        self.rep = lax.axis_size("rep")
        self.sector = lax.axis_size("sector")
        self.batch, self.slots, self.own_rows, self.order = vectors.shape
        assert self.batch == self.rep and self.sector % 4 == 0
        self.half = left_env.shape[2]
        self.chip_rows = self.own_rows * self.rep
        self.capacity = 2 * ((self.slots + 2 * self.sector - 1) // (2 * self.sector))
        self.flat = self.sector * self.capacity
        self.full = self.flat == self.slots
        self.source, self.target, self.valid = 0, self.flat, 2 * self.flat
        self.core, self.chip = 3 * self.flat, 3 * self.flat + 1

    def when_valid(self, plan, flat, action):
        if self.full:
            action()
        else:
            pl.when(plan[self.valid + flat] == 1)(action)


def write_plan(z, partner, plan, count):
    if not z.full:

        def clear(i, carry):
            plan[i] = 0
            return carry

        lax.fori_loop(0, 3 * z.flat, clear, 0)
    for d in range(z.sector):
        count[d] = 0
    factor = -(-(1 << 16) // z.slots)
    assert all(i * factor >> 16 == i // z.slots for i in range(z.sector * z.slots))
    for j in range(z.slots):
        sector = partner[0, j]
        group = (sector * factor) >> 16
        slot = sector - group * z.slots
        distance = jnp.where(group == 0, 0, z.sector - group)
        rank = count[distance]
        count[distance] = rank + 1
        index = distance * z.capacity + rank
        plan[z.source + index] = slot
        plan[z.target + index] = j
        plan[z.valid + index] = 1
    plan[z.core] = lax.axis_index("rep")
    plan[z.chip] = lax.axis_index("env")


def split_copy(source, target, slots, sem):
    step = slots // 4 if slots % 4 == 0 else slots
    copies = []
    for i in range(slots // step):
        part = pl.ds(i * step, step)
        copies.append(pltpu.make_async_copy(source.at[part], target.at[part], sem.at[i]))
    return copies


def load_body(z, partner, vectors, right, plan, *refs):
    rows, block, count, sem = refs[: z.rep], refs[z.rep], refs[-2], refs[-1]
    core = lax.axis_index("rep")
    copies = []
    for s, ref in enumerate(rows):
        mine = vectors.at[lax.rem(core + s, z.rep)]
        copies += split_copy(mine, ref, z.slots, sem.at[s])
    copies += split_copy(right.at[0], block.at[0], z.slots, sem.at[z.rep])
    for copy in copies:
        copy.start()
    write_plan(z, partner, plan, count)
    for copy in copies:
        copy.wait()


def load(z, partner, vectors, right_env):
    row = jax.ShapeDtypeStruct(vectors.shape[1:], jnp.bfloat16)
    plan, *made = pl.pallas_call(
        functools.partial(load_body, z),
        out_shape=[jax.ShapeDtypeStruct((3 * z.flat + 2,), jnp.int32)]
        + [row] * z.rep
        + [jax.ShapeDtypeStruct(right_env.shape, jnp.bfloat16)],
        in_specs=[SMEM, HBM, HBM],
        out_specs=[SMEM] + [VMEM] * (z.rep + 1),
        scratch_shapes=[
            pltpu.SMEM((z.sector,), jnp.int32),
            pltpu.SemaphoreType.DMA((z.rep + 1, 4)),
        ],
        compiler_params=pltpu.CompilerParams(vmem_limit_bytes=LIMIT),
        cost_estimate=BRIEF,
    )(
        partner,
        pltpu.with_memory_space_constraint(vectors, pltpu.HBM),
        pltpu.with_memory_space_constraint(right_env, pltpu.HBM),
    )
    return plan, made[: z.rep], made[z.rep]


def plan_only(z, partner):
    return pl.pallas_call(
        functools.partial(write_plan, z),
        out_shape=jax.ShapeDtypeStruct((3 * z.flat + 2,), jnp.int32),
        in_specs=[SMEM],
        out_specs=SMEM,
        scratch_shapes=[pltpu.SMEM((z.sector,), jnp.int32)],
        compiler_params=pltpu.CompilerParams(vmem_limit_bytes=SMALL),
        cost_estimate=BRIEF,
    )(partner)


def gate(arrays, after):
    def body(*refs):
        pass

    return pl.pallas_call(
        body,
        out_shape=[jax.ShapeDtypeStruct(a.shape, a.dtype) for a in arrays],
        in_specs=[ANY] * (len(arrays) + len(after)),
        out_specs=[ANY] * len(arrays),
        input_output_aliases={i: i for i in range(len(arrays))},
        compiler_params=pltpu.CompilerParams(vmem_limit_bytes=SMALL),
        cost_estimate=BRIEF,
    )(*arrays, *after)


def pick(z, core, place, candidates):
    chosen = candidates[0]
    for s in range(1, z.rep):
        chosen = jnp.where(lax.rem(core + z.rep - s, z.rep) == place, candidates[s], chosen)
    return chosen


def line(ref, core, slot):
    return ref[core, slot] if len(ref.shape) == 4 else ref[slot]


def products_body(z, pieces, spans, *refs):
    refs = list(refs)
    plan = refs.pop(0)
    right = [refs.pop(0) for _ in range(z.rep)]
    rows = [[refs.pop(0) for _ in range(z.rep)] for _ in range(pieces)]
    outs = refs[-len(spans) :]
    core = plan[z.core]
    for (first, count), out in zip(spans, outs):
        for i in range(count):
            slot = plan[z.source + first + i]
            halves = [ref[0, slot] for ref in right]
            parts = [[line(ref, core, slot) for ref in piece] for piece in rows]
            block = jnp.concatenate([pick(z, core, k, halves) for k in range(z.rep)], axis=0)
            lines = jnp.concatenate(
                [pick(z, core, k, part) for part in parts for k in range(z.rep)], axis=0
            )
            out[i] = lax.dot_general(
                lines, block, (((1,), (1,)), ((), ())), preferred_element_type=jnp.float32
            ).astype(jnp.bfloat16)


def products(z, plan, right, rows, spans, after=()):
    pieces = len(rows)
    flat = [ref for piece in rows for ref in piece]
    height = pieces * z.chip_rows
    return pl.pallas_call(
        functools.partial(products_body, z, pieces, spans),
        out_shape=[
            jax.ShapeDtypeStruct((count, height, z.order), jnp.bfloat16) for _, count in spans
        ],
        in_specs=[SMEM] + [VMEM] * (len(right) + len(flat)) + [ANY] * len(after),
        out_specs=[VMEM] * len(spans),
        compiler_params=pltpu.CompilerParams(vmem_limit_bytes=LIMIT),
        cost_estimate=BRIEF,
    )(plan, *right, *flat, *after)


def terms_body(z, spans, chained, last, kept, *refs):
    refs = list(refs)
    plan = refs.pop(0)
    left = [refs.pop(0) for _ in range(z.rep)]
    near = [refs.pop(0) for _ in spans]
    far = [refs.pop(0) for _ in spans]
    vec = [[refs.pop(0) for _ in range(z.rep)] for _ in range(z.env)]
    so_far = refs.pop(0) if chained else None
    own_sums = refs.pop(0) if last else None
    kept = [[refs.pop(0) for _ in range(z.rep - 1)] for _ in range(kept)]
    pbuf, tbuf = refs[-2:]
    dots = refs[-3]
    outs = refs[-3 - z.env * z.rep : -3]
    core, chip = plan[z.core], plan[z.chip]
    total = so_far[...] if chained else jnp.zeros((8, z.order), jnp.float32)
    n = 0
    for d, (first, count, skip) in enumerate(spans):
        for i in range(count):
            slot = plan[z.target + first + i]
            for e in range(z.env):
                place = lax.rem(chip + z.env - e, z.env)
                if e == 0:
                    lines = near[d][skip + i]
                else:
                    lines = far[d][i, (e - 1) * z.chip_rows : e * z.chip_rows]
                pbuf[n, pl.ds(aligned(place, z.chip_rows), z.chip_rows)] = lines
            halves = [ref[0, slot] for ref in left]
            block = jnp.concatenate([pick(z, core, k, halves) for k in range(z.rep)], axis=0)
            tbuf[n] = jnp.dot(block, pbuf[n], preferred_element_type=jnp.float32).astype(
                jnp.bfloat16
            )
            folded = jnp.zeros(total.shape, jnp.float32)
            for e in range(z.env):
                for s in range(z.rep):
                    place = lax.rem(chip + e, z.env) * z.rep + lax.rem(core + s, z.rep)
                    term = tbuf[n, pl.ds(aligned(place, z.own_rows), z.own_rows)]
                    if last and e + s:
                        outs[e * z.rep + s][n * z.own_rows : (n + 1) * z.own_rows] = term
                    else:
                        outs[e * z.rep + s][n] = term
                    lines = line(vec[(z.env - e) % z.env][(z.rep - s) % z.rep], core, slot)
                    both = lines.astype(jnp.float32) * term.astype(jnp.float32)
                    folded += jnp.sum(both.reshape(-1, *total.shape), axis=0)
            if not z.full:
                folded = jnp.where(plan[z.valid + first + i] == 1, folded, 0.0)
            total += folded
            n += 1
    if not last:
        dots[...] = total
        return
    row = lax.broadcasted_iota(jnp.int32, dots.shape, 0)
    column = lax.broadcasted_iota(jnp.int32, dots.shape, 1)
    value = jnp.where(column == core, jnp.sum(total), 0.0)
    for v in range(z.batch):
        value += jnp.where(column == v, own_sums[v], 0.0)
    split = jnp.zeros(dots.shape, jnp.float32)
    for k in range(3):
        piece = value.astype(jnp.bfloat16).astype(jnp.float32)
        split = jnp.where(row == k, piece, split)
        value = value - piece
    split = split.astype(jnp.bfloat16)
    dots[...] = split
    at = n * z.own_rows
    for blocks in kept:
        for s, block in enumerate(blocks):
            for i in range(block.shape[0]):
                outs[1 + s][at + i * z.own_rows : at + (i + 1) * z.own_rows] = block[i]
        at += blocks[0].shape[0] * z.own_rows
    for out in outs[1:]:
        out[out.shape[0] - TAIL :] = split


def terms(z, plan, left, near, far, vec, spans, so_far=None, own_sums=None, kept=(), after=()):
    count = sum(span[1] for span in spans)
    flat = [ref for piece in vec for ref in piece]
    shapes = [(count, z.own_rows, z.order)] * (z.env * z.rep)
    whole = (count, z.order, z.order)
    last = own_sums is not None
    sums = jax.ShapeDtypeStruct((8, z.order), jnp.float32)
    if last:
        shapes[1:] = [(count * z.own_rows + TAIL, z.order)] * (z.env * z.rep - 1)
        more = sum(blocks[0].shape[0] for blocks in kept)
        shapes[1 : z.rep] = [((count + more) * z.own_rows + TAIL, z.order)] * (z.rep - 1)
        sums = jax.ShapeDtypeStruct((TAIL, z.order), jnp.bfloat16)
    extra = [] if so_far is None else [so_far]
    specs = [VMEM] * len(extra)
    if last:
        extra.append(own_sums)
        specs.append(SMEM)
    extra += [block for blocks in kept for block in blocks]
    specs += [VMEM] * (len(extra) - len(specs))
    *made, dots = pl.pallas_call(
        functools.partial(terms_body, z, spans, so_far is not None, last, len(kept)),
        out_shape=[jax.ShapeDtypeStruct(shape, jnp.bfloat16) for shape in shapes] + [sums],
        in_specs=[SMEM]
        + [VMEM] * (len(left) + len(near) + len(far) + len(flat))
        + specs
        + [ANY] * len(after),
        out_specs=[VMEM] * (len(shapes) + 1),
        scratch_shapes=[pltpu.VMEM(whole, jnp.bfloat16), pltpu.VMEM(whole, jnp.bfloat16)],
        compiler_params=pltpu.CompilerParams(vmem_limit_bytes=LIMIT),
        cost_estimate=BRIEF,
    )(plan, *left, *near, *far, *flat, *extra, *after)
    return made, dots


def for_terms(z, plans, parts, spans, action):
    n = 0
    for first, count, _ in spans:
        for i in range(count):
            for e, plan in enumerate(plans):

                def act():
                    blocks = []
                    for ref, skip in parts[e]:
                        if len(ref.shape) == 3:
                            blocks.append(lambda ref=ref: ref[n])
                        else:
                            rows = slice((skip + n) * z.own_rows, (skip + n + 1) * z.own_rows)
                            blocks.append(lambda ref=ref, rows=rows: ref[rows])
                    action(plan[z.target + first + i], blocks)

                z.when_valid(plan, first + i, act)
            n += 1


def add_terms(z, plans, image, parts, spans):
    core = plans[0][z.core]

    def add(slot, blocks):
        for s, block in enumerate(blocks):
            v = lax.rem(core + z.rep - s, z.rep)
            image[v, slot] += block().astype(jnp.float32)

    for_terms(z, plans, parts, spans, add)


def gather_body(z, chunks, skip, *refs):
    refs = list(refs)
    plans = [refs.pop(0) for _ in range(z.env)]
    energy, vectors = refs.pop(0), refs.pop(0)
    so_far, image, sem = refs[-3:]

    def start(j, carry):
        for v in range(z.batch):
            so_far[v, j] = energy[j] * vectors[v, j].astype(jnp.float32)
        return carry

    lax.fori_loop(0, z.slots, start, 0, unroll=2)
    joined = [refs.pop(0) for _ in range(z.rep - 1)]
    for spans in chunks:
        parts = [[(refs.pop(0), 0)] + [(ref, skip) for ref in joined]]
        for _ in range(1, z.env):
            parts.append([(refs.pop(0), 0) for _ in range(z.rep)])
        add_terms(z, plans, so_far, parts, spans)
        skip += sum(span[1] for span in spans)
    copies = []
    for v in range(z.batch):
        copies += split_copy(so_far.at[v], image.at[v], z.slots, sem.at[v])
    for copy in copies:
        copy.start()
    for copy in copies:
        copy.wait()


def gather_terms(z, plans, energy, vectors, joined, skip, parts, chunks, after=()):
    flat = [*joined]
    for chunk in parts:
        flat += [chunk[0][0]] + [ref for piece in chunk[1:] for ref in piece]
    shape = jax.ShapeDtypeStruct(vectors.shape, jnp.float32)
    return pl.pallas_call(
        functools.partial(gather_body, z, chunks, skip),
        out_shape=[shape, pltpu.HBM(vectors.shape, jnp.float32)],
        in_specs=[SMEM] * (z.env + 1) + [VMEM] * (1 + len(flat)) + [ANY] * len(after),
        out_specs=[VMEM, HBM],
        scratch_shapes=[pltpu.SemaphoreType.DMA((z.batch, 4))],
        compiler_params=pltpu.CompilerParams(vmem_limit_bytes=LIMIT),
        cost_estimate=BRIEF,
    )(*plans, energy, vectors, *flat, *after)


def image_body(z, spans, *refs):
    refs = list(refs)
    plans = [refs.pop(0) for _ in range(z.env)]
    so_far = refs.pop(0)
    parts = [[(refs.pop(0), 0) for _ in range(z.rep)] for _ in range(z.env)]
    image, token, sums, sem = refs[-4:]
    token[...] = jnp.zeros_like(token)

    def take(slot, blocks):
        for v in range(z.batch):
            sums[v, slot] = so_far[v, slot]

    for_terms(z, plans, parts, spans, take)
    add_terms(z, plans, sums, parts, spans)
    for wait in (False, True):
        used = []

        def put(slot, blocks):
            for v in range(z.batch):
                copy = pltpu.make_async_copy(
                    sums.at[v, slot], image.at[v, slot], sem.at[len(used), v]
                )
                if wait:
                    copy.wait()
                else:
                    copy.start()
            used.append(slot)

        for_terms(z, plans, parts, spans, put)


def make_image(z, plans, so_far, image, parts, spans):
    flat = [ref for piece in parts for ref in piece]
    count = z.env * sum(span[1] for span in spans)
    return pl.pallas_call(
        functools.partial(image_body, z, spans),
        out_shape=[
            pltpu.HBM(image.shape, jnp.float32),
            jax.ShapeDtypeStruct((8, 128), jnp.float32),
        ],
        in_specs=[SMEM] * z.env + [VMEM] * (1 + len(flat)) + [HBM],
        out_specs=[HBM, VMEM],
        input_output_aliases={z.env + 1 + len(flat): 0},
        scratch_shapes=[
            pltpu.VMEM(image.shape, jnp.float32),
            pltpu.SemaphoreType.DMA((count, z.batch)),
        ],
        compiler_params=pltpu.CompilerParams(vmem_limit_bytes=LIMIT),
        cost_estimate=BRIEF,
    )(*plans, so_far, *flat, image)


def in_order(parts, places, count):
    total = 0.0
    for place in range(count):
        for part, at in zip(parts, places):
            total = total + jnp.where(at == place, part, 0.0)
    return total


def chips_body(z, count, plan, own, *refs):
    arrived, out = refs[:count], refs[-1]
    core, chip = plan[z.core], plan[z.chip]
    parts, places = [], []
    for e in range(z.env):
        for s in range(z.rep):
            ref = arrived[e * z.rep + s - 1] if e + s else own
            tail = ref[ref.shape[0] - TAIL :].astype(jnp.float32)
            parts.append(tail[0:1] + tail[1:2] + tail[2:3])
            at = lax.rem(chip + z.env - e, z.env) * z.rep + lax.rem(core + z.rep - s, z.rep)
            places.append(at)
    total = in_order(parts, places, z.env * z.rep)
    out[...] = jnp.broadcast_to(total, out.shape)


def chip_sums(z, plan, own, arrived, after):
    return pl.pallas_call(
        functools.partial(chips_body, z, len(arrived)),
        out_shape=jax.ShapeDtypeStruct((8, z.order), jnp.float32),
        in_specs=[SMEM] + [VMEM] * (1 + len(arrived)) + [ANY] * len(after),
        out_specs=VMEM,
        compiler_params=pltpu.CompilerParams(vmem_limit_bytes=SMALL),
        cost_estimate=BRIEF,
    )(plan, own, *arrived, *after)


def mean_body(z, count, scale, *refs):
    out = refs[-1]
    me = lax.axis_index("sector")
    parts = [ref[0:1] for ref in refs[:count]]
    total = parts[0]
    if count > 1:
        places = [lax.rem(me + z.sector - step, z.sector) for step in range(count)]
        total = in_order(parts, places, count)
    out[...] = total[:, : out.shape[1]] * scale


def mean_over_sectors(z, array, entries, after):
    held = [array]
    if z.sector <= 4:
        held += [shift(array, "sector", z.sector, step) for step in range(1, z.sector)]
    else:
        held = [total_over(array, "sector")]
    made = pl.pallas_call(
        functools.partial(mean_body, z, len(held), 1.0 / entries),
        out_shape=jax.ShapeDtypeStruct((1, z.batch), jnp.float32),
        in_specs=[VMEM] * len(held) + [ANY] * len(after),
        out_specs=VMEM,
        compiler_params=pltpu.CompilerParams(vmem_limit_bytes=SMALL),
        cost_estimate=BRIEF,
    )(*held, *after)
    return made.reshape(z.batch)


def shift(array, axis, size, step):
    return lax.ppermute(array, axis, [(i, (i + step) % size) for i in range(size)])


def shift_both(z, array, e, s):
    perm = []
    for x in range(z.env):
        for c in range(z.rep):
            perm.append((x * z.rep + c, (x + e) % z.env * z.rep + (c + s) % z.rep))
    return lax.ppermute(array, ("env", "rep"), perm)


def total_over(array, axis):
    size = lax.axis_size(axis)
    if size & (size - 1):
        return lax.psum(array, axis)
    step = 1
    while step < size:
        array = array + lax.ppermute(array, axis, [(i, i ^ step) for i in range(size)])
        step *= 2
    return array


def on_device(vectors, left_env, right_env, energy, partner):
    z = Sizes(vectors, left_env)
    each = z.sector // 4
    span = z.capacity

    def spans_of(g, low=0, high=span):
        return [((g * each + d) * span + low, high - low, low) for d in range(each)]

    chunks = {g: spans_of(g) for g in range(4)}
    cut = 2 * span // 3
    chunks[2], chunks[4] = spans_of(2, 0, cut), spans_of(2, cut, span)

    def around(array):
        return [array] + [shift(array, "rep", z.rep, s) for s in range(1, z.rep)]

    def across(arrays, g):
        steps = [g * each + d for d in range(each)]
        return [shift(a, "sector", z.sector, k) if k else a for a, k in zip(arrays, steps)]

    partners = [shift(partner, "env", z.env, e) for e in range(1, z.env)]
    vector_others = around(vectors)[1:]
    right_others = around(right_env)[1:]
    left = around(left_env)
    plan, own, right_own = load(z, partner, vectors, right_env)
    own = gate(own, partners)
    right = [right_own] + right_others
    near_rows = [own[0]] + vector_others
    vec = [near_rows]
    for e in range(1, z.env):
        vec.append([shift_both(z, own[s], e, s) for s in range(z.rep)])
    plans = [plan] + [plan_only(z, other) for other in partners]

    def near_products(g, after):
        return products(z, plan, right, [near_rows], [c[:2] for c in spans_of(g)], after)

    def far_products(g, after):
        return products(z, plan, right, vec[1:], [c[:2] for c in chunks[g]], after)

    near, far, parts = {}, {}, {}
    spans = [piece[:2] for g in (1, 3) for piece in chunks[g]]
    made = products(z, plan, right, [near_rows], spans)
    near[1], near[3] = across(made[:each], 1), across(made[each:], 3)
    made = near_products(2, (made[0], *left[1:]))
    near[2] = across(made, 2)

    def send_terms(g, so_far, own_sums, kept, after):
        made, folded = terms(
            z, plan, left, near[2 if g == 4 else g], far[g], vec, chunks[g], so_far,
            own_sums, kept, after
        )
        first = made[: z.rep]
        if own_sums is not None:
            first[1:] = [shift(first[s], "rep", z.rep, s) for s in range(1, z.rep)]
        parts[g] = [first]
        for e in range(1, z.env):
            parts[g].append([shift_both(z, made[e * z.rep + s], e, s) for s in range(z.rep)])
        return folded

    def arrived(g):
        return [part for piece in parts[g][1:] for part in piece]

    near[0] = near_products(0, made[:1])
    far1 = far_products(1, (near[0][0], *plans[1:]))
    far1 = gate(far1, [*near[1], *near[3]])
    far[1] = across(far1, 1)
    far[0] = far_products(0, far1[:1])
    dots = send_terms(0, None, None, (), ())
    far3 = far_products(3, (dots,))
    far2 = far_products(2, far3[:1])
    far4 = far_products(4, far2[:1])
    far3 = gate(far3, [far4[0], *near[2], *arrived(0)[:1]])
    far[3] = across(far3, 3)
    far2 = gate([*far2, *far4], [far3[0], *far[1]])
    far[2], far[4] = across(far2[:each], 2), across(far2[each:], 2)
    dots = send_terms(1, dots, None, (), (far2[0], *arrived(0)[1:]))
    dots = send_terms(3, dots, None, (), arrived(1)[:1])
    own_block = vectors.astype(jnp.float32)
    own_sums = jnp.sum(energy[None, :, None, None] * own_block * own_block, axis=(1, 2, 3))
    dots = send_terms(2, dots, None, (), arrived(1)[1:] + arrived(3)[:1])
    early = (0, 1, 3, 2)
    kept = [parts[g][0][1:] for g in early]
    dots = send_terms(4, dots, own_sums, kept, arrived(3)[1:] + arrived(2)[:1])
    so_far, image = gather_terms(
        z,
        plans,
        energy,
        vectors,
        parts[4][0][1:],
        sum(piece[1] for piece in chunks[4]),
        [parts[g] for g in early],
        [chunks[g] for g in early],
        (dots,),
    )
    sums = chip_sums(z, plan, dots, parts[4][0][1:] + arrived(4), (so_far,))
    image, token = make_image(z, plans, so_far, image, parts[4], chunks[4])
    entries = z.slots * z.sector * z.order * z.order
    return (image, mean_over_sectors(z, sums, entries, (token,)))


def solution(mesh):
    return jax.shard_map(
        on_device,
        mesh=mesh,
        in_specs=(
            P(None, ("groups", "sector"), ("env", "rep"), None),
            P("env", ("groups", "sector"), "rep", None),
            P("env", ("groups", "sector"), "rep", None),
            P(("groups", "sector")),
            P("env", "groups"),
        ),
        out_specs=(P(None, ("groups", "sector"), ("env", "rep"), None), P("groups")),
        check_vma=False,
    )
```

```python
import functools

import jax
import jax.numpy as jnp
from jax import lax
from jax.experimental import pallas as pl
from jax.experimental.pallas import tpu as pltpu
from jax.sharding import PartitionSpec as P

ANY = pl.BlockSpec(memory_space=pl.ANY)
HBM = pl.BlockSpec(memory_space=pltpu.HBM)
SMEM = pl.BlockSpec(memory_space=pltpu.SMEM)
VMEM = pl.BlockSpec(memory_space=pltpu.VMEM)
LIMIT = 12 * 1024 * 1024
SMALL = 2 * 1024 * 1024
TAIL = 16
BRIEF = pl.CostEstimate(flops=0, bytes_accessed=0, transcendentals=0)


def aligned(index, size):
    return pl.multiple_of(index * size, size)


class Sizes:
    def __init__(self, vectors, left_env):
        self.env = lax.axis_size("env")
        self.rep = lax.axis_size("rep")
        self.sector = lax.axis_size("sector")
        self.batch, self.slots, self.own_rows, self.order = vectors.shape
        assert self.batch == self.rep and self.sector % 4 == 0
        self.half = left_env.shape[2]
        self.chip_rows = self.own_rows * self.rep
        self.capacity = 2 * ((self.slots + 2 * self.sector - 1) // (2 * self.sector))
        self.flat = self.sector * self.capacity
        self.full = self.flat == self.slots
        self.source, self.target, self.valid = 0, self.flat, 2 * self.flat
        self.core, self.chip = 3 * self.flat, 3 * self.flat + 1

    def when_valid(self, plan, flat, action):
        if self.full:
            action()
        else:
            pl.when(plan[self.valid + flat] == 1)(action)


def write_plan(z, partner, plan, count):
    if not z.full:

        def clear(i, carry):
            plan[i] = 0
            return carry

        lax.fori_loop(0, 3 * z.flat, clear, 0)
    for d in range(z.sector):
        count[d] = 0
    factor = -(-(1 << 16) // z.slots)
    assert all(i * factor >> 16 == i // z.slots for i in range(z.sector * z.slots))
    for j in range(z.slots):
        sector = partner[0, j]
        group = (sector * factor) >> 16
        slot = sector - group * z.slots
        distance = jnp.where(group == 0, 0, z.sector - group)
        rank = count[distance]
        count[distance] = rank + 1
        index = distance * z.capacity + rank
        plan[z.source + index] = slot
        plan[z.target + index] = j
        plan[z.valid + index] = 1
    plan[z.core] = lax.axis_index("rep")
    plan[z.chip] = lax.axis_index("env")


def split_copy(source, target, slots, sem):
    step = slots // 4 if slots % 4 == 0 else slots
    copies = []
    for i in range(slots // step):
        part = pl.ds(i * step, step)
        copies.append(pltpu.make_async_copy(source.at[part], target.at[part], sem.at[i]))
    return copies


def load_body(z, partner, lane, vectors, right, plan, to_send, *refs):
    rows, block, count, sem = refs[: z.rep], refs[z.rep], refs[-2], refs[-1]
    core = lax.axis_index("rep")
    copies = []
    for s, ref in enumerate(rows):
        mine = vectors.at[lax.rem(core + s, z.rep)]
        copies += split_copy(mine, ref, z.slots, sem.at[s])
    copies += split_copy(right.at[0], block.at[0], z.slots, sem.at[z.rep])
    for copy in copies:
        copy.start()
    write_plan(z, partner, plan, count)
    to_send[...] = lane[...]
    for copy in copies:
        copy.wait()


def load(z, partner, vectors, right_env):
    row = jax.ShapeDtypeStruct(vectors.shape[1:], jnp.bfloat16)
    plan, to_send, *made = pl.pallas_call(
        functools.partial(load_body, z),
        out_shape=[
            jax.ShapeDtypeStruct((3 * z.flat + 2,), jnp.int32),
            jax.ShapeDtypeStruct(partner.shape, jnp.int32),
        ]
        + [row] * z.rep
        + [jax.ShapeDtypeStruct(right_env.shape, jnp.bfloat16)],
        in_specs=[SMEM, VMEM, HBM, HBM],
        out_specs=[SMEM] + [VMEM] * (z.rep + 2),
        scratch_shapes=[
            pltpu.SMEM((z.sector,), jnp.int32),
            pltpu.SemaphoreType.DMA((z.rep + 1, 4)),
        ],
        compiler_params=pltpu.CompilerParams(vmem_limit_bytes=LIMIT),
        cost_estimate=BRIEF,
    )(
        partner,
        partner,
        pltpu.with_memory_space_constraint(vectors, pltpu.HBM),
        pltpu.with_memory_space_constraint(right_env, pltpu.HBM),
    )
    return plan, to_send, made[: z.rep], made[z.rep]


def plan_only(z, partner):
    return pl.pallas_call(
        functools.partial(write_plan, z),
        out_shape=jax.ShapeDtypeStruct((3 * z.flat + 2,), jnp.int32),
        in_specs=[SMEM],
        out_specs=SMEM,
        scratch_shapes=[pltpu.SMEM((z.sector,), jnp.int32)],
        compiler_params=pltpu.CompilerParams(vmem_limit_bytes=SMALL),
        cost_estimate=BRIEF,
    )(partner)


def gate(arrays, after):
    def body(*refs):
        pass

    return pl.pallas_call(
        body,
        out_shape=[jax.ShapeDtypeStruct(a.shape, a.dtype) for a in arrays],
        in_specs=[ANY] * (len(arrays) + len(after)),
        out_specs=[ANY] * len(arrays),
        input_output_aliases={i: i for i in range(len(arrays))},
        compiler_params=pltpu.CompilerParams(vmem_limit_bytes=SMALL),
        cost_estimate=BRIEF,
    )(*arrays, *after)


def pick(z, core, place, candidates):
    chosen = candidates[0]
    for s in range(1, z.rep):
        chosen = jnp.where(lax.rem(core + z.rep - s, z.rep) == place, candidates[s], chosen)
    return chosen


def line(ref, core, slot):
    return ref[core, slot] if len(ref.shape) == 4 else ref[slot]


def products_body(z, pieces, spans, *refs):
    refs = list(refs)
    plan = refs.pop(0)
    right = [refs.pop(0) for _ in range(z.rep)]
    rows = [[refs.pop(0) for _ in range(z.rep)] for _ in range(pieces)]
    outs = refs[-len(spans) :]
    core = plan[z.core]
    for (first, count), out in zip(spans, outs):
        for i in range(count):
            slot = plan[z.source + first + i]
            halves = [ref[0, slot] for ref in right]
            parts = [[line(ref, core, slot) for ref in piece] for piece in rows]
            block = jnp.concatenate([pick(z, core, k, halves) for k in range(z.rep)], axis=0)
            lines = jnp.concatenate(
                [pick(z, core, k, part) for part in parts for k in range(z.rep)], axis=0
            )
            out[i] = lax.dot_general(
                lines, block, (((1,), (1,)), ((), ())), preferred_element_type=jnp.float32
            ).astype(jnp.bfloat16)


def products(z, plan, right, rows, spans, after=()):
    pieces = len(rows)
    flat = [ref for piece in rows for ref in piece]
    height = pieces * z.chip_rows
    return pl.pallas_call(
        functools.partial(products_body, z, pieces, spans),
        out_shape=[
            jax.ShapeDtypeStruct((count, height, z.order), jnp.bfloat16) for _, count in spans
        ],
        in_specs=[SMEM] + [VMEM] * (len(right) + len(flat)) + [ANY] * len(after),
        out_specs=[VMEM] * len(spans),
        compiler_params=pltpu.CompilerParams(vmem_limit_bytes=LIMIT),
        cost_estimate=BRIEF,
    )(plan, *right, *flat, *after)


def terms_body(z, spans, chained, last, kept, *refs):
    refs = list(refs)
    plan = refs.pop(0)
    left = [refs.pop(0) for _ in range(z.rep)]
    near = [refs.pop(0) for _ in spans]
    far = [refs.pop(0) for _ in spans]
    vec = [[refs.pop(0) for _ in range(z.rep)] for _ in range(z.env)]
    so_far = refs.pop(0) if chained else None
    own_sums = refs.pop(0) if last else None
    kept = [[refs.pop(0) for _ in range(z.rep - 1)] for _ in range(kept)]
    pbuf, tbuf = refs[-2:]
    dots = refs[-3]
    outs = refs[-3 - z.env * z.rep : -3]
    core, chip = plan[z.core], plan[z.chip]
    total = so_far[...] if chained else jnp.zeros((8, z.order), jnp.float32)
    n = 0
    for d, (first, count) in enumerate(spans):
        for i in range(count):
            slot = plan[z.target + first + i]
            for e in range(z.env):
                place = lax.rem(chip + z.env - e, z.env)
                if e == 0:
                    lines = near[d][i]
                else:
                    lines = far[d][i, (e - 1) * z.chip_rows : e * z.chip_rows]
                pbuf[n, pl.ds(aligned(place, z.chip_rows), z.chip_rows)] = lines
            halves = [ref[0, slot] for ref in left]
            block = jnp.concatenate([pick(z, core, k, halves) for k in range(z.rep)], axis=0)
            tbuf[n] = jnp.dot(block, pbuf[n], preferred_element_type=jnp.float32).astype(
                jnp.bfloat16
            )
            folded = jnp.zeros(total.shape, jnp.float32)
            for e in range(z.env):
                for s in range(z.rep):
                    place = lax.rem(chip + e, z.env) * z.rep + lax.rem(core + s, z.rep)
                    term = tbuf[n, pl.ds(aligned(place, z.own_rows), z.own_rows)]
                    if last and e + s:
                        outs[e * z.rep + s][n * z.own_rows : (n + 1) * z.own_rows] = term
                    else:
                        outs[e * z.rep + s][n] = term
                    lines = line(vec[(z.env - e) % z.env][(z.rep - s) % z.rep], core, slot)
                    both = lines.astype(jnp.float32) * term.astype(jnp.float32)
                    folded += jnp.sum(both.reshape(-1, *total.shape), axis=0)
            if not z.full:
                folded = jnp.where(plan[z.valid + first + i] == 1, folded, 0.0)
            total += folded
            n += 1
    if not last:
        dots[...] = total
        return
    row = lax.broadcasted_iota(jnp.int32, dots.shape, 0)
    column = lax.broadcasted_iota(jnp.int32, dots.shape, 1)
    value = jnp.where(column == core, jnp.sum(total), 0.0)
    for v in range(z.batch):
        value += jnp.where(column == v, own_sums[v], 0.0)
    split = jnp.zeros(dots.shape, jnp.float32)
    for k in range(3):
        piece = value.astype(jnp.bfloat16).astype(jnp.float32)
        split = jnp.where(row == k, piece, split)
        value = value - piece
    split = split.astype(jnp.bfloat16)
    dots[...] = split
    at = n * z.own_rows
    for blocks in kept:
        for s, block in enumerate(blocks):
            for i in range(block.shape[0]):
                outs[1 + s][at + i * z.own_rows : at + (i + 1) * z.own_rows] = block[i]
        at += blocks[0].shape[0] * z.own_rows
    for out in outs[1:]:
        out[out.shape[0] - TAIL :] = split


def terms(z, plan, left, near, far, vec, spans, so_far=None, own_sums=None, kept=(), after=()):
    count = sum(span[1] for span in spans)
    flat = [ref for piece in vec for ref in piece]
    shapes = [(count, z.own_rows, z.order)] * (z.env * z.rep)
    whole = (count, z.order, z.order)
    last = own_sums is not None
    sums = jax.ShapeDtypeStruct((8, z.order), jnp.float32)
    if last:
        shapes[1:] = [(count * z.own_rows + TAIL, z.order)] * (z.env * z.rep - 1)
        more = sum(blocks[0].shape[0] for blocks in kept)
        shapes[1 : z.rep] = [((count + more) * z.own_rows + TAIL, z.order)] * (z.rep - 1)
        sums = jax.ShapeDtypeStruct((TAIL, z.order), jnp.bfloat16)
    extra = [] if so_far is None else [so_far]
    specs = [VMEM] * len(extra)
    if last:
        extra.append(own_sums)
        specs.append(SMEM)
    extra += [block for blocks in kept for block in blocks]
    specs += [VMEM] * (len(extra) - len(specs))
    *made, dots = pl.pallas_call(
        functools.partial(terms_body, z, spans, so_far is not None, last, len(kept)),
        out_shape=[jax.ShapeDtypeStruct(shape, jnp.bfloat16) for shape in shapes] + [sums],
        in_specs=[SMEM]
        + [VMEM] * (len(left) + len(near) + len(far) + len(flat))
        + specs
        + [ANY] * len(after),
        out_specs=[VMEM] * (len(shapes) + 1),
        scratch_shapes=[pltpu.VMEM(whole, jnp.bfloat16), pltpu.VMEM(whole, jnp.bfloat16)],
        compiler_params=pltpu.CompilerParams(vmem_limit_bytes=LIMIT),
        cost_estimate=BRIEF,
    )(plan, *left, *near, *far, *flat, *extra, *after)
    return made, dots


def for_terms(z, plans, parts, spans, action):
    n = 0
    for first, count in spans:
        for i in range(count):
            for e, plan in enumerate(plans):

                def act():
                    blocks = []
                    for ref, skip in parts[e]:
                        if len(ref.shape) == 3:
                            blocks.append(lambda ref=ref: ref[n])
                        else:
                            rows = slice((skip + n) * z.own_rows, (skip + n + 1) * z.own_rows)
                            blocks.append(lambda ref=ref, rows=rows: ref[rows])
                    action(plan[z.target + first + i], blocks)

                z.when_valid(plan, first + i, act)
            n += 1


def add_terms(z, plans, image, parts, spans):
    core = plans[0][z.core]

    def add(slot, blocks):
        for s, block in enumerate(blocks):
            v = lax.rem(core + z.rep - s, z.rep)
            image[v, slot] += block().astype(jnp.float32)

    for_terms(z, plans, parts, spans, add)


def gather_body(z, chunks, skip, *refs):
    refs = list(refs)
    plans = [refs.pop(0) for _ in range(z.env)]
    energy, vectors = refs.pop(0), refs.pop(0)
    so_far, image, sem = refs[-3:]

    def start(j, carry):
        for v in range(z.batch):
            so_far[v, j] = energy[j] * vectors[v, j].astype(jnp.float32)
        return carry

    lax.fori_loop(0, z.slots, start, 0, unroll=2)
    joined = [refs.pop(0) for _ in range(z.rep - 1)]
    for spans in chunks:
        parts = [[(refs.pop(0), 0)] + [(ref, skip) for ref in joined]]
        for _ in range(1, z.env):
            parts.append([(refs.pop(0), 0) for _ in range(z.rep)])
        add_terms(z, plans, so_far, parts, spans)
        skip += sum(span[1] for span in spans)
    copies = []
    for v in range(z.batch):
        copies += split_copy(so_far.at[v], image.at[v], z.slots, sem.at[v])
    for copy in copies:
        copy.start()
    for copy in copies:
        copy.wait()


def gather_terms(z, plans, energy, vectors, joined, skip, parts, chunks, after=()):
    flat = [*joined]
    for chunk in parts:
        flat += [chunk[0][0]] + [ref for piece in chunk[1:] for ref in piece]
    shape = jax.ShapeDtypeStruct(vectors.shape, jnp.float32)
    return pl.pallas_call(
        functools.partial(gather_body, z, chunks, skip),
        out_shape=[shape, pltpu.HBM(vectors.shape, jnp.float32)],
        in_specs=[SMEM] * (z.env + 1) + [VMEM] * (1 + len(flat)) + [ANY] * len(after),
        out_specs=[VMEM, HBM],
        scratch_shapes=[pltpu.SemaphoreType.DMA((z.batch, 4))],
        compiler_params=pltpu.CompilerParams(vmem_limit_bytes=LIMIT),
        cost_estimate=BRIEF,
    )(*plans, energy, vectors, *flat, *after)


def image_body(z, spans, *refs):
    refs = list(refs)
    plans = [refs.pop(0) for _ in range(z.env)]
    so_far = refs.pop(0)
    parts = [[(refs.pop(0), 0) for _ in range(z.rep)] for _ in range(z.env)]
    image, token, sums, sem = refs[-4:]
    token[...] = jnp.zeros_like(token)

    def take(slot, blocks):
        for v in range(z.batch):
            sums[v, slot] = so_far[v, slot]

    for_terms(z, plans, parts, spans, take)
    add_terms(z, plans, sums, parts, spans)
    for wait in (False, True):
        used = []

        def put(slot, blocks):
            for v in range(z.batch):
                copy = pltpu.make_async_copy(
                    sums.at[v, slot], image.at[v, slot], sem.at[len(used), v]
                )
                if wait:
                    copy.wait()
                else:
                    copy.start()
            used.append(slot)

        for_terms(z, plans, parts, spans, put)


def make_image(z, plans, so_far, image, parts, spans):
    flat = [ref for piece in parts for ref in piece]
    count = z.env * sum(span[1] for span in spans)
    return pl.pallas_call(
        functools.partial(image_body, z, spans),
        out_shape=[
            pltpu.HBM(image.shape, jnp.float32),
            jax.ShapeDtypeStruct((8, 128), jnp.float32),
        ],
        in_specs=[SMEM] * z.env + [VMEM] * (1 + len(flat)) + [HBM],
        out_specs=[HBM, VMEM],
        input_output_aliases={z.env + 1 + len(flat): 0},
        scratch_shapes=[
            pltpu.VMEM(image.shape, jnp.float32),
            pltpu.SemaphoreType.DMA((count, z.batch)),
        ],
        compiler_params=pltpu.CompilerParams(vmem_limit_bytes=LIMIT),
        cost_estimate=BRIEF,
    )(*plans, so_far, *flat, image)


def in_order(parts, places, count):
    total = 0.0
    for place in range(count):
        for part, at in zip(parts, places):
            total = total + jnp.where(at == place, part, 0.0)
    return total


def chips_body(z, count, plan, own, *refs):
    arrived, out = refs[:count], refs[-1]
    core, chip = plan[z.core], plan[z.chip]
    parts, places = [], []
    for e in range(z.env):
        for s in range(z.rep):
            ref = arrived[e * z.rep + s - 1] if e + s else own
            tail = ref[ref.shape[0] - TAIL :].astype(jnp.float32)
            parts.append(tail[0:1] + tail[1:2] + tail[2:3])
            at = lax.rem(chip + z.env - e, z.env) * z.rep + lax.rem(core + z.rep - s, z.rep)
            places.append(at)
    total = in_order(parts, places, z.env * z.rep)
    out[...] = jnp.broadcast_to(total, out.shape)


def chip_sums(z, plan, own, arrived, after):
    return pl.pallas_call(
        functools.partial(chips_body, z, len(arrived)),
        out_shape=jax.ShapeDtypeStruct((8, z.order), jnp.float32),
        in_specs=[SMEM] + [VMEM] * (1 + len(arrived)) + [ANY] * len(after),
        out_specs=VMEM,
        compiler_params=pltpu.CompilerParams(vmem_limit_bytes=SMALL),
        cost_estimate=BRIEF,
    )(plan, own, *arrived, *after)


def mean_body(z, count, scale, *refs):
    out = refs[-1]
    me = lax.axis_index("sector")
    parts = [ref[0:1] for ref in refs[:count]]
    total = parts[0]
    if count > 1:
        places = [lax.rem(me + z.sector - step, z.sector) for step in range(count)]
        total = in_order(parts, places, count)
    out[...] = total[:, : out.shape[1]] * scale


def mean_over_sectors(z, array, entries, after):
    held = [array]
    if z.sector <= 4:
        held += [shift(array, "sector", z.sector, step) for step in range(1, z.sector)]
    else:
        held = [total_over(array, "sector")]
    made = pl.pallas_call(
        functools.partial(mean_body, z, len(held), 1.0 / entries),
        out_shape=jax.ShapeDtypeStruct((1, z.batch), jnp.float32),
        in_specs=[VMEM] * len(held) + [ANY] * len(after),
        out_specs=VMEM,
        compiler_params=pltpu.CompilerParams(vmem_limit_bytes=SMALL),
        cost_estimate=BRIEF,
    )(*held, *after)
    return made.reshape(z.batch)


def shift(array, axis, size, step):
    return lax.ppermute(array, axis, [(i, (i + step) % size) for i in range(size)])


def shift_both(z, array, e, s):
    perm = []
    for x in range(z.env):
        for c in range(z.rep):
            perm.append((x * z.rep + c, (x + e) % z.env * z.rep + (c + s) % z.rep))
    return lax.ppermute(array, ("env", "rep"), perm)


def total_over(array, axis):
    size = lax.axis_size(axis)
    if size & (size - 1):
        return lax.psum(array, axis)
    step = 1
    while step < size:
        array = array + lax.ppermute(array, axis, [(i, i ^ step) for i in range(size)])
        step *= 2
    return array


def on_device(vectors, left_env, right_env, energy, partner):
    z = Sizes(vectors, left_env)
    each = z.sector // 4
    span = z.capacity

    def spans_of(g):
        return [((g * each + d) * span, span) for d in range(each)]

    chunks = {g: spans_of(g) for g in range(4)}

    def around(array):
        return [array] + [shift(array, "rep", z.rep, s) for s in range(1, z.rep)]

    def across(arrays, g):
        steps = [g * each + d for d in range(each)]
        return [shift(a, "sector", z.sector, k) if k else a for a, k in zip(arrays, steps)]

    vector_others = around(vectors)[1:]
    right_others = around(right_env)[1:]
    left = around(left_env)
    plan, to_send, own, right_own = load(z, partner, vectors, right_env)
    partners = [shift(to_send, "env", z.env, e) for e in range(1, z.env)]
    own = gate(own, partners)
    right = [right_own] + right_others
    near_rows = [own[0]] + vector_others
    vec = [near_rows]
    for e in range(1, z.env):
        vec.append([shift_both(z, own[s], e, s) for s in range(z.rep)])
    plans = [plan] + [plan_only(z, other) for other in partners]

    def near_products(g, after):
        return products(z, plan, right, [near_rows], chunks[g], after)

    def far_products(g, after):
        return products(z, plan, right, vec[1:], chunks[g], after)

    near, far, parts = {}, {}, {}
    spans = chunks[1] + chunks[3]
    made = products(z, plan, right, [near_rows], spans)
    near[1], near[3] = across(made[:each], 1), across(made[each:], 3)
    made = near_products(2, (made[0], *left[1:]))
    near[2] = across(made, 2)

    def send_terms(g, so_far, own_sums, kept, after):
        made, folded = terms(
            z, plan, left, near[g], far[g], vec, chunks[g], so_far,
            own_sums, kept, after
        )
        first = made[: z.rep]
        if own_sums is not None:
            first[1:] = [shift(first[s], "rep", z.rep, s) for s in range(1, z.rep)]
        parts[g] = [first]
        for e in range(1, z.env):
            parts[g].append([shift_both(z, made[e * z.rep + s], e, s) for s in range(z.rep)])
        return folded

    def arrived(g):
        return [part for piece in parts[g][1:] for part in piece]

    near[0] = near_products(0, made[:1])
    far1 = far_products(1, (near[0][0], *plans[1:]))
    far1 = gate(far1, [*near[1], *near[3]])
    far[1] = across(far1, 1)
    far[0] = far_products(0, far1[:1])
    dots = send_terms(0, None, None, (), ())
    far3 = far_products(3, (dots,))
    far2 = far_products(2, far3[:1])
    far3 = gate(far3, [far2[0], *near[2], *arrived(0)[:1]])
    far[3] = across(far3, 3)
    far2 = gate(far2, [far3[0], *far[1]])
    far[2] = across(far2, 2)
    dots = send_terms(1, dots, None, (), (far2[0], *arrived(0)[1:]))
    dots = send_terms(3, dots, None, (), arrived(1)[:1])
    own_block = vectors.astype(jnp.float32)
    own_sums = jnp.sum(energy[None, :, None, None] * own_block * own_block, axis=(1, 2, 3))
    early = (0, 1, 3)
    kept = [parts[g][0][1:] for g in early]
    dots = send_terms(2, dots, own_sums, kept, arrived(1)[1:] + arrived(3))
    so_far, image = gather_terms(
        z,
        plans,
        energy,
        vectors,
        parts[2][0][1:],
        sum(piece[1] for piece in chunks[2]),
        [parts[g] for g in early],
        [chunks[g] for g in early],
        (dots,),
    )
    sums = chip_sums(z, plan, dots, parts[2][0][1:] + arrived(2), (so_far,))
    image, token = make_image(z, plans, so_far, image, parts[2], chunks[2])
    entries = z.slots * z.sector * z.order * z.order
    return (image, mean_over_sectors(z, sums, entries, (token,)))


def solution(mesh):
    return jax.shard_map(
        on_device,
        mesh=mesh,
        in_specs=(
            P(None, ("groups", "sector"), ("env", "rep"), None),
            P("env", ("groups", "sector"), "rep", None),
            P("env", ("groups", "sector"), "rep", None),
            P(("groups", "sector")),
            P("env", "groups"),
        ),
        out_specs=(P(None, ("groups", "sector"), ("env", "rep"), None), P("groups")),
        check_vma=False,
    )
```

```python
import functools

import jax
import jax.numpy as jnp
from jax import lax
from jax.experimental import pallas as pl
from jax.experimental.pallas import tpu as pltpu
from jax.sharding import PartitionSpec as P

ANY = pl.BlockSpec(memory_space=pl.ANY)
HBM = pl.BlockSpec(memory_space=pltpu.HBM)
SMEM = pl.BlockSpec(memory_space=pltpu.SMEM)
VMEM = pl.BlockSpec(memory_space=pltpu.VMEM)
LIMIT = 12 * 1024 * 1024
SMALL = 2 * 1024 * 1024
TAIL = 16
BRIEF = pl.CostEstimate(flops=0, bytes_accessed=0, transcendentals=0)


def aligned(index, size):
    return pl.multiple_of(index * size, size)


class Sizes:
    def __init__(self, vectors, left_env):
        self.env = lax.axis_size("env")
        self.rep = lax.axis_size("rep")
        self.sector = lax.axis_size("sector")
        self.batch, self.slots, self.own_rows, self.order = vectors.shape
        assert self.batch == self.rep and self.sector % 4 == 0
        self.half = left_env.shape[2]
        self.chip_rows = self.own_rows * self.rep
        self.capacity = 2 * ((self.slots + 2 * self.sector - 1) // (2 * self.sector))
        self.flat = self.sector * self.capacity
        self.full = self.flat == self.slots
        self.source, self.target, self.valid = 0, self.flat, 2 * self.flat
        self.core, self.chip = 3 * self.flat, 3 * self.flat + 1

    def when_valid(self, plan, flat, action):
        if self.full:
            action()
        else:
            pl.when(plan[self.valid + flat] == 1)(action)


def write_plan(z, partner, plan, count):
    if not z.full:

        def clear(i, carry):
            plan[i] = 0
            return carry

        lax.fori_loop(0, 3 * z.flat, clear, 0)
    for d in range(z.sector):
        count[d] = 0
    factor = -(-(1 << 16) // z.slots)
    assert all(i * factor >> 16 == i // z.slots for i in range(z.sector * z.slots))
    for j in range(z.slots):
        sector = partner[0, j]
        group = (sector * factor) >> 16
        slot = sector - group * z.slots
        distance = jnp.where(group == 0, 0, z.sector - group)
        rank = count[distance]
        count[distance] = rank + 1
        index = distance * z.capacity + rank
        plan[z.source + index] = slot
        plan[z.target + index] = j
        plan[z.valid + index] = 1
    plan[z.core] = lax.axis_index("rep")
    plan[z.chip] = lax.axis_index("env")


def split_copy(source, target, slots, sem):
    step = slots // 4 if slots % 4 == 0 else slots
    copies = []
    for i in range(slots // step):
        part = pl.ds(i * step, step)
        copies.append(pltpu.make_async_copy(source.at[part], target.at[part], sem.at[i]))
    return copies


def load_body(z, partner, vectors, right, plan, *refs):
    rows, block, count, sem = refs[: z.rep], refs[z.rep], refs[-2], refs[-1]
    core = lax.axis_index("rep")
    copies = []
    for s, ref in enumerate(rows):
        mine = vectors.at[lax.rem(core + s, z.rep)]
        copies += split_copy(mine, ref, z.slots, sem.at[s])
    copies += split_copy(right.at[0], block.at[0], z.slots, sem.at[z.rep])
    for copy in copies:
        copy.start()
    write_plan(z, partner, plan, count)
    for copy in copies:
        copy.wait()


def load(z, partner, vectors, right_env):
    row = jax.ShapeDtypeStruct(vectors.shape[1:], jnp.bfloat16)
    plan, *made = pl.pallas_call(
        functools.partial(load_body, z),
        out_shape=[jax.ShapeDtypeStruct((3 * z.flat + 2,), jnp.int32)]
        + [row] * z.rep
        + [jax.ShapeDtypeStruct(right_env.shape, jnp.bfloat16)],
        in_specs=[SMEM, HBM, HBM],
        out_specs=[SMEM] + [VMEM] * (z.rep + 1),
        scratch_shapes=[
            pltpu.SMEM((z.sector,), jnp.int32),
            pltpu.SemaphoreType.DMA((z.rep + 1, 4)),
        ],
        compiler_params=pltpu.CompilerParams(vmem_limit_bytes=LIMIT),
        cost_estimate=BRIEF,
    )(
        partner,
        pltpu.with_memory_space_constraint(vectors, pltpu.HBM),
        pltpu.with_memory_space_constraint(right_env, pltpu.HBM),
    )
    return plan, made[: z.rep], made[z.rep]


def plan_only(z, partner):
    return pl.pallas_call(
        functools.partial(write_plan, z),
        out_shape=jax.ShapeDtypeStruct((3 * z.flat + 2,), jnp.int32),
        in_specs=[SMEM],
        out_specs=SMEM,
        scratch_shapes=[pltpu.SMEM((z.sector,), jnp.int32)],
        compiler_params=pltpu.CompilerParams(vmem_limit_bytes=SMALL),
        cost_estimate=BRIEF,
    )(partner)


def gate(arrays, after):
    def body(*refs):
        pass

    return pl.pallas_call(
        body,
        out_shape=[jax.ShapeDtypeStruct(a.shape, a.dtype) for a in arrays],
        in_specs=[ANY] * (len(arrays) + len(after)),
        out_specs=[ANY] * len(arrays),
        input_output_aliases={i: i for i in range(len(arrays))},
        compiler_params=pltpu.CompilerParams(vmem_limit_bytes=SMALL),
        cost_estimate=BRIEF,
    )(*arrays, *after)


def pick(z, core, place, candidates):
    chosen = candidates[0]
    for s in range(1, z.rep):
        chosen = jnp.where(lax.rem(core + z.rep - s, z.rep) == place, candidates[s], chosen)
    return chosen


def line(ref, core, slot):
    return ref[core, slot] if len(ref.shape) == 4 else ref[slot]


def products_body(z, pieces, spans, *refs):
    refs = list(refs)
    plan = refs.pop(0)
    right = [refs.pop(0) for _ in range(z.rep)]
    rows = [[refs.pop(0) for _ in range(z.rep)] for _ in range(pieces)]
    outs = refs[-len(spans) :]
    core = plan[z.core]
    for (first, count), out in zip(spans, outs):
        for i in range(count):
            slot = plan[z.source + first + i]
            halves = [ref[0, slot] for ref in right]
            parts = [[line(ref, core, slot) for ref in piece] for piece in rows]
            block = jnp.concatenate([pick(z, core, k, halves) for k in range(z.rep)], axis=0)
            lines = jnp.concatenate(
                [pick(z, core, k, part) for part in parts for k in range(z.rep)], axis=0
            )
            out[i] = lax.dot_general(
                lines, block, (((1,), (1,)), ((), ())), preferred_element_type=jnp.float32
            ).astype(jnp.bfloat16)


def products(z, plan, right, rows, spans, after=()):
    pieces = len(rows)
    flat = [ref for piece in rows for ref in piece]
    height = pieces * z.chip_rows
    return pl.pallas_call(
        functools.partial(products_body, z, pieces, spans),
        out_shape=[
            jax.ShapeDtypeStruct((count, height, z.order), jnp.bfloat16) for _, count in spans
        ],
        in_specs=[SMEM] + [VMEM] * (len(right) + len(flat)) + [ANY] * len(after),
        out_specs=[VMEM] * len(spans),
        compiler_params=pltpu.CompilerParams(vmem_limit_bytes=LIMIT),
        cost_estimate=BRIEF,
    )(plan, *right, *flat, *after)


def terms_body(z, spans, chained, last, kept, *refs):
    refs = list(refs)
    plan = refs.pop(0)
    left = [refs.pop(0) for _ in range(z.rep)]
    near = [refs.pop(0) for _ in spans]
    far = [refs.pop(0) for _ in spans]
    vec = [[refs.pop(0) for _ in range(z.rep)] for _ in range(z.env)]
    so_far = refs.pop(0) if chained else None
    own_sums = refs.pop(0) if last else None
    kept = [[refs.pop(0) for _ in range(z.rep - 1)] for _ in range(kept)]
    pbuf, tbuf = refs[-2:]
    dots = refs[-3]
    outs = refs[-3 - z.env * z.rep : -3]
    core, chip = plan[z.core], plan[z.chip]
    total = so_far[...] if chained else jnp.zeros((8, z.order), jnp.float32)
    n = 0
    for d, (first, count, skip) in enumerate(spans):
        for i in range(count):
            slot = plan[z.target + first + i]
            for e in range(z.env):
                place = lax.rem(chip + z.env - e, z.env)
                if e == 0:
                    lines = near[d][skip + i]
                else:
                    lines = far[d][i, (e - 1) * z.chip_rows : e * z.chip_rows]
                pbuf[n, pl.ds(aligned(place, z.chip_rows), z.chip_rows)] = lines
            halves = [ref[0, slot] for ref in left]
            block = jnp.concatenate([pick(z, core, k, halves) for k in range(z.rep)], axis=0)
            tbuf[n] = jnp.dot(block, pbuf[n], preferred_element_type=jnp.float32).astype(
                jnp.bfloat16
            )
            folded = jnp.zeros(total.shape, jnp.float32)
            for e in range(z.env):
                for s in range(z.rep):
                    place = lax.rem(chip + e, z.env) * z.rep + lax.rem(core + s, z.rep)
                    term = tbuf[n, pl.ds(aligned(place, z.own_rows), z.own_rows)]
                    if last and e + s:
                        outs[e * z.rep + s][n * z.own_rows : (n + 1) * z.own_rows] = term
                    else:
                        outs[e * z.rep + s][n] = term
                    lines = line(vec[(z.env - e) % z.env][(z.rep - s) % z.rep], core, slot)
                    both = lines.astype(jnp.float32) * term.astype(jnp.float32)
                    folded += jnp.sum(both.reshape(-1, *total.shape), axis=0)
            if not z.full:
                folded = jnp.where(plan[z.valid + first + i] == 1, folded, 0.0)
            total += folded
            n += 1
    if not last:
        dots[...] = total
        return
    row = lax.broadcasted_iota(jnp.int32, dots.shape, 0)
    column = lax.broadcasted_iota(jnp.int32, dots.shape, 1)
    value = jnp.where(column == core, jnp.sum(total), 0.0)
    for v in range(z.batch):
        value += jnp.where(column == v, own_sums[v], 0.0)
    split = jnp.zeros(dots.shape, jnp.float32)
    for k in range(3):
        piece = value.astype(jnp.bfloat16).astype(jnp.float32)
        split = jnp.where(row == k, piece, split)
        value = value - piece
    split = split.astype(jnp.bfloat16)
    dots[...] = split
    at = n * z.own_rows
    for blocks in kept:
        for s, block in enumerate(blocks):
            for i in range(block.shape[0]):
                outs[1 + s][at + i * z.own_rows : at + (i + 1) * z.own_rows] = block[i]
        at += blocks[0].shape[0] * z.own_rows
    for out in outs[1:]:
        out[out.shape[0] - TAIL :] = split


def terms(z, plan, left, near, far, vec, spans, so_far=None, own_sums=None, kept=(), after=()):
    count = sum(span[1] for span in spans)
    flat = [ref for piece in vec for ref in piece]
    shapes = [(count, z.own_rows, z.order)] * (z.env * z.rep)
    whole = (count, z.order, z.order)
    last = own_sums is not None
    sums = jax.ShapeDtypeStruct((8, z.order), jnp.float32)
    if last:
        shapes[1:] = [(count * z.own_rows + TAIL, z.order)] * (z.env * z.rep - 1)
        more = sum(blocks[0].shape[0] for blocks in kept)
        shapes[1 : z.rep] = [((count + more) * z.own_rows + TAIL, z.order)] * (z.rep - 1)
        sums = jax.ShapeDtypeStruct((TAIL, z.order), jnp.bfloat16)
    extra = [] if so_far is None else [so_far]
    specs = [VMEM] * len(extra)
    if last:
        extra.append(own_sums)
        specs.append(SMEM)
    extra += [block for blocks in kept for block in blocks]
    specs += [VMEM] * (len(extra) - len(specs))
    *made, dots = pl.pallas_call(
        functools.partial(terms_body, z, spans, so_far is not None, last, len(kept)),
        out_shape=[jax.ShapeDtypeStruct(shape, jnp.bfloat16) for shape in shapes] + [sums],
        in_specs=[SMEM]
        + [VMEM] * (len(left) + len(near) + len(far) + len(flat))
        + specs
        + [ANY] * len(after),
        out_specs=[VMEM] * (len(shapes) + 1),
        scratch_shapes=[pltpu.VMEM(whole, jnp.bfloat16), pltpu.VMEM(whole, jnp.bfloat16)],
        compiler_params=pltpu.CompilerParams(vmem_limit_bytes=LIMIT),
        cost_estimate=BRIEF,
    )(plan, *left, *near, *far, *flat, *extra, *after)
    return made, dots


def for_terms(z, plans, parts, spans, action):
    n = 0
    for first, count, _ in spans:
        for i in range(count):
            for e, plan in enumerate(plans):

                def act():
                    blocks = []
                    for ref, skip in parts[e]:
                        if len(ref.shape) == 3:
                            blocks.append(lambda ref=ref: ref[n])
                        else:
                            rows = slice((skip + n) * z.own_rows, (skip + n + 1) * z.own_rows)
                            blocks.append(lambda ref=ref, rows=rows: ref[rows])
                    action(plan[z.target + first + i], blocks)

                z.when_valid(plan, first + i, act)
            n += 1


def add_terms(z, plans, image, parts, spans):
    core = plans[0][z.core]

    def add(slot, blocks):
        for s, block in enumerate(blocks):
            v = lax.rem(core + z.rep - s, z.rep)
            image[v, slot] += block().astype(jnp.float32)

    for_terms(z, plans, parts, spans, add)


def gather_body(z, chunks, skip, *refs):
    refs = list(refs)
    plans = [refs.pop(0) for _ in range(z.env)]
    energy, vectors = refs.pop(0), refs.pop(0)
    so_far, image, sem = refs[-3:]

    def start(j, carry):
        for v in range(z.batch):
            so_far[v, j] = energy[j] * vectors[v, j].astype(jnp.float32)
        return carry

    lax.fori_loop(0, z.slots, start, 0, unroll=2)
    joined = [refs.pop(0) for _ in range(z.rep - 1)]
    for spans in chunks:
        parts = [[(refs.pop(0), 0)] + [(ref, skip) for ref in joined]]
        for _ in range(1, z.env):
            parts.append([(refs.pop(0), 0) for _ in range(z.rep)])
        add_terms(z, plans, so_far, parts, spans)
        skip += sum(span[1] for span in spans)
    copies = []
    for v in range(z.batch):
        copies += split_copy(so_far.at[v], image.at[v], z.slots, sem.at[v])
    for copy in copies:
        copy.start()
    for copy in copies:
        copy.wait()


def gather_terms(z, plans, energy, vectors, joined, skip, parts, chunks, after=()):
    flat = [*joined]
    for chunk in parts:
        flat += [chunk[0][0]] + [ref for piece in chunk[1:] for ref in piece]
    shape = jax.ShapeDtypeStruct(vectors.shape, jnp.float32)
    return pl.pallas_call(
        functools.partial(gather_body, z, chunks, skip),
        out_shape=[shape, pltpu.HBM(vectors.shape, jnp.float32)],
        in_specs=[SMEM] * (z.env + 1) + [VMEM] * (1 + len(flat)) + [ANY] * len(after),
        out_specs=[VMEM, HBM],
        scratch_shapes=[pltpu.SemaphoreType.DMA((z.batch, 4))],
        compiler_params=pltpu.CompilerParams(vmem_limit_bytes=LIMIT),
        cost_estimate=BRIEF,
    )(*plans, energy, vectors, *flat, *after)


def image_body(z, spans, *refs):
    refs = list(refs)
    plans = [refs.pop(0) for _ in range(z.env)]
    so_far = refs.pop(0)
    parts = [[(refs.pop(0), 0) for _ in range(z.rep)] for _ in range(z.env)]
    image, token, sums, sem = refs[-4:]
    token[...] = jnp.zeros_like(token)

    def take(slot, blocks):
        for v in range(z.batch):
            sums[v, slot] = so_far[v, slot]

    for_terms(z, plans, parts, spans, take)
    add_terms(z, plans, sums, parts, spans)
    for wait in (False, True):
        used = []

        def put(slot, blocks):
            for v in range(z.batch):
                copy = pltpu.make_async_copy(
                    sums.at[v, slot], image.at[v, slot], sem.at[len(used), v]
                )
                if wait:
                    copy.wait()
                else:
                    copy.start()
            used.append(slot)

        for_terms(z, plans, parts, spans, put)


def make_image(z, plans, so_far, image, parts, spans):
    flat = [ref for piece in parts for ref in piece]
    count = z.env * sum(span[1] for span in spans)
    return pl.pallas_call(
        functools.partial(image_body, z, spans),
        out_shape=[
            pltpu.HBM(image.shape, jnp.float32),
            jax.ShapeDtypeStruct((8, 128), jnp.float32),
        ],
        in_specs=[SMEM] * z.env + [VMEM] * (1 + len(flat)) + [HBM],
        out_specs=[HBM, VMEM],
        input_output_aliases={z.env + 1 + len(flat): 0},
        scratch_shapes=[
            pltpu.VMEM(image.shape, jnp.float32),
            pltpu.SemaphoreType.DMA((count, z.batch)),
        ],
        compiler_params=pltpu.CompilerParams(vmem_limit_bytes=LIMIT),
        cost_estimate=BRIEF,
    )(*plans, so_far, *flat, image)


def in_order(parts, places, count):
    total = 0.0
    for place in range(count):
        for part, at in zip(parts, places):
            total = total + jnp.where(at == place, part, 0.0)
    return total


def chips_body(z, count, plan, own, *refs):
    arrived, out = refs[:count], refs[-1]
    core, chip = plan[z.core], plan[z.chip]
    parts, places = [], []
    for e in range(z.env):
        for s in range(z.rep):
            ref = arrived[e * z.rep + s - 1] if e + s else own
            tail = ref[ref.shape[0] - TAIL :].astype(jnp.float32)
            parts.append(tail[0:1] + tail[1:2] + tail[2:3])
            at = lax.rem(chip + z.env - e, z.env) * z.rep + lax.rem(core + z.rep - s, z.rep)
            places.append(at)
    total = in_order(parts, places, z.env * z.rep)
    out[...] = jnp.broadcast_to(total, out.shape)


def chip_sums(z, plan, own, arrived, after):
    return pl.pallas_call(
        functools.partial(chips_body, z, len(arrived)),
        out_shape=jax.ShapeDtypeStruct((8, z.order), jnp.float32),
        in_specs=[SMEM] + [VMEM] * (1 + len(arrived)) + [ANY] * len(after),
        out_specs=VMEM,
        compiler_params=pltpu.CompilerParams(vmem_limit_bytes=SMALL),
        cost_estimate=BRIEF,
    )(plan, own, *arrived, *after)


def mean_body(z, count, scale, *refs):
    out = refs[-1]
    me = lax.axis_index("sector")
    parts = [ref[0:1] for ref in refs[:count]]
    total = parts[0]
    if count > 1:
        places = [lax.rem(me + z.sector - step, z.sector) for step in range(count)]
        total = in_order(parts, places, count)
    out[...] = total[:, : out.shape[1]] * scale


def mean_over_sectors(z, array, entries, after):
    held = [array]
    if z.sector <= 4:
        held += [shift(array, "sector", z.sector, step) for step in range(1, z.sector)]
    else:
        held = [total_over(array, "sector")]
    made = pl.pallas_call(
        functools.partial(mean_body, z, len(held), 1.0 / entries),
        out_shape=jax.ShapeDtypeStruct((1, z.batch), jnp.float32),
        in_specs=[VMEM] * len(held) + [ANY] * len(after),
        out_specs=VMEM,
        compiler_params=pltpu.CompilerParams(vmem_limit_bytes=SMALL),
        cost_estimate=BRIEF,
    )(*held, *after)
    return made.reshape(z.batch)


def shift(array, axis, size, step):
    return lax.ppermute(array, axis, [(i, (i + step) % size) for i in range(size)])


def shift_both(z, array, e, s):
    perm = []
    for x in range(z.env):
        for c in range(z.rep):
            perm.append((x * z.rep + c, (x + e) % z.env * z.rep + (c + s) % z.rep))
    return lax.ppermute(array, ("env", "rep"), perm)


def total_over(array, axis):
    size = lax.axis_size(axis)
    if size & (size - 1):
        return lax.psum(array, axis)
    step = 1
    while step < size:
        array = array + lax.ppermute(array, axis, [(i, i ^ step) for i in range(size)])
        step *= 2
    return array


def on_device(vectors, left_env, right_env, energy, partner):
    z = Sizes(vectors, left_env)
    each = z.sector // 4
    span = z.capacity

    def spans_of(g, low=0, high=span):
        return [((g * each + d) * span + low, high - low, low) for d in range(each)]

    chunks = {g: spans_of(g) for g in range(4)}
    cut = 2 * span // 3
    chunks[2], chunks[4] = spans_of(2, 0, cut), spans_of(2, cut, span)

    def around(array):
        return [array] + [shift(array, "rep", z.rep, s) for s in range(1, z.rep)]

    def across(arrays, g):
        steps = [g * each + d for d in range(each)]
        return [shift(a, "sector", z.sector, k) if k else a for a, k in zip(arrays, steps)]

    vector_others = around(vectors)[1:]
    right_others = around(right_env)[1:]
    left = around(left_env)
    plan, own, right_own = load(z, partner, vectors, right_env)
    right = [right_own] + right_others
    near_rows = [own[0]] + vector_others
    vec = [near_rows]
    for e in range(1, z.env):
        vec.append([shift_both(z, own[s], e, s) for s in range(z.rep)])
    def near_products(g, after):
        return products(z, plan, right, [near_rows], [c[:2] for c in spans_of(g)], after)

    def far_products(g, after):
        return products(z, plan, right, vec[1:], [c[:2] for c in chunks[g]], after)

    near, far, parts = {}, {}, {}
    spans = [piece[:2] for g in (1, 3) for piece in chunks[g]]
    made = products(z, plan, right, [near_rows], spans)
    near[1], near[3] = across(made[:each], 1), across(made[each:], 3)
    made = near_products(2, (made[0], *left[1:]))
    near[2] = across(made, 2)

    def send_terms(g, so_far, own_sums, kept, after):
        made, folded = terms(
            z, plan, left, near[2 if g == 4 else g], far[g], vec, chunks[g], so_far,
            own_sums, kept, after
        )
        first = made[: z.rep]
        if own_sums is not None:
            first[1:] = [shift(first[s], "rep", z.rep, s) for s in range(1, z.rep)]
        parts[g] = [first]
        for e in range(1, z.env):
            parts[g].append([shift_both(z, made[e * z.rep + s], e, s) for s in range(z.rep)])
        return folded

    def arrived(g):
        return [part for piece in parts[g][1:] for part in piece]

    near[0] = near_products(0, made[:1])
    far1 = far_products(1, near[0][:1])
    far1 = gate(far1, [*near[1], *near[3]])
    far[1] = across(far1, 1)
    far[0] = far_products(0, far1[:1])
    partners = [shift(partner, "env", z.env, e) for e in range(1, z.env)]
    plans = [plan] + [plan_only(z, other) for other in partners]
    dots = send_terms(0, None, None, (), plans[1:])
    far3 = far_products(3, (dots,))
    far2 = far_products(2, far3[:1])
    far4 = far_products(4, far2[:1])
    far3 = gate(far3, [far4[0], *near[2]])
    far[3] = across(far3, 3)
    far2 = gate(far2, [far3[0], *far[1]])
    far[2] = across(far2, 2)
    far4 = gate(far4, far[2])
    far[4] = across(far4, 2)
    dots = send_terms(1, dots, None, (), (far2[0], *arrived(0)))
    dots = send_terms(3, dots, None, (), arrived(1)[:1])
    own_block = vectors.astype(jnp.float32)
    own_sums = jnp.sum(energy[None, :, None, None] * own_block * own_block, axis=(1, 2, 3))
    dots = send_terms(2, dots, None, (), [far4[0]] + arrived(1)[1:] + arrived(3)[:1])
    early = (0, 1, 3, 2)
    kept = [parts[g][0][1:] for g in early]
    dots = send_terms(4, dots, own_sums, kept, arrived(3)[1:] + arrived(2)[:1])
    so_far, image = gather_terms(
        z,
        plans,
        energy,
        vectors,
        parts[4][0][1:],
        sum(piece[1] for piece in chunks[4]),
        [parts[g] for g in early],
        [chunks[g] for g in early],
        (dots,),
    )
    sums = chip_sums(z, plan, dots, parts[4][0][1:] + arrived(4), (so_far,))
    image, token = make_image(z, plans, so_far, image, parts[4], chunks[4])
    entries = z.slots * z.sector * z.order * z.order
    return (image, mean_over_sectors(z, sums, entries, (token,)))


def solution(mesh):
    return jax.shard_map(
        on_device,
        mesh=mesh,
        in_specs=(
            P(None, ("groups", "sector"), ("env", "rep"), None),
            P("env", ("groups", "sector"), "rep", None),
            P("env", ("groups", "sector"), "rep", None),
            P(("groups", "sector")),
            P("env", "groups"),
        ),
        out_specs=(P(None, ("groups", "sector"), ("env", "rep"), None), P("groups")),
        check_vma=False,
    )
```

```python
import functools

import jax
import jax.numpy as jnp
from jax import lax
from jax.experimental import pallas as pl
from jax.experimental.pallas import tpu as pltpu
from jax.sharding import PartitionSpec as P

ANY = pl.BlockSpec(memory_space=pl.ANY)
HBM = pl.BlockSpec(memory_space=pltpu.HBM)
SMEM = pl.BlockSpec(memory_space=pltpu.SMEM)
VMEM = pl.BlockSpec(memory_space=pltpu.VMEM)
LIMIT = 12 * 1024 * 1024
SMALL = 2 * 1024 * 1024
TAIL = 16
BRIEF = pl.CostEstimate(flops=0, bytes_accessed=0, transcendentals=0)


def aligned(index, size):
    return pl.multiple_of(index * size, size)


class Sizes:
    def __init__(self, vectors, left_env):
        self.env = lax.axis_size("env")
        self.rep = lax.axis_size("rep")
        self.sector = lax.axis_size("sector")
        self.batch, self.slots, self.own_rows, self.order = vectors.shape
        assert self.batch == self.rep and self.sector % 4 == 0
        self.half = left_env.shape[2]
        self.chip_rows = self.own_rows * self.rep
        self.capacity = 2 * ((self.slots + 2 * self.sector - 1) // (2 * self.sector))
        self.flat = self.sector * self.capacity
        self.full = self.flat == self.slots
        self.source, self.target, self.valid = 0, self.flat, 2 * self.flat
        self.core, self.chip = 3 * self.flat, 3 * self.flat + 1

    def when_valid(self, plan, flat, action):
        if self.full:
            action()
        else:
            pl.when(plan[self.valid + flat] == 1)(action)


def write_plan(z, partner, plan, count):
    if not z.full:

        def clear(i, carry):
            plan[i] = 0
            return carry

        lax.fori_loop(0, 3 * z.flat, clear, 0)
    for d in range(z.sector):
        count[d] = 0
    factor = -(-(1 << 16) // z.slots)
    assert all(i * factor >> 16 == i // z.slots for i in range(z.sector * z.slots))
    for j in range(z.slots):
        sector = partner[0, j]
        group = (sector * factor) >> 16
        slot = sector - group * z.slots
        distance = jnp.where(group == 0, 0, z.sector - group)
        rank = count[distance]
        count[distance] = rank + 1
        index = distance * z.capacity + rank
        plan[z.source + index] = slot
        plan[z.target + index] = j
        plan[z.valid + index] = 1
    plan[z.core] = lax.axis_index("rep")
    plan[z.chip] = lax.axis_index("env")


def split_copy(source, target, slots, sem):
    step = slots // 4 if slots % 4 == 0 else slots
    copies = []
    for i in range(slots // step):
        part = pl.ds(i * step, step)
        copies.append(pltpu.make_async_copy(source.at[part], target.at[part], sem.at[i]))
    return copies


def load_body(z, partner, vectors, right, plan, *refs):
    rows, block, count, sem = refs[: z.rep], refs[z.rep], refs[-2], refs[-1]
    core = lax.axis_index("rep")
    copies = []
    for s, ref in enumerate(rows):
        mine = vectors.at[lax.rem(core + s, z.rep)]
        copies += split_copy(mine, ref, z.slots, sem.at[s])
    copies += split_copy(right.at[0], block.at[0], z.slots, sem.at[z.rep])
    for copy in copies:
        copy.start()
    write_plan(z, partner, plan, count)
    for copy in copies:
        copy.wait()


def load(z, partner, vectors, right_env):
    row = jax.ShapeDtypeStruct(vectors.shape[1:], jnp.bfloat16)
    plan, *made = pl.pallas_call(
        functools.partial(load_body, z),
        out_shape=[jax.ShapeDtypeStruct((3 * z.flat + 2,), jnp.int32)]
        + [row] * z.rep
        + [jax.ShapeDtypeStruct(right_env.shape, jnp.bfloat16)],
        in_specs=[SMEM, HBM, HBM],
        out_specs=[SMEM] + [VMEM] * (z.rep + 1),
        scratch_shapes=[
            pltpu.SMEM((z.sector,), jnp.int32),
            pltpu.SemaphoreType.DMA((z.rep + 1, 4)),
        ],
        compiler_params=pltpu.CompilerParams(vmem_limit_bytes=LIMIT),
        cost_estimate=BRIEF,
    )(
        partner,
        pltpu.with_memory_space_constraint(vectors, pltpu.HBM),
        pltpu.with_memory_space_constraint(right_env, pltpu.HBM),
    )
    return plan, made[: z.rep], made[z.rep]


def plan_only(z, partner):
    return pl.pallas_call(
        functools.partial(write_plan, z),
        out_shape=jax.ShapeDtypeStruct((3 * z.flat + 2,), jnp.int32),
        in_specs=[SMEM],
        out_specs=SMEM,
        scratch_shapes=[pltpu.SMEM((z.sector,), jnp.int32)],
        compiler_params=pltpu.CompilerParams(vmem_limit_bytes=SMALL),
        cost_estimate=BRIEF,
    )(partner)


def gate(arrays, after):
    def body(*refs):
        pass

    return pl.pallas_call(
        body,
        out_shape=[jax.ShapeDtypeStruct(a.shape, a.dtype) for a in arrays],
        in_specs=[ANY] * (len(arrays) + len(after)),
        out_specs=[ANY] * len(arrays),
        input_output_aliases={i: i for i in range(len(arrays))},
        compiler_params=pltpu.CompilerParams(vmem_limit_bytes=SMALL),
        cost_estimate=BRIEF,
    )(*arrays, *after)


def pick(z, core, place, candidates):
    chosen = candidates[0]
    for s in range(1, z.rep):
        chosen = jnp.where(lax.rem(core + z.rep - s, z.rep) == place, candidates[s], chosen)
    return chosen


def line(ref, core, slot):
    return ref[core, slot] if len(ref.shape) == 4 else ref[slot]


def products_body(z, pieces, spans, *refs):
    refs = list(refs)
    plan = refs.pop(0)
    right = [refs.pop(0) for _ in range(z.rep)]
    rows = [[refs.pop(0) for _ in range(z.rep)] for _ in range(pieces)]
    outs = refs[-len(spans) :]
    core = plan[z.core]
    for (first, count), out in zip(spans, outs):
        for i in range(count):
            slot = plan[z.source + first + i]
            halves = [ref[0, slot] for ref in right]
            parts = [[line(ref, core, slot) for ref in piece] for piece in rows]
            block = jnp.concatenate([pick(z, core, k, halves) for k in range(z.rep)], axis=0)
            lines = jnp.concatenate(
                [pick(z, core, k, part) for part in parts for k in range(z.rep)], axis=0
            )
            out[i] = lax.dot_general(
                lines, block, (((1,), (1,)), ((), ())), preferred_element_type=jnp.float32
            ).astype(jnp.bfloat16)


def products(z, plan, right, rows, spans, after=()):
    pieces = len(rows)
    flat = [ref for piece in rows for ref in piece]
    height = pieces * z.chip_rows
    return pl.pallas_call(
        functools.partial(products_body, z, pieces, spans),
        out_shape=[
            jax.ShapeDtypeStruct((count, height, z.order), jnp.bfloat16) for _, count in spans
        ],
        in_specs=[SMEM] + [VMEM] * (len(right) + len(flat)) + [ANY] * len(after),
        out_specs=[VMEM] * len(spans),
        compiler_params=pltpu.CompilerParams(vmem_limit_bytes=LIMIT),
        cost_estimate=BRIEF,
    )(plan, *right, *flat, *after)


def terms_body(z, spans, chained, last, kept, *refs):
    refs = list(refs)
    plan = refs.pop(0)
    left = [refs.pop(0) for _ in range(z.rep)]
    near = [refs.pop(0) for _ in spans]
    far = [refs.pop(0) for _ in spans]
    vec = [[refs.pop(0) for _ in range(z.rep)] for _ in range(z.env)]
    so_far = refs.pop(0) if chained else None
    own_sums = refs.pop(0) if last else None
    kept = [[refs.pop(0) for _ in range(z.rep - 1)] for _ in range(kept)]
    pbuf, tbuf = refs[-2:]
    dots = refs[-3]
    outs = refs[-3 - z.env * z.rep : -3]
    core, chip = plan[z.core], plan[z.chip]
    total = so_far[...] if chained else jnp.zeros((8, z.order), jnp.float32)
    n = 0
    for d, (first, count, skip) in enumerate(spans):
        for i in range(count):
            slot = plan[z.target + first + i]
            for e in range(z.env):
                place = lax.rem(chip + z.env - e, z.env)
                if e == 0:
                    lines = near[d][skip + i]
                else:
                    lines = far[d][i, (e - 1) * z.chip_rows : e * z.chip_rows]
                pbuf[n, pl.ds(aligned(place, z.chip_rows), z.chip_rows)] = lines
            halves = [ref[0, slot] for ref in left]
            block = jnp.concatenate([pick(z, core, k, halves) for k in range(z.rep)], axis=0)
            tbuf[n] = jnp.dot(block, pbuf[n], preferred_element_type=jnp.float32).astype(
                jnp.bfloat16
            )
            folded = jnp.zeros(total.shape, jnp.float32)
            for e in range(z.env):
                for s in range(z.rep):
                    place = lax.rem(chip + e, z.env) * z.rep + lax.rem(core + s, z.rep)
                    term = tbuf[n, pl.ds(aligned(place, z.own_rows), z.own_rows)]
                    if last and e + s:
                        outs[e * z.rep + s][n * z.own_rows : (n + 1) * z.own_rows] = term
                    else:
                        outs[e * z.rep + s][n] = term
                    lines = line(vec[(z.env - e) % z.env][(z.rep - s) % z.rep], core, slot)
                    both = lines.astype(jnp.float32) * term.astype(jnp.float32)
                    folded += jnp.sum(both.reshape(-1, *total.shape), axis=0)
            if not z.full:
                folded = jnp.where(plan[z.valid + first + i] == 1, folded, 0.0)
            total += folded
            n += 1
    if not last:
        dots[...] = total
        return
    row = lax.broadcasted_iota(jnp.int32, dots.shape, 0)
    column = lax.broadcasted_iota(jnp.int32, dots.shape, 1)
    value = jnp.where(column == core, jnp.sum(total), 0.0)
    for v in range(z.batch):
        value += jnp.where(column == v, own_sums[v], 0.0)
    split = jnp.zeros(dots.shape, jnp.float32)
    for k in range(3):
        piece = value.astype(jnp.bfloat16).astype(jnp.float32)
        split = jnp.where(row == k, piece, split)
        value = value - piece
    split = split.astype(jnp.bfloat16)
    dots[...] = split
    at = n * z.own_rows
    for blocks in kept:
        for s, block in enumerate(blocks):
            for i in range(block.shape[0]):
                outs[1 + s][at + i * z.own_rows : at + (i + 1) * z.own_rows] = block[i]
        at += blocks[0].shape[0] * z.own_rows
    for out in outs[1:]:
        out[out.shape[0] - TAIL :] = split


def terms(z, plan, left, near, far, vec, spans, so_far=None, own_sums=None, kept=(), after=()):
    count = sum(span[1] for span in spans)
    flat = [ref for piece in vec for ref in piece]
    shapes = [(count, z.own_rows, z.order)] * (z.env * z.rep)
    whole = (count, z.order, z.order)
    last = own_sums is not None
    sums = jax.ShapeDtypeStruct((8, z.order), jnp.float32)
    if last:
        shapes[1:] = [(count * z.own_rows + TAIL, z.order)] * (z.env * z.rep - 1)
        more = sum(blocks[0].shape[0] for blocks in kept)
        shapes[1 : z.rep] = [((count + more) * z.own_rows + TAIL, z.order)] * (z.rep - 1)
        sums = jax.ShapeDtypeStruct((TAIL, z.order), jnp.bfloat16)
    extra = [] if so_far is None else [so_far]
    specs = [VMEM] * len(extra)
    if last:
        extra.append(own_sums)
        specs.append(SMEM)
    extra += [block for blocks in kept for block in blocks]
    specs += [VMEM] * (len(extra) - len(specs))
    *made, dots = pl.pallas_call(
        functools.partial(terms_body, z, spans, so_far is not None, last, len(kept)),
        out_shape=[jax.ShapeDtypeStruct(shape, jnp.bfloat16) for shape in shapes] + [sums],
        in_specs=[SMEM]
        + [VMEM] * (len(left) + len(near) + len(far) + len(flat))
        + specs
        + [ANY] * len(after),
        out_specs=[VMEM] * (len(shapes) + 1),
        scratch_shapes=[pltpu.VMEM(whole, jnp.bfloat16), pltpu.VMEM(whole, jnp.bfloat16)],
        compiler_params=pltpu.CompilerParams(vmem_limit_bytes=LIMIT),
        cost_estimate=BRIEF,
    )(plan, *left, *near, *far, *flat, *extra, *after)
    return made, dots


def for_terms(z, plans, parts, spans, action):
    n = 0
    for first, count, _ in spans:
        for i in range(count):
            for e, plan in enumerate(plans):

                def act():
                    blocks = []
                    for ref, skip in parts[e]:
                        if len(ref.shape) == 3:
                            blocks.append(lambda ref=ref: ref[n])
                        else:
                            rows = slice((skip + n) * z.own_rows, (skip + n + 1) * z.own_rows)
                            blocks.append(lambda ref=ref, rows=rows: ref[rows])
                    action(plan[z.target + first + i], blocks)

                z.when_valid(plan, first + i, act)
            n += 1


def add_terms(z, plans, image, parts, spans):
    core = plans[0][z.core]

    def add(slot, blocks):
        for s, block in enumerate(blocks):
            v = lax.rem(core + z.rep - s, z.rep)
            image[v, slot] += block().astype(jnp.float32)

    for_terms(z, plans, parts, spans, add)


def gather_body(z, chunks, skip, *refs):
    refs = list(refs)
    plans = [refs.pop(0) for _ in range(z.env)]
    energy, vectors = refs.pop(0), refs.pop(0)
    so_far, image, sem = refs[-3:]

    def start(j, carry):
        for v in range(z.batch):
            so_far[v, j] = energy[j] * vectors[v, j].astype(jnp.float32)
        return carry

    lax.fori_loop(0, z.slots, start, 0, unroll=2)
    joined = [refs.pop(0) for _ in range(z.rep - 1)]
    for spans in chunks:
        parts = [[(refs.pop(0), 0)] + [(ref, skip) for ref in joined]]
        for _ in range(1, z.env):
            parts.append([(refs.pop(0), 0) for _ in range(z.rep)])
        add_terms(z, plans, so_far, parts, spans)
        skip += sum(span[1] for span in spans)
    copies = []
    for v in range(z.batch):
        copies += split_copy(so_far.at[v], image.at[v], z.slots, sem.at[v])
    for copy in copies:
        copy.start()
    for copy in copies:
        copy.wait()


def gather_terms(z, plans, energy, vectors, joined, skip, parts, chunks, after=()):
    flat = [*joined]
    for chunk in parts:
        flat += [chunk[0][0]] + [ref for piece in chunk[1:] for ref in piece]
    shape = jax.ShapeDtypeStruct(vectors.shape, jnp.float32)
    return pl.pallas_call(
        functools.partial(gather_body, z, chunks, skip),
        out_shape=[shape, pltpu.HBM(vectors.shape, jnp.float32)],
        in_specs=[SMEM] * (z.env + 1) + [VMEM] * (1 + len(flat)) + [ANY] * len(after),
        out_specs=[VMEM, HBM],
        scratch_shapes=[pltpu.SemaphoreType.DMA((z.batch, 4))],
        compiler_params=pltpu.CompilerParams(vmem_limit_bytes=LIMIT),
        cost_estimate=BRIEF,
    )(*plans, energy, vectors, *flat, *after)


def image_body(z, spans, *refs):
    refs = list(refs)
    plans = [refs.pop(0) for _ in range(z.env)]
    so_far = refs.pop(0)
    parts = [[(refs.pop(0), 0) for _ in range(z.rep)] for _ in range(z.env)]
    image, token, sums, sem = refs[-4:]
    token[...] = jnp.zeros_like(token)

    def take(slot, blocks):
        for v in range(z.batch):
            sums[v, slot] = so_far[v, slot]

    for_terms(z, plans, parts, spans, take)
    add_terms(z, plans, sums, parts, spans)
    for wait in (False, True):
        used = []

        def put(slot, blocks):
            for v in range(z.batch):
                copy = pltpu.make_async_copy(
                    sums.at[v, slot], image.at[v, slot], sem.at[len(used), v]
                )
                if wait:
                    copy.wait()
                else:
                    copy.start()
            used.append(slot)

        for_terms(z, plans, parts, spans, put)


def make_image(z, plans, so_far, image, parts, spans):
    flat = [ref for piece in parts for ref in piece]
    count = z.env * sum(span[1] for span in spans)
    return pl.pallas_call(
        functools.partial(image_body, z, spans),
        out_shape=[
            pltpu.HBM(image.shape, jnp.float32),
            jax.ShapeDtypeStruct((8, 128), jnp.float32),
        ],
        in_specs=[SMEM] * z.env + [VMEM] * (1 + len(flat)) + [HBM],
        out_specs=[HBM, VMEM],
        input_output_aliases={z.env + 1 + len(flat): 0},
        scratch_shapes=[
            pltpu.VMEM(image.shape, jnp.float32),
            pltpu.SemaphoreType.DMA((count, z.batch)),
        ],
        compiler_params=pltpu.CompilerParams(vmem_limit_bytes=LIMIT),
        cost_estimate=BRIEF,
    )(*plans, so_far, *flat, image)


def in_order(parts, places, count):
    total = 0.0
    for place in range(count):
        for part, at in zip(parts, places):
            total = total + jnp.where(at == place, part, 0.0)
    return total


def chips_body(z, count, plan, own, *refs):
    arrived, out = refs[:count], refs[-1]
    core, chip = plan[z.core], plan[z.chip]
    parts, places = [], []
    for e in range(z.env):
        for s in range(z.rep):
            ref = arrived[e * z.rep + s - 1] if e + s else own
            tail = ref[ref.shape[0] - TAIL :].astype(jnp.float32)
            parts.append(tail[0:1] + tail[1:2] + tail[2:3])
            at = lax.rem(chip + z.env - e, z.env) * z.rep + lax.rem(core + z.rep - s, z.rep)
            places.append(at)
    total = in_order(parts, places, z.env * z.rep)
    out[...] = jnp.broadcast_to(total, out.shape)


def chip_sums(z, plan, own, arrived, after):
    return pl.pallas_call(
        functools.partial(chips_body, z, len(arrived)),
        out_shape=jax.ShapeDtypeStruct((8, z.order), jnp.float32),
        in_specs=[SMEM] + [VMEM] * (1 + len(arrived)) + [ANY] * len(after),
        out_specs=VMEM,
        compiler_params=pltpu.CompilerParams(vmem_limit_bytes=SMALL),
        cost_estimate=BRIEF,
    )(plan, own, *arrived, *after)


def mean_body(z, count, scale, *refs):
    out = refs[-1]
    me = lax.axis_index("sector")
    parts = [ref[0:1] for ref in refs[:count]]
    total = parts[0]
    if count > 1:
        places = [lax.rem(me + z.sector - step, z.sector) for step in range(count)]
        total = in_order(parts, places, count)
    out[...] = total[:, : out.shape[1]] * scale


def mean_over_sectors(z, array, entries, after):
    held = [array]
    if z.sector <= 4:
        held += [shift(array, "sector", z.sector, step) for step in range(1, z.sector)]
    else:
        held = [total_over(array, "sector")]
    made = pl.pallas_call(
        functools.partial(mean_body, z, len(held), 1.0 / entries),
        out_shape=jax.ShapeDtypeStruct((1, z.batch), jnp.float32),
        in_specs=[VMEM] * len(held) + [ANY] * len(after),
        out_specs=VMEM,
        compiler_params=pltpu.CompilerParams(vmem_limit_bytes=SMALL),
        cost_estimate=BRIEF,
    )(*held, *after)
    return made.reshape(z.batch)


def shift(array, axis, size, step):
    return lax.ppermute(array, axis, [(i, (i + step) % size) for i in range(size)])


def shift_both(z, array, e, s):
    perm = []
    for x in range(z.env):
        for c in range(z.rep):
            perm.append((x * z.rep + c, (x + e) % z.env * z.rep + (c + s) % z.rep))
    return lax.ppermute(array, ("env", "rep"), perm)


def total_over(array, axis):
    size = lax.axis_size(axis)
    if size & (size - 1):
        return lax.psum(array, axis)
    step = 1
    while step < size:
        array = array + lax.ppermute(array, axis, [(i, i ^ step) for i in range(size)])
        step *= 2
    return array


def on_device(vectors, left_env, right_env, energy, partner):
    z = Sizes(vectors, left_env)
    each = z.sector // 4
    span = z.capacity

    def spans_of(g, low=0, high=span):
        return [((g * each + d) * span + low, high - low, low) for d in range(each)]

    chunks = {g: spans_of(g) for g in range(4)}
    cut = 2 * span // 3
    chunks[2], chunks[4] = spans_of(2, 0, cut), spans_of(2, cut, span)

    def around(array):
        return [array] + [shift(array, "rep", z.rep, s) for s in range(1, z.rep)]

    def across(arrays, g):
        steps = [g * each + d for d in range(each)]
        return [shift(a, "sector", z.sector, k) if k else a for a, k in zip(arrays, steps)]

    partners = [shift(partner, "env", z.env, e) for e in range(1, z.env)]
    vector_others = around(vectors)[1:]
    right_others = around(right_env)[1:]
    left = around(left_env)
    plan, own, right_own = load(z, partner, vectors, right_env)
    own = gate(own, partners)
    plans = [plan] + [plan_only(z, other) for other in partners]
    right = [right_own] + right_others
    near_rows = [own[0]] + vector_others
    vec = [near_rows]
    for e in range(1, z.env):
        vec.append([shift_both(z, own[s], e, s) for s in range(z.rep)])
    def near_products(g, after):
        return products(z, plan, right, [near_rows], [c[:2] for c in spans_of(g)], after)

    def far_products(g, after):
        return products(z, plan, right, vec[1:], [c[:2] for c in chunks[g]], after)

    near, far, parts = {}, {}, {}
    spans = [piece[:2] for g in (1, 3) for piece in chunks[g]]
    made = products(z, plan, right, [near_rows], spans)
    near[1], near[3] = across(made[:each], 1), across(made[each:], 3)
    made = near_products(2, (made[0], *left[1:]))
    near[2] = across(made, 2)

    def send_terms(g, so_far, own_sums, kept, after):
        made, folded = terms(
            z, plan, left, near[2 if g == 4 else g], far[g], vec, chunks[g], so_far,
            own_sums, kept, after
        )
        first = made[: z.rep]
        if own_sums is not None:
            first[1:] = [shift(first[s], "rep", z.rep, s) for s in range(1, z.rep)]
        parts[g] = [first]
        for e in range(1, z.env):
            parts[g].append([shift_both(z, made[e * z.rep + s], e, s) for s in range(z.rep)])
        return folded

    def arrived(g):
        return [part for piece in parts[g][1:] for part in piece]

    near[0] = near_products(0, made[:1])
    far1 = far_products(1, (near[0][0], *plans[1:]))
    far1 = gate(far1, [*near[1], *near[3]])
    far[1] = across(far1, 1)
    far[0] = far_products(0, far1[:1])
    dots = send_terms(0, None, None, (), ())
    far3 = far_products(3, (dots,))
    far2 = far_products(2, far3[:1])
    far4 = far_products(4, far2[:1])
    far3 = gate(far3, [far4[0], *near[2], *arrived(0)[:1]])
    far[3] = across(far3, 3)
    far2 = gate(far2, [far3[0], *far[1]])
    far[2] = across(far2, 2)
    far4 = gate(far4, far[2])
    far[4] = across(far4, 2)
    dots = send_terms(1, dots, None, (), (far2[0], *arrived(0)))
    dots = send_terms(3, dots, None, (), arrived(1)[:1])
    own_block = vectors.astype(jnp.float32)
    own_sums = jnp.sum(energy[None, :, None, None] * own_block * own_block, axis=(1, 2, 3))
    dots = send_terms(2, dots, None, (), [far4[0]] + arrived(1)[1:] + arrived(3)[:1])
    early = (0, 1, 3, 2)
    kept = [parts[g][0][1:] for g in early]
    dots = send_terms(4, dots, own_sums, kept, arrived(3)[1:] + arrived(2))
    so_far, image = gather_terms(
        z,
        plans,
        energy,
        vectors,
        parts[4][0][1:],
        sum(piece[1] for piece in chunks[4]),
        [parts[g] for g in early],
        [chunks[g] for g in early],
        (dots,),
    )
    sums = chip_sums(z, plan, dots, parts[4][0][1:] + arrived(4), (so_far,))
    image, token = make_image(z, plans, so_far, image, parts[4], chunks[4])
    entries = z.slots * z.sector * z.order * z.order
    return (image, mean_over_sectors(z, sums, entries, (token,)))


def solution(mesh):
    return jax.shard_map(
        on_device,
        mesh=mesh,
        in_specs=(
            P(None, ("groups", "sector"), ("env", "rep"), None),
            P("env", ("groups", "sector"), "rep", None),
            P("env", ("groups", "sector"), "rep", None),
            P(("groups", "sector")),
            P("env", "groups"),
        ),
        out_specs=(P(None, ("groups", "sector"), ("env", "rep"), None), P("groups")),
        check_vma=False,
    )
```

```python
import functools

import jax
import jax.numpy as jnp
from jax import lax
from jax.experimental import pallas as pl
from jax.experimental.pallas import tpu as pltpu
from jax.sharding import PartitionSpec as P

ANY = pl.BlockSpec(memory_space=pl.ANY)
HBM = pl.BlockSpec(memory_space=pltpu.HBM)
SMEM = pl.BlockSpec(memory_space=pltpu.SMEM)
VMEM = pl.BlockSpec(memory_space=pltpu.VMEM)
LIMIT = 12 * 1024 * 1024
SMALL = 2 * 1024 * 1024
TAIL = 16
BRIEF = pl.CostEstimate(flops=0, bytes_accessed=0, transcendentals=0)


def aligned(index, size):
    return pl.multiple_of(index * size, size)


class Sizes:
    def __init__(self, vectors, left_env):
        self.env = lax.axis_size("env")
        self.rep = lax.axis_size("rep")
        self.sector = lax.axis_size("sector")
        self.batch, self.slots, self.own_rows, self.order = vectors.shape
        assert self.batch == self.rep and self.sector % 4 == 0
        assert self.sector & (self.sector - 1) == 0
        self.half = left_env.shape[2]
        self.chip_rows = self.own_rows * self.rep
        self.capacity = 2 * ((self.slots + 2 * self.sector - 1) // (2 * self.sector))
        self.flat = self.sector * self.capacity
        self.full = self.flat == self.slots
        self.source, self.target, self.valid = 0, self.flat, 2 * self.flat
        self.core, self.chip = 3 * self.flat, 3 * self.flat + 1

    def when_valid(self, plan, flat, action):
        if self.full:
            action()
        else:
            pl.when(plan[self.valid + flat] == 1)(action)


def write_plan(z, partner, plan, count):
    if not z.full:

        def clear(i, carry):
            plan[i] = 0
            return carry

        lax.fori_loop(0, 3 * z.flat, clear, 0)
    for d in range(z.sector):
        count[d] = 0
    factor = -(-(1 << 16) // z.slots)
    assert all(i * factor >> 16 == i // z.slots for i in range(z.sector * z.slots))
    for j in range(z.slots):
        sector = partner[0, j]
        group = (sector * factor) >> 16
        slot = sector - group * z.slots
        distance = jnp.where(group == 0, 0, z.sector - group)
        rank = count[distance]
        count[distance] = rank + 1
        index = distance * z.capacity + rank
        plan[z.source + index] = slot
        plan[z.target + index] = j
        plan[z.valid + index] = 1
    plan[z.core] = lax.axis_index("rep")
    plan[z.chip] = lax.axis_index("env")


def split_copy(source, target, slots, sem):
    step = slots // 4 if slots % 4 == 0 else slots
    copies = []
    for i in range(slots // step):
        part = pl.ds(i * step, step)
        copies.append(pltpu.make_async_copy(source.at[part], target.at[part], sem.at[i]))
    return copies


def load_body(z, partner, vectors, right, plan, *refs):
    rows, block, count, sem = refs[: z.rep], refs[z.rep], refs[-2], refs[-1]
    core = lax.axis_index("rep")
    copies = []
    for s, ref in enumerate(rows):
        mine = vectors.at[lax.rem(core + s, z.rep)]
        copies += split_copy(mine, ref, z.slots, sem.at[s])
    copies += split_copy(right.at[0], block.at[0], z.slots, sem.at[z.rep])
    for copy in copies:
        copy.start()
    write_plan(z, partner, plan, count)
    for copy in copies:
        copy.wait()


def load(z, partner, vectors, right_env):
    row = jax.ShapeDtypeStruct(vectors.shape[1:], jnp.bfloat16)
    plan, *made = pl.pallas_call(
        functools.partial(load_body, z),
        out_shape=[jax.ShapeDtypeStruct((3 * z.flat + 2,), jnp.int32)]
        + [row] * z.rep
        + [jax.ShapeDtypeStruct(right_env.shape, jnp.bfloat16)],
        in_specs=[SMEM, HBM, HBM],
        out_specs=[SMEM] + [VMEM] * (z.rep + 1),
        scratch_shapes=[
            pltpu.SMEM((z.sector,), jnp.int32),
            pltpu.SemaphoreType.DMA((z.rep + 1, 4)),
        ],
        compiler_params=pltpu.CompilerParams(vmem_limit_bytes=LIMIT),
        cost_estimate=BRIEF,
    )(
        partner,
        pltpu.with_memory_space_constraint(vectors, pltpu.HBM),
        pltpu.with_memory_space_constraint(right_env, pltpu.HBM),
    )
    return plan, made[: z.rep], made[z.rep]


def plan_only(z, partner):
    return pl.pallas_call(
        functools.partial(write_plan, z),
        out_shape=jax.ShapeDtypeStruct((3 * z.flat + 2,), jnp.int32),
        in_specs=[SMEM],
        out_specs=SMEM,
        scratch_shapes=[pltpu.SMEM((z.sector,), jnp.int32)],
        compiler_params=pltpu.CompilerParams(vmem_limit_bytes=SMALL),
        cost_estimate=BRIEF,
    )(partner)


def gate(arrays, after):
    def body(*refs):
        pass

    return pl.pallas_call(
        body,
        out_shape=[jax.ShapeDtypeStruct(a.shape, a.dtype) for a in arrays],
        in_specs=[ANY] * (len(arrays) + len(after)),
        out_specs=[ANY] * len(arrays),
        input_output_aliases={i: i for i in range(len(arrays))},
        compiler_params=pltpu.CompilerParams(vmem_limit_bytes=SMALL),
        cost_estimate=BRIEF,
    )(*arrays, *after)


def pick(z, core, place, candidates):
    chosen = candidates[0]
    for s in range(1, z.rep):
        chosen = jnp.where(lax.rem(core + z.rep - s, z.rep) == place, candidates[s], chosen)
    return chosen


def line(ref, core, slot):
    return ref[core, slot] if len(ref.shape) == 4 else ref[slot]


def products_body(z, pieces, spans, *refs):
    refs = list(refs)
    plan = refs.pop(0)
    right = [refs.pop(0) for _ in range(z.rep)]
    rows = [[refs.pop(0) for _ in range(z.rep)] for _ in range(pieces)]
    outs = refs[-len(spans) :]
    core = plan[z.core]
    for (first, count), out in zip(spans, outs):
        for i in range(count):
            slot = plan[z.source + first + i]
            halves = [ref[0, slot] for ref in right]
            parts = [[line(ref, core, slot) for ref in piece] for piece in rows]
            block = jnp.concatenate([pick(z, core, k, halves) for k in range(z.rep)], axis=0)
            lines = jnp.concatenate(
                [pick(z, core, k, part) for part in parts for k in range(z.rep)], axis=0
            )
            out[i] = lax.dot_general(
                lines, block, (((1,), (1,)), ((), ())), preferred_element_type=jnp.float32
            ).astype(jnp.bfloat16)


def products(z, plan, right, rows, spans, after=()):
    pieces = len(rows)
    flat = [ref for piece in rows for ref in piece]
    height = pieces * z.chip_rows
    return pl.pallas_call(
        functools.partial(products_body, z, pieces, spans),
        out_shape=[
            jax.ShapeDtypeStruct((count, height, z.order), jnp.bfloat16) for _, count in spans
        ],
        in_specs=[SMEM] + [VMEM] * (len(right) + len(flat)) + [ANY] * len(after),
        out_specs=[VMEM] * len(spans),
        compiler_params=pltpu.CompilerParams(vmem_limit_bytes=LIMIT),
        cost_estimate=BRIEF,
    )(plan, *right, *flat, *after)


def terms_body(z, spans, chained, last, kept, *refs):
    refs = list(refs)
    plan = refs.pop(0)
    left = [refs.pop(0) for _ in range(z.rep)]
    near = [refs.pop(0) for _ in spans]
    far = [refs.pop(0) for _ in spans]
    vec = [[refs.pop(0) for _ in range(z.rep)] for _ in range(z.env)]
    so_far = refs.pop(0) if chained else None
    own_sums = refs.pop(0) if last else None
    kept = [[refs.pop(0) for _ in range(z.rep - 1)] for _ in range(kept)]
    pbuf, tbuf = refs[-2:]
    dots = refs[-3]
    outs = refs[-3 - z.env * z.rep : -3]
    core, chip = plan[z.core], plan[z.chip]
    total = so_far[...] if chained else jnp.zeros((8, z.order), jnp.float32)
    n = 0
    for d, (first, count, skip) in enumerate(spans):
        for i in range(count):
            slot = plan[z.target + first + i]
            for e in range(z.env):
                place = lax.rem(chip + z.env - e, z.env)
                if e == 0:
                    lines = near[d][skip + i]
                else:
                    lines = far[d][i, (e - 1) * z.chip_rows : e * z.chip_rows]
                pbuf[n, pl.ds(aligned(place, z.chip_rows), z.chip_rows)] = lines
            halves = [ref[0, slot] for ref in left]
            block = jnp.concatenate([pick(z, core, k, halves) for k in range(z.rep)], axis=0)
            tbuf[n] = jnp.dot(block, pbuf[n], preferred_element_type=jnp.float32).astype(
                jnp.bfloat16
            )
            folded = jnp.zeros(total.shape, jnp.float32)
            for e in range(z.env):
                for s in range(z.rep):
                    place = lax.rem(chip + e, z.env) * z.rep + lax.rem(core + s, z.rep)
                    term = tbuf[n, pl.ds(aligned(place, z.own_rows), z.own_rows)]
                    if last and e + s:
                        outs[e * z.rep + s][n * z.own_rows : (n + 1) * z.own_rows] = term
                    else:
                        outs[e * z.rep + s][n] = term
                    lines = line(vec[(z.env - e) % z.env][(z.rep - s) % z.rep], core, slot)
                    both = lines.astype(jnp.float32) * term.astype(jnp.float32)
                    folded += jnp.sum(both.reshape(-1, *total.shape), axis=0)
            if not z.full:
                folded = jnp.where(plan[z.valid + first + i] == 1, folded, 0.0)
            total += folded
            n += 1
    if not last:
        dots[...] = total
        return
    row = lax.broadcasted_iota(jnp.int32, dots.shape, 0)
    column = lax.broadcasted_iota(jnp.int32, dots.shape, 1)
    value = jnp.where(column == core, jnp.sum(total), 0.0)
    for v in range(z.batch):
        value += jnp.where(column == v, own_sums[v], 0.0)
    split = jnp.zeros(dots.shape, jnp.float32)
    for k in range(3):
        piece = value.astype(jnp.bfloat16).astype(jnp.float32)
        split = jnp.where(row == k, piece, split)
        value = value - piece
    split = split.astype(jnp.bfloat16)
    dots[...] = split
    at = n * z.own_rows
    for blocks in kept:
        for s, block in enumerate(blocks):
            for i in range(block.shape[0]):
                outs[1 + s][at + i * z.own_rows : at + (i + 1) * z.own_rows] = block[i]
        at += blocks[0].shape[0] * z.own_rows
    for out in outs[1:]:
        out[out.shape[0] - TAIL :] = split


def terms(z, plan, left, near, far, vec, spans, so_far=None, own_sums=None, kept=(), after=()):
    count = sum(span[1] for span in spans)
    flat = [ref for piece in vec for ref in piece]
    shapes = [(count, z.own_rows, z.order)] * (z.env * z.rep)
    whole = (count, z.order, z.order)
    last = own_sums is not None
    sums = jax.ShapeDtypeStruct((8, z.order), jnp.float32)
    if last:
        shapes[1:] = [(count * z.own_rows + TAIL, z.order)] * (z.env * z.rep - 1)
        more = sum(blocks[0].shape[0] for blocks in kept)
        shapes[1 : z.rep] = [((count + more) * z.own_rows + TAIL, z.order)] * (z.rep - 1)
        sums = jax.ShapeDtypeStruct((TAIL, z.order), jnp.bfloat16)
    extra = [] if so_far is None else [so_far]
    specs = [VMEM] * len(extra)
    if last:
        extra.append(own_sums)
        specs.append(SMEM)
    extra += [block for blocks in kept for block in blocks]
    specs += [VMEM] * (len(extra) - len(specs))
    *made, dots = pl.pallas_call(
        functools.partial(terms_body, z, spans, so_far is not None, last, len(kept)),
        out_shape=[jax.ShapeDtypeStruct(shape, jnp.bfloat16) for shape in shapes] + [sums],
        in_specs=[SMEM]
        + [VMEM] * (len(left) + len(near) + len(far) + len(flat))
        + specs
        + [ANY] * len(after),
        out_specs=[VMEM] * (len(shapes) + 1),
        scratch_shapes=[pltpu.VMEM(whole, jnp.bfloat16), pltpu.VMEM(whole, jnp.bfloat16)],
        compiler_params=pltpu.CompilerParams(vmem_limit_bytes=LIMIT),
        cost_estimate=BRIEF,
    )(plan, *left, *near, *far, *flat, *extra, *after)
    return made, dots


def for_terms(z, plans, parts, spans, action):
    n = 0
    for first, count, _ in spans:
        for i in range(count):
            for e, plan in enumerate(plans):

                def act():
                    blocks = []
                    for ref, skip in parts[e]:
                        if len(ref.shape) == 3:
                            blocks.append(lambda ref=ref: ref[n])
                        else:
                            rows = slice((skip + n) * z.own_rows, (skip + n + 1) * z.own_rows)
                            blocks.append(lambda ref=ref, rows=rows: ref[rows])
                    action(plan[z.target + first + i], blocks)

                z.when_valid(plan, first + i, act)
            n += 1


def add_terms(z, plans, image, parts, spans):
    core = plans[0][z.core]

    def add(slot, blocks):
        for s, block in enumerate(blocks):
            v = lax.rem(core + z.rep - s, z.rep)
            image[v, slot] += block().astype(jnp.float32)

    for_terms(z, plans, parts, spans, add)


def gather_body(z, chunks, skip, *refs):
    refs = list(refs)
    plans = [refs.pop(0) for _ in range(z.env)]
    energy, vectors = refs.pop(0), refs.pop(0)
    so_far, image, sem = refs[-3:]

    def start(j, carry):
        for v in range(z.batch):
            so_far[v, j] = energy[j] * vectors[v, j].astype(jnp.float32)
        return carry

    lax.fori_loop(0, z.slots, start, 0, unroll=2)
    joined = [refs.pop(0) for _ in range(z.rep - 1)]
    for spans in chunks:
        parts = [[(refs.pop(0), 0)] + [(ref, skip) for ref in joined]]
        for _ in range(1, z.env):
            parts.append([(refs.pop(0), 0) for _ in range(z.rep)])
        add_terms(z, plans, so_far, parts, spans)
        skip += sum(span[1] for span in spans)
    copies = []
    for v in range(z.batch):
        copies += split_copy(so_far.at[v], image.at[v], z.slots, sem.at[v])
    for copy in copies:
        copy.start()
    for copy in copies:
        copy.wait()


def gather_terms(z, plans, energy, vectors, joined, skip, parts, chunks, after=()):
    flat = [*joined]
    for chunk in parts:
        flat += [chunk[0][0]] + [ref for piece in chunk[1:] for ref in piece]
    shape = jax.ShapeDtypeStruct(vectors.shape, jnp.float32)
    return pl.pallas_call(
        functools.partial(gather_body, z, chunks, skip),
        out_shape=[shape, pltpu.HBM(vectors.shape, jnp.float32)],
        in_specs=[SMEM] * (z.env + 1) + [VMEM] * (1 + len(flat)) + [ANY] * len(after),
        out_specs=[VMEM, HBM],
        scratch_shapes=[pltpu.SemaphoreType.DMA((z.batch, 4))],
        compiler_params=pltpu.CompilerParams(vmem_limit_bytes=LIMIT),
        cost_estimate=BRIEF,
    )(*plans, energy, vectors, *flat, *after)


def image_body(z, spans, *refs):
    refs = list(refs)
    plans = [refs.pop(0) for _ in range(z.env)]
    so_far = refs.pop(0)
    parts = [[(refs.pop(0), 0) for _ in range(z.rep)] for _ in range(z.env)]
    image, token, sums, sem = refs[-4:]
    token[...] = jnp.zeros_like(token)

    def take(slot, blocks):
        for v in range(z.batch):
            sums[v, slot] = so_far[v, slot]

    for_terms(z, plans, parts, spans, take)
    add_terms(z, plans, sums, parts, spans)
    for wait in (False, True):
        used = []

        def put(slot, blocks):
            for v in range(z.batch):
                copy = pltpu.make_async_copy(
                    sums.at[v, slot], image.at[v, slot], sem.at[len(used), v]
                )
                if wait:
                    copy.wait()
                else:
                    copy.start()
            used.append(slot)

        for_terms(z, plans, parts, spans, put)


def make_image(z, plans, so_far, image, parts, spans):
    flat = [ref for piece in parts for ref in piece]
    count = z.env * sum(span[1] for span in spans)
    return pl.pallas_call(
        functools.partial(image_body, z, spans),
        out_shape=[
            pltpu.HBM(image.shape, jnp.float32),
            jax.ShapeDtypeStruct((8, 128), jnp.float32),
        ],
        in_specs=[SMEM] * z.env + [VMEM] * (1 + len(flat)) + [HBM],
        out_specs=[HBM, VMEM],
        input_output_aliases={z.env + 1 + len(flat): 0},
        scratch_shapes=[
            pltpu.VMEM(image.shape, jnp.float32),
            pltpu.SemaphoreType.DMA((count, z.batch)),
        ],
        compiler_params=pltpu.CompilerParams(vmem_limit_bytes=LIMIT),
        cost_estimate=BRIEF,
    )(*plans, so_far, *flat, image)


def in_order(parts, places, count):
    total = 0.0
    for place in range(count):
        for part, at in zip(parts, places):
            total = total + jnp.where(at == place, part, 0.0)
    return total


def chips_body(z, count, plan, own, *refs):
    arrived, out = refs[:count], refs[-1]
    core, chip = plan[z.core], plan[z.chip]
    parts, places = [], []
    for e in range(z.env):
        for s in range(z.rep):
            ref = arrived[e * z.rep + s - 1] if e + s else own
            tail = ref[ref.shape[0] - TAIL :].astype(jnp.float32)
            parts.append(tail[0:1] + tail[1:2] + tail[2:3])
            at = lax.rem(chip + z.env - e, z.env) * z.rep + lax.rem(core + z.rep - s, z.rep)
            places.append(at)
    total = in_order(parts, places, z.env * z.rep)
    out[...] = jnp.broadcast_to(total, out.shape)


def chip_sums(z, plan, own, arrived, after):
    return pl.pallas_call(
        functools.partial(chips_body, z, len(arrived)),
        out_shape=jax.ShapeDtypeStruct((8, z.order), jnp.float32),
        in_specs=[SMEM] + [VMEM] * (1 + len(arrived)) + [ANY] * len(after),
        out_specs=VMEM,
        compiler_params=pltpu.CompilerParams(vmem_limit_bytes=SMALL),
        cost_estimate=BRIEF,
    )(plan, own, *arrived, *after)


def mean_body(z, scale, ours, theirs, *refs):
    out = refs[-1]
    total = ours[0:1] + theirs[0:1]
    out[...] = total[:, : out.shape[1]] * scale


def mean_over_sectors(z, array, entries, after):
    step = 1
    while 2 * step < z.sector:
        array = array + exchange(z, array, step)
        step *= 2
    made = pl.pallas_call(
        functools.partial(mean_body, z, 1.0 / entries),
        out_shape=jax.ShapeDtypeStruct((1, z.batch), jnp.float32),
        in_specs=[VMEM] * 2 + [ANY] * len(after),
        out_specs=VMEM,
        compiler_params=pltpu.CompilerParams(vmem_limit_bytes=SMALL),
        cost_estimate=BRIEF,
    )(array, exchange(z, array, step), *after)
    return made.reshape(z.batch)


def shift(array, axis, size, step):
    return lax.ppermute(array, axis, [(i, (i + step) % size) for i in range(size)])


def shift_both(z, array, e, s):
    perm = []
    for x in range(z.env):
        for c in range(z.rep):
            perm.append((x * z.rep + c, (x + e) % z.env * z.rep + (c + s) % z.rep))
    return lax.ppermute(array, ("env", "rep"), perm)


def exchange(z, array, step):
    return lax.ppermute(array, "sector", [(i, i ^ step) for i in range(z.sector)])


def on_device(vectors, left_env, right_env, energy, partner):
    z = Sizes(vectors, left_env)
    each = z.sector // 4
    span = z.capacity

    def spans_of(g, low=0, high=span):
        return [((g * each + d) * span + low, high - low, low) for d in range(each)]

    chunks = {g: spans_of(g) for g in range(4)}
    cut = 2 * span // 3
    chunks[2], chunks[4] = spans_of(2, 0, cut), spans_of(2, cut, span)

    def around(array):
        return [array] + [shift(array, "rep", z.rep, s) for s in range(1, z.rep)]

    def across(arrays, g):
        steps = [g * each + d for d in range(each)]
        return [shift(a, "sector", z.sector, k) if k else a for a, k in zip(arrays, steps)]

    partners = [shift(partner, "env", z.env, e) for e in range(1, z.env)]
    vector_others = around(vectors)[1:]
    right_others = around(right_env)[1:]
    left = around(left_env)
    plan, own, right_own = load(z, partner, vectors, right_env)
    own = gate(own, partners)
    plans = [plan] + [plan_only(z, other) for other in partners]
    right = [right_own] + right_others
    near_rows = [own[0]] + vector_others
    vec = [near_rows]
    for e in range(1, z.env):
        vec.append([shift_both(z, own[s], e, s) for s in range(z.rep)])
    def near_products(g, after):
        return products(z, plan, right, [near_rows], [c[:2] for c in spans_of(g)], after)

    def far_products(g, after):
        return products(z, plan, right, vec[1:], [c[:2] for c in chunks[g]], after)

    near, far, parts = {}, {}, {}
    spans = [piece[:2] for g in (1, 3) for piece in chunks[g]]
    made = products(z, plan, right, [near_rows], spans)
    near[1], near[3] = across(made[:each], 1), across(made[each:], 3)
    made = near_products(2, (made[0], *left[1:]))
    near[2] = across(made, 2)

    def send_terms(g, so_far, own_sums, kept, after):
        made, folded = terms(
            z, plan, left, near[2 if g == 4 else g], far[g], vec, chunks[g], so_far,
            own_sums, kept, after
        )
        first = made[: z.rep]
        if own_sums is not None:
            first[1:] = [shift(first[s], "rep", z.rep, s) for s in range(1, z.rep)]
        parts[g] = [first]
        for e in range(1, z.env):
            parts[g].append([shift_both(z, made[e * z.rep + s], e, s) for s in range(z.rep)])
        return folded

    def arrived(g):
        return [part for piece in parts[g][1:] for part in piece]

    near[0] = near_products(0, made[:1])
    far1 = far_products(1, (near[0][0], *plans[1:]))
    far1 = gate(far1, [*near[1], *near[3]])
    far[1] = across(far1, 1)
    far[0] = far_products(0, far1[:1])
    dots = send_terms(0, None, None, (), ())
    far3 = far_products(3, (dots,))
    far2 = far_products(2, far3[:1])
    far4 = far_products(4, far2[:1])
    far3 = gate(far3, [far4[0], *near[2], *arrived(0)[:1]])
    far[3] = across(far3, 3)
    far2 = gate(far2, [far3[0], *far[1]])
    far[2] = across(far2, 2)
    far4 = gate(far4, far[2])
    far[4] = across(far4, 2)
    dots = send_terms(1, dots, None, (), (far2[0], *arrived(0)))
    dots = send_terms(3, dots, None, (), arrived(1)[:1])
    own_block = vectors.astype(jnp.float32)
    own_sums = jnp.sum(energy[None, :, None, None] * own_block * own_block, axis=(1, 2, 3))
    dots = send_terms(2, dots, None, (), [far4[0]] + arrived(1)[1:] + arrived(3)[:1])
    early = (0, 1, 3, 2)
    kept = [parts[g][0][1:] for g in early]
    dots = send_terms(4, dots, own_sums, kept, arrived(3)[1:] + arrived(2))
    so_far, image = gather_terms(
        z,
        plans,
        energy,
        vectors,
        parts[4][0][1:],
        sum(piece[1] for piece in chunks[4]),
        [parts[g] for g in early],
        [chunks[g] for g in early],
        (dots,),
    )
    sums = chip_sums(z, plan, dots, parts[4][0][1:] + arrived(4), (so_far,))
    image, token = make_image(z, plans, so_far, image, parts[4], chunks[4])
    entries = z.slots * z.sector * z.order * z.order
    return (image, mean_over_sectors(z, sums, entries, (token,)))


def solution(mesh):
    return jax.shard_map(
        on_device,
        mesh=mesh,
        in_specs=(
            P(None, ("groups", "sector"), ("env", "rep"), None),
            P("env", ("groups", "sector"), "rep", None),
            P("env", ("groups", "sector"), "rep", None),
            P(("groups", "sector")),
            P("env", "groups"),
        ),
        out_specs=(P(None, ("groups", "sector"), ("env", "rep"), None), P("groups")),
        check_vma=False,
    )
```

```python
import functools

import jax
import jax.numpy as jnp
from jax import lax
from jax.experimental import pallas as pl
from jax.experimental.pallas import tpu as pltpu
from jax.sharding import PartitionSpec as P

ANY = pl.BlockSpec(memory_space=pl.ANY)
HBM = pl.BlockSpec(memory_space=pltpu.HBM)
SMEM = pl.BlockSpec(memory_space=pltpu.SMEM)
VMEM = pl.BlockSpec(memory_space=pltpu.VMEM)
LIMIT = 12 * 1024 * 1024
SMALL = 2 * 1024 * 1024
TAIL = 16
BRIEF = pl.CostEstimate(flops=0, bytes_accessed=0, transcendentals=0)


def aligned(index, size):
    return pl.multiple_of(index * size, size)


class Sizes:
    def __init__(self, vectors, left_env):
        self.env = lax.axis_size("env")
        self.rep = lax.axis_size("rep")
        self.sector = lax.axis_size("sector")
        self.batch, self.slots, self.own_rows, self.order = vectors.shape
        assert self.batch == self.rep and self.sector % 4 == 0
        self.half = left_env.shape[2]
        self.chip_rows = self.own_rows * self.rep
        self.capacity = 2 * ((self.slots + 2 * self.sector - 1) // (2 * self.sector))
        self.flat = self.sector * self.capacity
        self.full = self.flat == self.slots
        self.source, self.target, self.valid = 0, self.flat, 2 * self.flat
        self.core, self.chip = 3 * self.flat, 3 * self.flat + 1

    def when_valid(self, plan, flat, action):
        if self.full:
            action()
        else:
            pl.when(plan[self.valid + flat] == 1)(action)


def write_plan(z, partner, plan, count):
    if not z.full:

        def clear(i, carry):
            plan[i] = 0
            return carry

        lax.fori_loop(0, 3 * z.flat, clear, 0)
    for d in range(z.sector):
        count[d] = 0
    factor = -(-(1 << 16) // z.slots)
    assert all(i * factor >> 16 == i // z.slots for i in range(z.sector * z.slots))
    for j in range(z.slots):
        sector = partner[0, j]
        group = (sector * factor) >> 16
        slot = sector - group * z.slots
        distance = jnp.where(group == 0, 0, z.sector - group)
        rank = count[distance]
        count[distance] = rank + 1
        index = distance * z.capacity + rank
        plan[z.source + index] = slot
        plan[z.target + index] = j
        plan[z.valid + index] = 1
    plan[z.core] = lax.axis_index("rep")
    plan[z.chip] = lax.axis_index("env")


def split_copy(source, target, slots, sem):
    step = slots // 4 if slots % 4 == 0 else slots
    copies = []
    for i in range(slots // step):
        part = pl.ds(i * step, step)
        copies.append(pltpu.make_async_copy(source.at[part], target.at[part], sem.at[i]))
    return copies


def load_body(z, partner, vectors, right, plan, *refs):
    rows, block, count, sem = refs[: z.rep], refs[z.rep], refs[-2], refs[-1]
    core = lax.axis_index("rep")
    copies = []
    for s, ref in enumerate(rows):
        mine = vectors.at[lax.rem(core + s, z.rep)]
        copies += split_copy(mine, ref, z.slots, sem.at[s])
    copies += split_copy(right.at[0], block.at[0], z.slots, sem.at[z.rep])
    for copy in copies:
        copy.start()
    write_plan(z, partner, plan, count)
    for copy in copies:
        copy.wait()


def load(z, partner, vectors, right_env):
    row = jax.ShapeDtypeStruct(vectors.shape[1:], jnp.bfloat16)
    plan, *made = pl.pallas_call(
        functools.partial(load_body, z),
        out_shape=[jax.ShapeDtypeStruct((3 * z.flat + 2,), jnp.int32)]
        + [row] * z.rep
        + [jax.ShapeDtypeStruct(right_env.shape, jnp.bfloat16)],
        in_specs=[SMEM, HBM, HBM],
        out_specs=[SMEM] + [VMEM] * (z.rep + 1),
        scratch_shapes=[
            pltpu.SMEM((z.sector,), jnp.int32),
            pltpu.SemaphoreType.DMA((z.rep + 1, 4)),
        ],
        compiler_params=pltpu.CompilerParams(vmem_limit_bytes=LIMIT),
        cost_estimate=BRIEF,
    )(
        partner,
        pltpu.with_memory_space_constraint(vectors, pltpu.HBM),
        pltpu.with_memory_space_constraint(right_env, pltpu.HBM),
    )
    return plan, made[: z.rep], made[z.rep]


def plan_only(z, partner):
    return pl.pallas_call(
        functools.partial(write_plan, z),
        out_shape=jax.ShapeDtypeStruct((3 * z.flat + 2,), jnp.int32),
        in_specs=[SMEM],
        out_specs=SMEM,
        scratch_shapes=[pltpu.SMEM((z.sector,), jnp.int32)],
        compiler_params=pltpu.CompilerParams(vmem_limit_bytes=SMALL),
        cost_estimate=BRIEF,
    )(partner)


def gate(arrays, after):
    def body(*refs):
        pass

    return pl.pallas_call(
        body,
        out_shape=[jax.ShapeDtypeStruct(a.shape, a.dtype) for a in arrays],
        in_specs=[ANY] * (len(arrays) + len(after)),
        out_specs=[ANY] * len(arrays),
        input_output_aliases={i: i for i in range(len(arrays))},
        compiler_params=pltpu.CompilerParams(vmem_limit_bytes=SMALL),
        cost_estimate=BRIEF,
    )(*arrays, *after)


def pick(z, core, place, candidates):
    chosen = candidates[0]
    for s in range(1, z.rep):
        chosen = jnp.where(lax.rem(core + z.rep - s, z.rep) == place, candidates[s], chosen)
    return chosen


def line(ref, core, slot):
    return ref[core, slot] if len(ref.shape) == 4 else ref[slot]


def products_body(z, pieces, spans, *refs):
    refs = list(refs)
    plan = refs.pop(0)
    right = [refs.pop(0) for _ in range(z.rep)]
    rows = [[refs.pop(0) for _ in range(z.rep)] for _ in range(pieces)]
    outs = refs[-len(spans) :]
    core = plan[z.core]
    for (first, count), out in zip(spans, outs):
        for i in range(count):
            slot = plan[z.source + first + i]
            halves = [ref[0, slot] for ref in right]
            parts = [[line(ref, core, slot) for ref in piece] for piece in rows]
            block = jnp.concatenate([pick(z, core, k, halves) for k in range(z.rep)], axis=0)
            lines = jnp.concatenate(
                [pick(z, core, k, part) for part in parts for k in range(z.rep)], axis=0
            )
            out[i] = lax.dot_general(
                lines, block, (((1,), (1,)), ((), ())), preferred_element_type=jnp.float32
            ).astype(jnp.bfloat16)


def products(z, plan, right, rows, spans, after=()):
    pieces = len(rows)
    flat = [ref for piece in rows for ref in piece]
    height = pieces * z.chip_rows
    return pl.pallas_call(
        functools.partial(products_body, z, pieces, spans),
        out_shape=[
            jax.ShapeDtypeStruct((count, height, z.order), jnp.bfloat16) for _, count in spans
        ],
        in_specs=[SMEM] + [VMEM] * (len(right) + len(flat)) + [ANY] * len(after),
        out_specs=[VMEM] * len(spans),
        compiler_params=pltpu.CompilerParams(vmem_limit_bytes=LIMIT),
        cost_estimate=BRIEF,
    )(plan, *right, *flat, *after)


def terms_body(z, spans, chained, last, kept, *refs):
    refs = list(refs)
    plan = refs.pop(0)
    left = [refs.pop(0) for _ in range(z.rep)]
    near = [refs.pop(0) for _ in spans]
    far = [refs.pop(0) for _ in spans]
    vec = [[refs.pop(0) for _ in range(z.rep)] for _ in range(z.env)]
    so_far = refs.pop(0) if chained else None
    own_sums = refs.pop(0) if last else None
    kept = [[refs.pop(0) for _ in range(z.rep - 1)] for _ in range(kept)]
    pbuf, tbuf = refs[-2:]
    dots = refs[-3]
    outs = refs[-3 - z.env * z.rep : -3]
    core, chip = plan[z.core], plan[z.chip]
    total = so_far[...] if chained else jnp.zeros((8, z.order), jnp.float32)
    n = 0
    for d, (first, count, skip) in enumerate(spans):
        for i in range(count):
            slot = plan[z.target + first + i]
            for e in range(z.env):
                place = lax.rem(chip + z.env - e, z.env)
                if e == 0:
                    lines = near[d][skip + i]
                else:
                    lines = far[d][i, (e - 1) * z.chip_rows : e * z.chip_rows]
                pbuf[n, pl.ds(aligned(place, z.chip_rows), z.chip_rows)] = lines
            halves = [ref[0, slot] for ref in left]
            block = jnp.concatenate([pick(z, core, k, halves) for k in range(z.rep)], axis=0)
            tbuf[n] = jnp.dot(block, pbuf[n], preferred_element_type=jnp.float32).astype(
                jnp.bfloat16
            )
            folded = jnp.zeros(total.shape, jnp.float32)
            for e in range(z.env):
                for s in range(z.rep):
                    place = lax.rem(chip + e, z.env) * z.rep + lax.rem(core + s, z.rep)
                    term = tbuf[n, pl.ds(aligned(place, z.own_rows), z.own_rows)]
                    if last and e + s:
                        outs[e * z.rep + s][n * z.own_rows : (n + 1) * z.own_rows] = term
                    else:
                        outs[e * z.rep + s][n] = term
                    lines = line(vec[(z.env - e) % z.env][(z.rep - s) % z.rep], core, slot)
                    both = lines.astype(jnp.float32) * term.astype(jnp.float32)
                    folded += jnp.sum(both.reshape(-1, *total.shape), axis=0)
            if not z.full:
                folded = jnp.where(plan[z.valid + first + i] == 1, folded, 0.0)
            total += folded
            n += 1
    if not last:
        dots[...] = total
        return
    row = lax.broadcasted_iota(jnp.int32, dots.shape, 0)
    column = lax.broadcasted_iota(jnp.int32, dots.shape, 1)
    value = jnp.where(column == core, jnp.sum(total), 0.0)
    for v in range(z.batch):
        value += jnp.where(column == v, own_sums[v], 0.0)
    split = jnp.zeros(dots.shape, jnp.float32)
    for k in range(3):
        piece = value.astype(jnp.bfloat16).astype(jnp.float32)
        split = jnp.where(row == k, piece, split)
        value = value - piece
    split = split.astype(jnp.bfloat16)
    dots[...] = split
    at = n * z.own_rows
    for blocks in kept:
        for s, block in enumerate(blocks):
            for i in range(block.shape[0]):
                outs[1 + s][at + i * z.own_rows : at + (i + 1) * z.own_rows] = block[i]
        at += blocks[0].shape[0] * z.own_rows
    for out in outs[1:]:
        out[out.shape[0] - TAIL :] = split


def terms(z, plan, left, near, far, vec, spans, so_far=None, own_sums=None, kept=(), after=()):
    count = sum(span[1] for span in spans)
    flat = [ref for piece in vec for ref in piece]
    shapes = [(count, z.own_rows, z.order)] * (z.env * z.rep)
    whole = (count, z.order, z.order)
    last = own_sums is not None
    sums = jax.ShapeDtypeStruct((8, z.order), jnp.float32)
    if last:
        shapes[1:] = [(count * z.own_rows + TAIL, z.order)] * (z.env * z.rep - 1)
        more = sum(blocks[0].shape[0] for blocks in kept)
        shapes[1 : z.rep] = [((count + more) * z.own_rows + TAIL, z.order)] * (z.rep - 1)
        sums = jax.ShapeDtypeStruct((TAIL, z.order), jnp.bfloat16)
    extra = [] if so_far is None else [so_far]
    specs = [VMEM] * len(extra)
    if last:
        extra.append(own_sums)
        specs.append(SMEM)
    extra += [block for blocks in kept for block in blocks]
    specs += [VMEM] * (len(extra) - len(specs))
    *made, dots = pl.pallas_call(
        functools.partial(terms_body, z, spans, so_far is not None, last, len(kept)),
        out_shape=[jax.ShapeDtypeStruct(shape, jnp.bfloat16) for shape in shapes] + [sums],
        in_specs=[SMEM]
        + [VMEM] * (len(left) + len(near) + len(far) + len(flat))
        + specs
        + [ANY] * len(after),
        out_specs=[VMEM] * (len(shapes) + 1),
        scratch_shapes=[pltpu.VMEM(whole, jnp.bfloat16), pltpu.VMEM(whole, jnp.bfloat16)],
        compiler_params=pltpu.CompilerParams(vmem_limit_bytes=LIMIT),
        cost_estimate=BRIEF,
    )(plan, *left, *near, *far, *flat, *extra, *after)
    return made, dots


def for_terms(z, plans, parts, spans, action):
    n = 0
    for first, count, _ in spans:
        for i in range(count):
            for e, plan in enumerate(plans):

                def act():
                    blocks = []
                    for ref, skip in parts[e]:
                        if len(ref.shape) == 3:
                            blocks.append(lambda ref=ref: ref[n])
                        else:
                            rows = slice((skip + n) * z.own_rows, (skip + n + 1) * z.own_rows)
                            blocks.append(lambda ref=ref, rows=rows: ref[rows])
                    action(plan[z.target + first + i], blocks)

                z.when_valid(plan, first + i, act)
            n += 1


def add_terms(z, plans, image, parts, spans, kinds):
    core = plans[0][z.core]

    def add(slot, blocks):
        for s in kinds:
            block = blocks[s]
            v = lax.rem(core + z.rep - s, z.rep)
            image[v, slot] += block().astype(jnp.float32)

    for_terms(z, plans, parts, spans, add)


def gather_body(z, chunks, skip, *refs):
    refs = list(refs)
    plans = [refs.pop(0) for _ in range(z.env)]
    energy, vectors = refs.pop(0), refs.pop(0)
    so_far, image, sem = refs[-3:]

    core = plans[0][z.core]
    joined = [refs.pop(0) for _ in range(z.rep - 1)]
    chunk_parts = []
    for spans in chunks:
        parts = [[(refs.pop(0), 0)] + [(ref, skip) for ref in joined]]
        for _ in range(1, z.env):
            parts.append([(refs.pop(0), 0) for _ in range(z.rep)])
        chunk_parts.append(parts)
        skip += sum(span[1] for span in spans)
    copies = []
    for s in range(z.rep):
        v = lax.rem(core + z.rep - s, z.rep)

        def start(j, carry):
            so_far[v, j] = energy[j] * vectors[v, j].astype(jnp.float32)
            return carry

        lax.fori_loop(0, z.slots, start, 0, unroll=4)
        for parts, spans in zip(chunk_parts, chunks):
            add_terms(z, plans, so_far, parts, spans, (s,))
        made = split_copy(so_far.at[v], image.at[v], z.slots, sem.at[s])
        for copy in made:
            copy.start()
        copies += made
    for copy in copies:
        copy.wait()


def gather_terms(z, plans, energy, vectors, joined, skip, parts, chunks, after=()):
    flat = [*joined]
    for chunk in parts:
        flat += [chunk[0][0]] + [ref for piece in chunk[1:] for ref in piece]
    shape = jax.ShapeDtypeStruct(vectors.shape, jnp.float32)
    return pl.pallas_call(
        functools.partial(gather_body, z, chunks, skip),
        out_shape=[shape, pltpu.HBM(vectors.shape, jnp.float32)],
        in_specs=[SMEM] * (z.env + 1) + [VMEM] * (1 + len(flat)) + [ANY] * len(after),
        out_specs=[VMEM, HBM],
        scratch_shapes=[pltpu.SemaphoreType.DMA((z.batch, 4))],
        compiler_params=pltpu.CompilerParams(vmem_limit_bytes=LIMIT),
        cost_estimate=BRIEF,
    )(*plans, energy, vectors, *flat, *after)


def image_body(z, spans, *refs):
    refs = list(refs)
    plans = [refs.pop(0) for _ in range(z.env)]
    so_far = refs.pop(0)
    parts = [[(refs.pop(0), 0) for _ in range(z.rep)] for _ in range(z.env)]
    image, token, sums, sem = refs[-4:]
    token[...] = jnp.zeros_like(token)

    def take(slot, blocks):
        for v in range(z.batch):
            sums[v, slot] = so_far[v, slot]

    for_terms(z, plans, parts, spans, take)
    add_terms(z, plans, sums, parts, spans, range(z.rep))
    for wait in (False, True):
        used = []

        def put(slot, blocks):
            for v in range(z.batch):
                copy = pltpu.make_async_copy(
                    sums.at[v, slot], image.at[v, slot], sem.at[len(used), v]
                )
                if wait:
                    copy.wait()
                else:
                    copy.start()
            used.append(slot)

        for_terms(z, plans, parts, spans, put)


def make_image(z, plans, so_far, image, parts, spans):
    flat = [ref for piece in parts for ref in piece]
    count = z.env * sum(span[1] for span in spans)
    return pl.pallas_call(
        functools.partial(image_body, z, spans),
        out_shape=[
            pltpu.HBM(image.shape, jnp.float32),
            jax.ShapeDtypeStruct((8, 128), jnp.float32),
        ],
        in_specs=[SMEM] * z.env + [VMEM] * (1 + len(flat)) + [HBM],
        out_specs=[HBM, VMEM],
        input_output_aliases={z.env + 1 + len(flat): 0},
        scratch_shapes=[
            pltpu.VMEM(image.shape, jnp.float32),
            pltpu.SemaphoreType.DMA((count, z.batch)),
        ],
        compiler_params=pltpu.CompilerParams(vmem_limit_bytes=LIMIT),
        cost_estimate=BRIEF,
    )(*plans, so_far, *flat, image)


def in_order(parts, places, count):
    total = 0.0
    for place in range(count):
        for part, at in zip(parts, places):
            total = total + jnp.where(at == place, part, 0.0)
    return total


def chips_body(z, count, plan, own, *refs):
    arrived, out = refs[:count], refs[-1]
    core, chip = plan[z.core], plan[z.chip]
    parts, places = [], []
    for e in range(z.env):
        for s in range(z.rep):
            ref = arrived[e * z.rep + s - 1] if e + s else own
            tail = ref[ref.shape[0] - TAIL :].astype(jnp.float32)
            parts.append(tail[0:1] + tail[1:2] + tail[2:3])
            at = lax.rem(chip + z.env - e, z.env) * z.rep + lax.rem(core + z.rep - s, z.rep)
            places.append(at)
    total = in_order(parts, places, z.env * z.rep)
    out[...] = jnp.broadcast_to(total, out.shape)


def chip_sums(z, plan, own, arrived, after):
    return pl.pallas_call(
        functools.partial(chips_body, z, len(arrived)),
        out_shape=jax.ShapeDtypeStruct((8, z.order), jnp.float32),
        in_specs=[SMEM] + [VMEM] * (1 + len(arrived)) + [ANY] * len(after),
        out_specs=VMEM,
        compiler_params=pltpu.CompilerParams(vmem_limit_bytes=SMALL),
        cost_estimate=BRIEF,
    )(plan, own, *arrived, *after)


def mean_body(z, count, scale, *refs):
    out = refs[-1]
    me = lax.axis_index("sector")
    parts = [ref[0:1] for ref in refs[:count]]
    total = parts[0]
    if count > 1:
        places = [lax.rem(me + z.sector - step, z.sector) for step in range(count)]
        total = in_order(parts, places, count)
    out[...] = total[:, : out.shape[1]] * scale


def mean_over_sectors(z, array, entries, after):
    held = [array]
    if z.sector <= 4:
        held += [shift(array, "sector", z.sector, step) for step in range(1, z.sector)]
    else:
        held = [total_over(array, "sector")]
    made = pl.pallas_call(
        functools.partial(mean_body, z, len(held), 1.0 / entries),
        out_shape=jax.ShapeDtypeStruct((1, z.batch), jnp.float32),
        in_specs=[VMEM] * len(held) + [ANY] * len(after),
        out_specs=VMEM,
        compiler_params=pltpu.CompilerParams(vmem_limit_bytes=SMALL),
        cost_estimate=BRIEF,
    )(*held, *after)
    return made.reshape(z.batch)


def shift(array, axis, size, step):
    return lax.ppermute(array, axis, [(i, (i + step) % size) for i in range(size)])


def shift_both(z, array, e, s):
    perm = []
    for x in range(z.env):
        for c in range(z.rep):
            perm.append((x * z.rep + c, (x + e) % z.env * z.rep + (c + s) % z.rep))
    return lax.ppermute(array, ("env", "rep"), perm)


def total_over(array, axis):
    size = lax.axis_size(axis)
    if size & (size - 1):
        return lax.psum(array, axis)
    step = 1
    while step < size:
        array = array + lax.ppermute(array, axis, [(i, i ^ step) for i in range(size)])
        step *= 2
    return array


def on_device(vectors, left_env, right_env, energy, partner):
    z = Sizes(vectors, left_env)
    each = z.sector // 4
    span = z.capacity

    def spans_of(g, low=0, high=span):
        return [((g * each + d) * span + low, high - low, low) for d in range(each)]

    chunks = {g: spans_of(g) for g in range(4)}
    cut = 2 * span // 3
    chunks[2], chunks[4] = spans_of(2, 0, cut), spans_of(2, cut, span)

    def around(array):
        return [array] + [shift(array, "rep", z.rep, s) for s in range(1, z.rep)]

    def across(arrays, g):
        steps = [g * each + d for d in range(each)]
        return [shift(a, "sector", z.sector, k) if k else a for a, k in zip(arrays, steps)]

    partners = [shift(partner, "env", z.env, e) for e in range(1, z.env)]
    vector_others = around(vectors)[1:]
    right_others = around(right_env)[1:]
    left = around(left_env)
    plan, own, right_own = load(z, partner, vectors, right_env)
    own = gate(own, partners)
    plans = [plan] + [plan_only(z, other) for other in partners]
    right = [right_own] + right_others
    near_rows = [own[0]] + vector_others
    vec = [near_rows]
    for e in range(1, z.env):
        vec.append([shift_both(z, own[s], e, s) for s in range(z.rep)])
    def near_products(g, after):
        return products(z, plan, right, [near_rows], [c[:2] for c in spans_of(g)], after)

    def far_products(g, after):
        return products(z, plan, right, vec[1:], [c[:2] for c in chunks[g]], after)

    near, far, parts = {}, {}, {}
    spans = [piece[:2] for g in (1, 3) for piece in chunks[g]]
    made = products(z, plan, right, [near_rows], spans)
    near[1], near[3] = across(made[:each], 1), across(made[each:], 3)
    made = near_products(2, (made[0], *left[1:]))
    near[2] = across(made, 2)

    def send_terms(g, so_far, own_sums, kept, after):
        made, folded = terms(
            z, plan, left, near[2 if g == 4 else g], far[g], vec, chunks[g], so_far,
            own_sums, kept, after
        )
        first = made[: z.rep]
        if own_sums is not None:
            first[1:] = [shift(first[s], "rep", z.rep, s) for s in range(1, z.rep)]
        parts[g] = [first]
        for e in range(1, z.env):
            parts[g].append([shift_both(z, made[e * z.rep + s], e, s) for s in range(z.rep)])
        return folded

    def arrived(g):
        return [part for piece in parts[g][1:] for part in piece]

    near[0] = near_products(0, made[:1])
    far1 = far_products(1, (near[0][0], *plans[1:]))
    far1 = gate(far1, [*near[1], *near[3]])
    far[1] = across(far1, 1)
    far[0] = far_products(0, far1[:1])
    dots = send_terms(0, None, None, (), ())
    far3 = far_products(3, (dots,))
    far2 = far_products(2, far3[:1])
    far4 = far_products(4, far2[:1])
    far3 = gate(far3, [far4[0], *near[2], *arrived(0)[:1]])
    far[3] = across(far3, 3)
    far2 = gate(far2, [far3[0], *far[1]])
    far[2] = across(far2, 2)
    far4 = gate(far4, far[2])
    far[4] = across(far4, 2)
    dots = send_terms(1, dots, None, (), (far2[0], *arrived(0)))
    dots = send_terms(3, dots, None, (), arrived(1)[:1])
    own_block = vectors.astype(jnp.float32)
    own_sums = jnp.sum(energy[None, :, None, None] * own_block * own_block, axis=(1, 2, 3))
    dots = send_terms(2, dots, None, (), [far4[0]] + arrived(1)[1:] + arrived(3)[:1])
    early = (0, 1, 3, 2)
    kept = [parts[g][0][1:] for g in early]
    dots = send_terms(4, dots, own_sums, kept, arrived(3)[1:] + arrived(2))
    so_far, image = gather_terms(
        z,
        plans,
        energy,
        vectors,
        parts[4][0][1:],
        sum(piece[1] for piece in chunks[4]),
        [parts[g] for g in early],
        [chunks[g] for g in early],
        (dots,),
    )
    sums = chip_sums(z, plan, dots, parts[4][0][1:] + arrived(4), (so_far,))
    image, token = make_image(z, plans, so_far, image, parts[4], chunks[4])
    entries = z.slots * z.sector * z.order * z.order
    return (image, mean_over_sectors(z, sums, entries, (token,)))


def solution(mesh):
    return jax.shard_map(
        on_device,
        mesh=mesh,
        in_specs=(
            P(None, ("groups", "sector"), ("env", "rep"), None),
            P("env", ("groups", "sector"), "rep", None),
            P("env", ("groups", "sector"), "rep", None),
            P(("groups", "sector")),
            P("env", "groups"),
        ),
        out_specs=(P(None, ("groups", "sector"), ("env", "rep"), None), P("groups")),
        check_vma=False,
    )
```
